128 devices in a mesh: dom: 16 (over y, x_lo, core), st: 8 (over z, x_hi).
Axes of the slice: x: 4 (x_hi: 2, x_lo: 2; x = x_hi * 2 + x_lo), y: 4, z: 4, core: 2. Of those that a mesh axis runs over, the one named last changes fastest.
Arguments:
- states: bfloat16 [128, 64, 64, 128], P('st', 'dom'), may hold values from -6 to 6
- potential: float32 [64, 64, 128], P('dom'), may hold values from -2 to 0
- proj_values: float32 [64, 16, 16, 512], P('dom'), may hold values from -0.25 to 0.25
- block_list: int32 [64, 16, 16], P('dom'), may hold values from 0 to 12287, as said below
- tile_count: int32 [64, 16], P('dom'), may hold values from 1 to 16, as said below
- strength: float32 [12288], replicated, may hold values from 0.25 to 2
Outputs:
- rotated: bfloat16 [128, 64, 64, 128], P('st', 'dom')
The draws below stay inside these ranges and needn't reach their ends.
Inputs may be any that keep to these rules, and one draw needn't show every extreme that they name: `block_list`: entry (z, j, k) names projector 8 * a + r of atom a; atom a's home plane a // 24 lies within 4 planes of z, counted periodically over 64 planes. Slots 0 to tile_count - 1 of a tile are used, the others ignored; some tile uses all 16.
All inputs are finite; a program needn't handle non-finite values.
Results may differ from the reference program's by a relative error of at most 0.0056.
Values may be sent and summed in bfloat16 or wider, within the bound.
No kernel may reach another device: no remote copies, remote signals or barrier semaphores. Data moves between devices by JAX's collectives and lax.ppermute only.
A program may use at most 128 MiB of HBM per device.

```python
import math
import jax
import jax.numpy as jnp
from jax import lax

SD = 16
ZD = 4
NY = 64
NX = 128
TY = 4
K = 16
APP = 24
PPA = 8
NZ = 64
NSTATES = 128
NPROJ = 12288
TILES_Y = 16
TC = 512
CELLS = 524288


def draw_block_list(key, part):
    key = jax.random.fold_in(key, 11)
    first, second, third = jax.random.split(key, 3)
    shape = (NZ, NY // TY, K)
    plane = jnp.arange(NZ, dtype=jnp.int32)[:, None, None]
    offset = jax.random.randint(first, shape, -ZD, ZD + 1)
    home = jnp.mod(plane + offset, NZ)
    atom = home * APP + jax.random.randint(second, shape, 0, APP)
    chosen = atom * PPA + jax.random.randint(third, shape, 0, PPA)
    chosen = chosen.at[0, 0, 0].set(NZ * APP * PPA - 1)
    chosen = chosen.at[0, 0, 1].set(0)
    return chosen.astype(jnp.int32)


def draw_tile_count(key, part):
    key = jax.random.fold_in(key, 23)
    first, second, third = jax.random.split(key, 3)
    shape = (NZ, NY // TY)
    base = jax.random.randint(first, shape, 1, K + 1)
    vacant = jax.random.randint(second, (NZ, 1), 0, 4) == 0
    counts = jnp.where(vacant, (base + 1) // 2, base).reshape(-1)
    total = NZ * (NY // TY)
    place = jax.random.randint(third, (), 0, total)
    counts = counts.at[place].set(K)
    counts = counts.at[jnp.mod(place + 1, total)].set(1)
    return counts.reshape(shape).astype(jnp.int32)


def levels(stream_key, dims, cuts, smallest, high):
    def one(position, shards_of):
        steps = jax.random.uniform(jax.random.fold_in(jax.random.fold_in(stream_key, 6), position), (shards_of,), jnp.float32, smallest / len(cuts), high / len(cuts))
        return jnp.repeat(jnp.exp(steps), dims[position] // shards_of).reshape((-1,) + (1,) * (len(dims) - position - 1))

    factor_of = one(*cuts[0])
    for cut in cuts[1:]:
        factor_of = factor_of * one(*cut)
    return factor_of


def normal_values(stream_key, shape, deviation, reach, pieces=(), held_as=jnp.bfloat16):
    level = levels(stream_key, shape, pieces, -0.22, 0.18) if pieces else 1.0
    array = jax.random.normal(stream_key, shape, jnp.float32) * deviation * level
    return jnp.minimum(jnp.maximum(array, -reach), reach).astype(held_as)


def setup_inputs(seed: int = 0) -> dict:
    key_of = jax.random.split(jax.random.key(seed), 7)
    states = normal_values(key_of[0], (NSTATES, NZ, NY, NX), 1.0, 6.0, ((0, 8), (1, 16)))
    potential = jnp.clip(-2.0 + 2.0 * jax.random.uniform(key_of[1], (NZ, NY, NX), jnp.float32) ** levels(key_of[1], (NZ, NY, NX), ((0, 16),), -0.2, 0.2), -2.0, 0.0)
    proj_values = normal_values(key_of[2], (NZ, TILES_Y, K, TC), TC ** -0.5, 0.25, ((0, 16),), jnp.float32)
    block_list = draw_block_list(jax.random.fold_in(key_of[6], 71), 0)
    tile_count = draw_tile_count(jax.random.fold_in(key_of[6], 71), 0)
    strength = jnp.clip(jnp.exp(jax.random.uniform(key_of[5], (NPROJ,), jnp.float32, math.log(0.25), math.log(2.0))), 0.25, 2.0)
    return dict(states=states, potential=potential, proj_values=proj_values, block_list=block_list, tile_count=tile_count, strength=strength)


center = 8.25
half_width = 7.75

def second_difference(minus_two, minus_one, middle, plus_one, plus_two):
    return (16.0 * (minus_one + plus_one) - (minus_two + plus_two) - 30.0 * middle) / 12.0

def along_axis(field, axis):
    return second_difference(jnp.roll(field, 2, axis), jnp.roll(field, 1, axis), field, jnp.roll(field, -1, axis), jnp.roll(field, -2, axis))

def nonlocal_part(field, proj_masked, slot_ids, slot_strength):
    count = field.shape[0]
    tiles = field.reshape(count, proj_masked.shape[0], proj_masked.shape[2])
    partial_value = jnp.einsum('tkc,btc->tkb', proj_masked, tiles, precision=lax.Precision.HIGHEST)
    flat_ids = slot_ids.reshape(-1)
    table = jnp.zeros((NPROJ, count), jnp.float32).at[flat_ids].add(partial_value.reshape(-1, count))
    chosen = table[flat_ids].reshape(partial_value.shape) * slot_strength[..., None]
    applied = jnp.einsum('tkc,tkb->btc', proj_masked, chosen, precision=lax.Precision.HIGHEST)
    return applied.reshape(field.shape)

def reference(states, potential, proj_values, block_list, tile_count, strength):
    slot_ids = block_list.reshape(-1, K).astype(jnp.int32)
    used = (jnp.arange(K)[None, :] < tile_count.reshape(-1)[:, None]).astype(jnp.float32)
    proj_masked = proj_values.reshape(-1, K, TY * NX) * used[..., None]
    slot_strength = strength[slot_ids]

    def hamiltonian(field):
        kinetic = along_axis(field, 1) + along_axis(field, 2) + along_axis(field, 3)
        return -0.5 * kinetic + potential[None] * field + nonlocal_part(field, proj_masked, slot_ids, slot_strength)

    def filter_block(block):
        previous = block.astype(jnp.float32)
        current = (hamiltonian(previous) - center * previous) / half_width
        for degree in range(3):
            following = 2.0 * (hamiltonian(current) - center * current) / half_width - previous
            previous, current = (current, following)
        return current.astype(jnp.bfloat16)
    filtered = lax.map(filter_block, states.reshape(NSTATES // SD, SD, NZ, NY, NX)).reshape(NSTATES, -1)
    margin = jnp.dot(filtered.astype(jnp.float32), filtered.T.astype(jnp.float32), preferred_element_type=jnp.float32) / CELLS
    factor = jnp.linalg.cholesky(margin)
    inverse = jax.scipy.linalg.solve_triangular(factor, jnp.eye(NSTATES, dtype=jnp.float32), lower=True)
    inverse_b = inverse.astype(jnp.bfloat16)
    rotated = jnp.dot(inverse_b.astype(jnp.float32), filtered.astype(jnp.float32), preferred_element_type=jnp.float32).astype(jnp.bfloat16)
    return rotated.reshape(states.shape)
```

```python
import jax
import jax.numpy as jnp
from jax import lax
from jax.experimental import pallas as pl
from jax.experimental.pallas import tpu as pltpu
from jax.sharding import PartitionSpec as P

center = 8.25
half_width = 7.75

F32 = jnp.float32
BF16 = jnp.bfloat16
NT = (((1,), (1,)), ((), ()))
NN = (((1,), (0,)), ((), ()))


def passed_along(array, axis, by):
    devices = lax.axis_size(axis)
    return lax.ppermute(array, axis, [(i, (i + by) % devices) for i in range(devices)])


def call(kernel, out_shape, scratch=(), vmem=48, flops=0, nbytes=0):
    return pl.pallas_call(
        kernel,
        out_shape=out_shape,
        scratch_shapes=list(scratch),
        compiler_params=pltpu.CompilerParams(vmem_limit_bytes=vmem * 2**20),
        cost_estimate=pl.CostEstimate(flops=int(flops), bytes_accessed=int(nbytes), transcendentals=0),
    )


def block_mask(rows, cols, row_block, col_block):
    row = lax.broadcasted_iota(jnp.int32, (rows, cols), 0) // row_block
    col = lax.broadcasted_iota(jnp.int32, (rows, cols), 1) // col_block
    return row == col


def project(field, proj, states, slots):
    both = lax.dot_general(field, proj, NT, preferred_element_type=F32)
    both = jnp.where(block_mask(*both.shape, states, slots), both, 0.0)
    return jnp.sum(both.reshape(-1, states, both.shape[1]), axis=0)


def first_kernel(states, slots, field, proj_values, used, proj, partial):
    planes, cols = field.shape[0], proj.shape[1]
    for z in range(planes):
        proj[z] = proj_values[z].astype(BF16)
        at = slice(z * cols, (z + 1) * cols)
        partial[:, at] = (project(field[z], proj[z], states, slots) * used[:, at]).astype(BF16)


def coupling_kernel(ids, table):
    sources, count = ids.shape
    for e in range(sources):
        for q in range(0, count, 128):
            column = jnp.broadcast_to(ids[e : e + 1, q : q + 128], (128, 128)).T
            same = [
                jnp.where(column == ids[0:1, p : p + 128], 1.0, 0.0).astype(BF16)
                for p in range(0, count, 128)
            ]
            for i, p in enumerate(range(0, count, 128)):
                table[e * count + q : e * count + q + 128, p : p + 128] = same[i]


def step_kernel(sizes, first, last, *refs):
    states, slots, rows = sizes
    cur, below, above, own, *others = refs[:8]
    table, weight, used, proj, shifted = refs[8:13]
    rest = list(refs[13:])
    prev = None if first else rest.pop(0)
    if last:
        (nxt, applied) = rest
    else:
        (nxt, low, high, partial, applied) = rest
    planes, height, width = cur.shape
    tiles = height // states
    cols = proj.shape[1]
    gain = (1.0 if first else 2.0) / half_width
    near, far = -gain * 2.0 / 3.0, gain / 24.0

    terms = jnp.concatenate([own[...]] + [o[...] for o in others], axis=1)
    chosen = lax.dot_general(terms, table[...], NN, preferred_element_type=F32)
    chosen = (chosen * weight[...] * gain).astype(BF16)
    mask = block_mask(height, cols, states, slots)
    for z in range(planes):
        spread = jnp.broadcast_to(chosen[:, z * cols : (z + 1) * cols][None], (tiles, states, cols))
        spread = jnp.where(mask, spread.reshape(height, cols), jnp.zeros((), BF16))
        applied[z] = lax.dot_general(spread, proj[z], NN, preferred_element_type=F32)

    def lane(y):
        return slice(y * 128, (y + 1) * 128)

    def tile_step(j, carry):
        def at(t):
            return pl.ds(pl.multiple_of(t * states, states), states)

        here, left, right = at(j), at((j + tiles - 1) % tiles), at((j + 1) % tiles)

        def load(z, y):
            if z < 0:
                return below[z + 2, here, lane(y)].astype(F32)
            if z >= planes:
                return above[z - planes, here, lane(y)].astype(F32)
            if y < 0:
                return cur[z, left, lane(y + rows)].astype(F32)
            if y >= rows:
                return cur[z, right, lane(y - rows)].astype(F32)
            return cur[z, here, lane(y)].astype(F32)

        for y in range(rows):
            for z in range(planes):
                mid = load(z, y)
                one = load(z - 1, y) + load(z + 1, y) + load(z, y - 1) + load(z, y + 1)
                two = load(z - 2, y) + load(z + 2, y) + load(z, y - 2) + load(z, y + 2)
                one += pltpu.roll(mid, 1, 1) + pltpu.roll(mid, 127, 1)
                two += pltpu.roll(mid, 2, 1) + pltpu.roll(mid, 126, 1)
                local = shifted[z, pl.ds(j * rows + y, 1), :]
                new = near * one + far * two + local * mid * gain + applied[z, here, lane(y)]
                if not first:
                    new = new - prev[z, here, lane(y)].astype(F32)
                nxt[z, here, lane(y)] = new.astype(nxt.dtype)
                if not last:
                    if z < planes // 2:
                        low[z, here, lane(y)] = new.astype(BF16)
                    else:
                        high[z - planes // 2, here, lane(y)] = new.astype(BF16)
        return carry

    lax.fori_loop(0, tiles, tile_step, 0)
    if not last:
        for z in range(planes):
            half = low[z] if z < planes // 2 else high[z - planes // 2]
            at = slice(z * cols, (z + 1) * cols)
            partial[:, at] = (project(half, proj[z], states, slots) * used[:, at]).astype(BF16)


def gram_kernel(states, cells, margin):
    groups, height, width = cells.shape
    total = jnp.zeros(margin.shape, F32)
    for j in range(height // states):
        block = cells[:, j * states : (j + 1) * states, :].reshape(groups * states, width)
        total += lax.dot_general(block, block, NT, preferred_element_type=F32)
    margin[...] = total


def rotate_kernel(states, margin, cells, rotated, inverse):
    n = margin.shape[0]
    lanes = lax.broadcasted_iota(jnp.int32, (8, n), 1)
    subs = lax.broadcasted_iota(jnp.int32, (8, n), 0)
    work = [margin[8 * i : 8 * i + 8, :] for i in range(n // 8)]
    for k in range(n):
        b, r = divmod(k, 8)
        row = work[b][r : r + 1, :]
        pivot = row[:, k : k + 1]
        ahead = jnp.where(lanes[0:1] == k, 1.0, row)
        inverse[k : k + 1, :] = jnp.where(lanes[0:1] <= k, ahead, 0.0) * lax.rsqrt(pivot)
        scaled = ahead * (1.0 / pivot)
        for i in range(b, n // 8):
            column = work[i][:, k : k + 1]
            if i == b:
                column = jnp.where(subs[:, 0:1] > r, column, 0.0)
            work[i] = jnp.where(lanes == k, 0.0, work[i]) - column * scaled
    mine = inverse[...].astype(BF16)
    groups, height, width = cells.shape
    for j in range(height // states):
        block = cells[:, j * states : (j + 1) * states, :].reshape(groups * states, width)
        new = lax.dot_general(mine, block, NN, preferred_element_type=F32).astype(BF16)
        rotated[:, j * states : (j + 1) * states, :] = new.reshape(groups, states, width)


def per_device(states, potential, proj_values, block_list, tile_count, strength):
    local_states, planes, rows_y, cells_x = states.shape
    _, tiles, slots, tile_cells = proj_values.shape
    rows = rows_y // tiles
    domains, groups = lax.axis_size("dom"), lax.axis_size("st")
    total_cells = planes * rows_y * cells_x * domains
    height, cols, count = tiles * local_states, tiles * slots, planes * tiles * slots
    sizes = (local_states, slots, rows)
    shape = (planes, height, tile_cells)
    half = (planes // 2, height, tile_cells)

    field = states.reshape(local_states, planes, tiles, rows, cells_x)
    field = field.transpose(1, 2, 0, 3, 4).reshape(shape)
    ids = block_list.reshape(1, count).astype(F32)
    sources = (0, 1, -1, 2, -2)
    all_ids = jnp.concatenate([ids] + [passed_along(ids, "dom", by) for by in sources[1:]], axis=0)
    used = jnp.arange(slots)[None, :] < tile_count.reshape(-1, 1)
    used = used.astype(F32).reshape(1, count)
    weight = strength[block_list.reshape(-1)].reshape(1, count) * used
    shifted = potential + (3.75 - center)

    f32 = lambda s: jax.ShapeDtypeStruct(s, F32)
    bf16 = lambda s: jax.ShapeDtypeStruct(s, BF16)

    low, high = field[: planes // 2], field[planes // 2 :]
    proj, partial = call(
        lambda *r: first_kernel(local_states, slots, *r),
        (bf16((planes, cols, tile_cells)), bf16((local_states, count))),
        flops=5e8, nbytes=4 * 2**20,
    )(field, proj_values.reshape(planes, cols, tile_cells), used)
    table = call(coupling_kernel, bf16((len(sources) * count, count)), flops=1e7, nbytes=10 * 2**20)(all_ids)

    prev, cur = None, field
    for m in range(4):
        first, last = m == 0, m == 3
        below = passed_along(high, "dom", 1)
        above = passed_along(low, "dom", -1)
        terms = [partial] + [passed_along(partial, "dom", by) for by in sources[1:]]
        args = [cur, below, above] + terms + [table, weight, used, proj, shifted]
        if not first:
            args.append(prev)
        if last:
            outs = bf16(shape)
        else:
            outs = (f32(shape), bf16(half), bf16(half), bf16((local_states, count)))
        got = call(
            lambda *r, first=first, last=last: step_kernel(sizes, first, last, *r),
            outs,
            scratch=[pltpu.VMEM(shape, F32)],
            flops=2e9, nbytes=20 * 2**20,
        )(*args)
        if last:
            filtered = got
        else:
            prev = cur
            cur, low, high, partial = got

    cells = filtered.reshape(groups, planes * height // groups, tile_cells)
    cells = lax.all_to_all(cells, "st", 0, 0, tiled=True)
    nstates = groups * local_states
    part = call(lambda *r: gram_kernel(local_states, *r), f32((nstates, nstates)), flops=1e8, nbytes=2**20)(cells)
    both = ("dom", "st")
    per = nstates // (domains * groups)
    mine = lax.all_to_all(part.reshape(domains * groups, per, nstates), both, 0, 0, tiled=True)
    mine = jnp.sum(mine, axis=0, keepdims=True) / total_cells
    margin = lax.all_to_all(jnp.broadcast_to(mine, (domains * groups, per, nstates)), both, 0, 0, tiled=True)
    rotated = call(
        lambda *r: rotate_kernel(local_states, *r),
        bf16(cells.shape),
        scratch=[pltpu.VMEM((nstates, nstates), F32)],
        flops=2e8, nbytes=2**21,
    )(margin.reshape(nstates, nstates), cells)
    rotated = lax.all_to_all(rotated, "st", 0, 0, tiled=True)
    rotated = rotated.reshape(planes, tiles, local_states, rows, cells_x).transpose(2, 0, 1, 3, 4)
    return rotated.reshape(states.shape)


def solution(mesh):
    return jax.shard_map(
        per_device,
        mesh=mesh,
        in_specs=(
            P("st", "dom", None, None),
            P("dom", None, None),
            P("dom", None, None, None),
            P("dom", None, None),
            P("dom", None),
            P(),
        ),
        out_specs=P("st", "dom", None, None),
        check_vma=False,
    )
```

```python
import jax
import jax.numpy as jnp
from jax import lax
from jax.experimental import pallas as pl
from jax.experimental.pallas import tpu as pltpu
from jax.sharding import PartitionSpec as P

center = 8.25
half_width = 7.75

F32 = jnp.float32
BF16 = jnp.bfloat16
NT = (((1,), (1,)), ((), ()))
NN = (((1,), (0,)), ((), ()))


def passed_along(array, axis, by):
    devices = lax.axis_size(axis)
    return lax.ppermute(array, axis, [(i, (i + by) % devices) for i in range(devices)])


def call(kernel, out_shape, scratch=(), vmem=20, flops=0, nbytes=0, **specs):
    return pl.pallas_call(
        kernel,
        out_shape=out_shape,
        **specs,
        scratch_shapes=list(scratch),
        compiler_params=pltpu.CompilerParams(vmem_limit_bytes=vmem * 2**20),
        cost_estimate=pl.CostEstimate(flops=int(flops), bytes_accessed=int(nbytes), transcendentals=0),
    )


def rows_at(t, states, base=0):
    return pl.ds(pl.multiple_of(base + t * states, states), states)


def lane(y):
    return slice(y * 128, (y + 1) * 128)


def block_mask(rows, cols, row_block, col_block):
    row = lax.broadcasted_iota(jnp.int32, (rows, cols), 0) // row_block
    col = lax.broadcasted_iota(jnp.int32, (rows, cols), 1) // col_block
    return row == col


def project(field, proj, states, slots):
    both = lax.dot_general(field, proj, NT, preferred_element_type=F32)
    both = jnp.where(block_mask(*both.shape, states, slots), both, 0.0)
    return jnp.sum(both.reshape(-1, states, both.shape[1]), axis=0)


def write_message(message, base, partial):
    high, width = partial.shape[0], message.shape[1]
    for i in range(partial.shape[1] // width):
        message[base + i * high : base + (i + 1) * high, :] = partial[:, i * width : (i + 1) * width]


def read_message(message, base, high, count):
    width = message.shape[1]
    return jnp.concatenate(
        [message[base + i * high : base + (i + 1) * high, :] for i in range(count // width)], axis=1
    )


def spread_rows(digits, rows_of):
    tiles, slots = digits.shape
    cols = tiles * slots
    to = lax.broadcasted_iota(jnp.int32, (slots, cols), 1) % slots
    pick = jnp.where(lax.broadcasted_iota(jnp.int32, (slots, cols), 0) == to, 1.0, 0.0)
    wide = lax.dot_general(digits.astype(BF16), pick.astype(BF16), NN, preferred_element_type=F32)
    return jnp.sum(jnp.where(rows_of, wide, 0.0), axis=0, keepdims=True)


def first_kernel(states, slots, cells, proj_values, names, counts, *refs):
    field, proj, ids, used, partial, low, high, raw, sems = refs
    planes, height = field.shape[:2]
    cols = proj.shape[1]
    tiles, rows = height // states, cells.shape[1] * states // height
    half = planes // 2
    copies = [pltpu.make_async_copy(proj_values.at[z], raw.at[z], sems.at[z]) for z in range(planes)]
    for copy in copies:
        copy.start()
    rows_of = block_mask(tiles, cols, 1, slots)
    slot = (lax.broadcasted_iota(jnp.int32, (1, cols), 1) % slots).astype(F32)
    tops, bottoms = [], []
    for z in range(planes):
        name = names[z].astype(F32)
        top = jnp.floor(name * (1.0 / 128.0))
        tops.append(spread_rows(top, rows_of))
        bottoms.append(spread_rows(name - 128.0 * top, rows_of))
        count = jnp.broadcast_to(counts[z : z + 1, :].astype(F32), (tiles, tiles))
        count = jnp.where(block_mask(tiles, tiles, 1, 1), count, 0.0)
        count = jnp.broadcast_to(jnp.sum(count, axis=1, keepdims=True), (tiles, cols))
        count = jnp.sum(jnp.where(rows_of, count, 0.0), axis=0, keepdims=True)
        at = slice(z * cols, (z + 1) * cols)
        used[:, at] = jnp.where(slot < count, 1.0, 0.0)
        ids[:, at] = tops[z] * 128.0 + bottoms[z]
        for y in range(tiles * rows):
            field[z, (y // rows) * states : (y // rows + 1) * states, lane(y % rows)] = cells[z, y]
        message = low if z < half else high
        message[z % half * height : (z % half + 1) * height, :] = field[z]
    extra = partial.shape[0] - states
    row = lax.broadcasted_iota(jnp.int32, (extra, planes * cols), 0)
    top, bottom = jnp.concatenate(tops, axis=1), jnp.concatenate(bottoms, axis=1)
    partial[states:, :] = jnp.where(row == 0, top, jnp.where(row == 1, bottom, 0.0)).astype(BF16)
    for z in range(planes):
        copies[z].wait()
        proj[z] = raw[z].astype(BF16)
        at = slice(z * cols, (z + 1) * cols)
        partial[:states, at] = (project(field[z], proj[z], states, slots) * used[:, at]).astype(BF16)
    write_message(low, half * height, partial[...])
    write_message(high, half * height, partial[...])


def fill_table(parts, states, own_ids, table):
    count = own_ids.shape[1]
    for e, part in enumerate(parts):
        digits = part[states : states + 2, :].astype(F32)
        names = digits[0:1] * 128.0 + digits[1:2]
        for q in range(0, count, 128):
            column = jnp.broadcast_to(names[:, q : q + 128], (128, 128)).T
            for p in range(0, count, 128):
                same = jnp.where(column == own_ids[:, p : p + 128], 1.0, 0.0)
                table[e * count + q : e * count + q + 128, p : p + 128] = same.astype(BF16)


def local_kernel(sizes, first, *refs):
    states, slots, rows = sizes
    refs = list(refs)
    cur, potential, own = refs[:3]
    rest = refs[3:]
    if first:
        ids, base, share, table = rest
        fill_table([own[...]], states, ids, table)
    else:
        table, prev, base, share = rest
    planes, height, width = cur.shape
    tiles = height // states
    gain = (1.0 if first else 2.0) / half_width
    near, far = -gain * 2.0 / 3.0, gain / 24.0
    share[...] = lax.dot_general(own[:states, :], table[...], NN, preferred_element_type=F32)

    def tile_step(j, carry):
        here = rows_at(j, states)
        left, right = rows_at((j + tiles - 1) % tiles, states), rows_at((j + 1) % tiles, states)

        def load(z, y):
            if y < 0:
                return cur[z, left, lane(y + rows)].astype(F32)
            if y >= rows:
                return cur[z, right, lane(y - rows)].astype(F32)
            return cur[z, here, lane(y)].astype(F32)

        for y in range(rows):
            mids = [load(z, y) for z in range(planes)]
            for z in range(planes):
                mid = mids[z]
                one = load(z, y - 1) + load(z, y + 1)
                two = load(z, y - 2) + load(z, y + 2)
                one += pltpu.roll(mid, 1, 1) + pltpu.roll(mid, 127, 1)
                two += pltpu.roll(mid, 2, 1) + pltpu.roll(mid, 126, 1)
                for by in (-1, 1):
                    if 0 <= z + by < planes:
                        one += mids[z + by]
                    if 0 <= z + 2 * by < planes:
                        two += mids[z + 2 * by]
                new = near * one + far * two + (potential[z, pl.ds(j * rows + y, 1), :] + (3.75 - center)) * mid * gain
                if not first:
                    new = new - prev[z, here, lane(y)].astype(F32)
                base[z, here, lane(y)] = new
        return carry

    lax.fori_loop(0, tiles, tile_step, 0)


def step_kernel(sizes, first, last, *refs):
    states, slots, rows = sizes
    refs = list(refs)
    base, share, below, above, below2, above2, weight, used, proj = refs[:9]
    rest = refs[9:]
    planes, height, width = base.shape
    half = planes // 2
    tiles = height // states
    cols = proj.shape[1]
    count = planes * cols
    gain = (1.0 if first else 2.0) / half_width
    near, far = -gain * 2.0 / 3.0, gain / 24.0

    taken = below2.shape[0]
    parts = [read_message(r, half * height, taken, count) for r in (below, above)]
    parts += [below2[...], above2[...]]
    if first:
        ids, table = rest.pop(0), rest.pop(0)
        fill_table(parts, states, ids, table)
    else:
        table = rest.pop(0)
    if last:
        (nxt, applied) = rest
    else:
        (nxt, low, high, partial, applied) = rest

    terms = jnp.concatenate([part[:states] for part in parts], axis=1)
    chosen = lax.dot_general(terms, table[...], NN, preferred_element_type=F32) + share[...]
    chosen = (chosen * (weight[...] * used[...]) * gain).astype(BF16)
    mask = block_mask(height, cols, states, slots)
    for z in range(planes):
        spread = jnp.broadcast_to(chosen[:, z * cols : (z + 1) * cols][None], (tiles, states, cols))
        spread = jnp.where(mask, spread.reshape(height, cols), jnp.zeros((), BF16))
        applied[z] = lax.dot_general(spread, proj[z], NN, preferred_element_type=F32)

    def tile_step(j, carry):
        here = rows_at(j, states)
        for y in range(rows):
            b2, b1 = [below[rows_at(j, states, z * height), lane(y)].astype(F32) for z in range(half)]
            a1, a2 = [above[rows_at(j, states, z * height), lane(y)].astype(F32) for z in range(half)]
            outer = {0: near * b1 + far * b2, 1: far * b1}
            outer.update({planes - 2: far * a1, planes - 1: near * a1 + far * a2})
            for z in range(planes):
                new = base[z, here, lane(y)] + applied[z, here, lane(y)]
                if z in outer:
                    new += outer[z]
                nxt[z, here, lane(y)] = new.astype(nxt.dtype)
                if not last:
                    message = low if z < half else high
                    message[rows_at(j, states, z % half * height), lane(y)] = new.astype(BF16)
        return carry

    lax.fori_loop(0, tiles, tile_step, 0)
    if not last:
        for z in range(planes):
            message = low if z < half else high
            plane = message[z % half * height : (z % half + 1) * height, :]
            at = slice(z * cols, (z + 1) * cols)
            partial[:, at] = (project(plane, proj[z], states, slots) * used[:, at]).astype(BF16)
        write_message(low, half * height, partial[...])
        write_message(high, half * height, partial[...])


def gram_kernel(states, cells, margin):
    groups, height, width = cells.shape
    total = jnp.zeros(margin.shape, F32)
    for j in range(height // states):
        block = cells[:, j * states : (j + 1) * states, :].reshape(groups * states, width)
        total += lax.dot_general(block, block, NT, preferred_element_type=F32)
    margin[...] = total


def recip(x):
    r = pltpu.reciprocal(x, approx=True)
    r = r * (2.0 - x * r)
    return r * (2.0 - x * r)

def inverse_factor(margin, inverse):
    n = margin.shape[0]
    lanes = lax.broadcasted_iota(jnp.int32, (8, n), 1)
    subs = lax.broadcasted_iota(jnp.int32, (8, n), 0)
    eye = lax.broadcasted_iota(jnp.int32, (n, n), 0) == lax.broadcasted_iota(jnp.int32, (n, n), 1)
    full = margin[...]
    diagonal = jnp.where(eye, full, 0.0)
    across = lax.rsqrt(jnp.sum(diagonal, axis=0, keepdims=True))
    down = lax.rsqrt(jnp.sum(diagonal, axis=1, keepdims=True))
    full = full * down * across
    work = [full[8 * i : 8 * i + 8, :] for i in range(n // 8)]
    for k in range(0, n, 4):
        b, r = divmod(k, 8)
        rows = [work[b][r + p : r + p + 1, :] for p in range(4)]
        cols = [[jnp.broadcast_to(work[i][:, k + p : k + p + 1], (8, n)) for p in range(4)] for i in range(b, n // 8)]
        entry = lambda p, q: jnp.broadcast_to(cols[0][q][r + p : r + p + 1, :], (8, n))
        s = {(p, q): entry(p, q) for p in range(4) for q in range(p + 1)}
        rows = [jnp.where(lanes == k + p, 1.0, jnp.where((lanes >= k) & (lanes < k + 4), 0.0, jnp.broadcast_to(rows[p], (8, n)))) for p in range(4)]
        a, bb, c = s[0, 0], s[1, 0], s[1, 1]
        det = recip(a * c - bb * bb)
        i00, i01, i11 = c * det, -bb * det, a * det
        x = {}
        for q in (2, 3):
            x[0, q] = i00 * s[q, 0] + i01 * s[q, 1]
            x[1, q] = i01 * s[q, 0] + i11 * s[q, 1]
        g22 = s[2, 2] - (s[2, 0] * x[0, 2] + s[2, 1] * x[1, 2])
        g32 = s[3, 2] - (s[3, 0] * x[0, 2] + s[3, 1] * x[1, 2])
        g33 = s[3, 3] - (s[3, 0] * x[0, 3] + s[3, 1] * x[1, 3])
        det2 = recip(g22 * g33 - g32 * g32)
        h00, h01, h11 = g33 * det2, -g32 * det2, g22 * det2
        low2 = rows[2] - (x[0, 2] * rows[0] + x[1, 2] * rows[1])
        low3 = rows[3] - (x[0, 3] * rows[0] + x[1, 3] * rows[1])
        y2 = h00 * low2 + h01 * low3
        y3 = h01 * low2 + h11 * low3
        y0 = i00 * rows[0] + i01 * rows[1] - (x[0, 2] * y2 + x[0, 3] * y3)
        y1 = i01 * rows[0] + i11 * rows[1] - (x[1, 2] * y2 + x[1, 3] * y3)
        inside = (lanes >= k) & (lanes < k + 4)
        for i in range(b, n // 8):
            c4 = cols[i - b]
            if i == b and r == 0:
                c4 = [jnp.where(subs >= 4, v, 0.0) for v in c4]
            elif i == b:
                continue
            change = (c4[0] * y0 + c4[1] * y1) + (c4[2] * y2 + c4[3] * y3)
            work[i] = jnp.where(inside, 0.0, work[i]) - change
        ra = recip(a)
        l10 = bb * ra
        d1 = c - bb * l10
        rg = recip(g22)
        l32 = g32 * rg
        d3 = g33 - g32 * l32
        out = [rows[0] * lax.rsqrt(a), (rows[1] - l10 * rows[0]) * lax.rsqrt(d1), low2 * lax.rsqrt(g22), (low3 - l32 * low2) * lax.rsqrt(d3)]
        for p in range(4):
            inverse[k + p : k + p + 1, :] = (jnp.where(lanes <= k + p, out[p], 0.0) * across)[0:1]

def rotate_kernel(states, margin, cells, rotated, inverse):
    inverse_factor(margin, inverse)
    mine = inverse[...].astype(BF16)
    groups, height, width = cells.shape
    rows = width // 128
    for j in range(height // states):
        block = cells[:, j * states : (j + 1) * states, :].reshape(groups * states, width)
        new = lax.dot_general(mine, block, NN, preferred_element_type=F32).astype(BF16)
        new = new.reshape(groups, states, width)
        for y in range(rows):
            rotated[:, j * rows + y, :, :] = new[:, :, lane(y)]


def per_device(states, potential, proj_values, block_list, tile_count, strength):
    local_states, planes, rows_y, cells_x = states.shape
    _, tiles, slots, tile_cells = proj_values.shape
    rows = rows_y // tiles
    domains, groups = lax.axis_size("dom"), lax.axis_size("st")
    total_cells = planes * rows_y * cells_x * domains
    height, cols, count = tiles * local_states, tiles * slots, planes * tiles * slots
    sizes = (local_states, slots, rows)
    shape = (planes, height, tile_cells)
    id_rows = 16

    weight = strength[block_list.reshape(-1)].reshape(1, count)

    f32 = lambda s: jax.ShapeDtypeStruct(s, F32)
    bf16 = lambda s: jax.ShapeDtypeStruct(s, BF16)

    def sent(rows_taken):
        message = (planes // 2 * height + rows_taken * count // tile_cells, tile_cells)
        return bf16((rows_taken, count)), bf16(message), bf16(message)

    row = f32((1, count))
    anywhere, whole = pl.BlockSpec(memory_space=pl.ANY), pl.BlockSpec()
    field, proj, ids, used, partial, low, high = call(
        lambda *r: first_kernel(local_states, slots, *r),
        (bf16(shape), bf16((planes, cols, tile_cells)), row, row) + sent(local_states + id_rows),
        scratch=[pltpu.VMEM((planes, cols, tile_cells), F32), pltpu.SemaphoreType.DMA((planes,))],
        in_specs=[whole, anywhere, whole, whole],
        flops=5e8, nbytes=4 * 2**20,
    )(states.transpose(1, 2, 0, 3), proj_values.reshape(planes, cols, tile_cells), block_list, tile_count)

    prev, cur = None, field
    for m in range(4):
        first, last = m == 0, m == 3
        below2, above2 = passed_along(partial, "dom", 2), passed_along(partial, "dom", -2)
        below = passed_along(high, "dom", 1)
        above = passed_along(low, "dom", -1)
        outs = [f32(shape), f32((local_states, count))]
        args = [cur, potential, partial] + ([ids] if first else [own_table, prev])
        got = call(
            lambda *r, first=first: local_kernel(sizes, first, *r),
            outs + ([bf16((count, count))] if first else []),
            flops=1e9, nbytes=8 * 2**20,
        )(*args)
        if first:
            base, share, own_table = got
        else:
            base, share = got
        args = [base, share, below, above, below2, above2, weight, used, proj]
        args += [ids] if first else [table]
        outs = [bf16((4 * count, count))] if first else []
        if last:
            outs += [bf16(shape)]
        else:
            made = sent(local_states)
            outs += [f32(shape), made[1], made[2], made[0]]
        got = call(
            lambda *r, first=first, last=last: step_kernel(sizes, first, last, *r),
            outs,
            scratch=[pltpu.VMEM(shape, F32)],
            flops=1e9, nbytes=8 * 2**20,
        )(*args)
        if first:
            table, *got = got
        if last:
            (filtered,) = got
        else:
            prev = cur
            cur, low, high, partial = got

    cells = filtered.reshape(groups, planes * height // groups, tile_cells)
    cells = lax.all_to_all(cells, "st", 0, 0, tiled=True)
    nstates = groups * local_states
    part = call(lambda *r: gram_kernel(local_states, *r), f32((nstates, nstates)), flops=1e8, nbytes=2**20)(cells)
    both = ("dom", "st")
    per = nstates // (domains * groups)
    mine = lax.all_to_all(part.reshape(domains * groups, per, nstates), both, 0, 0, tiled=True)
    mine = jnp.sum(mine, axis=0, keepdims=True) / total_cells
    margin = lax.all_to_all(jnp.broadcast_to(mine, (domains * groups, per, nstates)), both, 0, 0, tiled=True)
    rotated = call(
        lambda *r: rotate_kernel(local_states, *r),
        bf16((groups, planes * rows_y // groups, local_states, cells_x)),
        scratch=[pltpu.VMEM((nstates, nstates), F32)],
        flops=2e8, nbytes=2**21,
    )(margin.reshape(nstates, nstates), cells)
    rotated = lax.all_to_all(rotated, "st", 0, 0, tiled=True)
    return rotated.reshape(planes, rows_y, local_states, cells_x).transpose(2, 0, 1, 3)


def solution(mesh):
    return jax.shard_map(
        per_device,
        mesh=mesh,
        in_specs=(
            P("st", "dom", None, None),
            P("dom", None, None),
            P("dom", None, None, None),
            P("dom", None, None),
            P("dom", None),
            P(),
        ),
        out_specs=P("st", "dom", None, None),
        check_vma=False,
    )
```

```python
import jax
import jax.numpy as jnp
from jax import lax
from jax.experimental import pallas as pl
from jax.experimental.pallas import tpu as pltpu
from jax.sharding import Mesh, PartitionSpec as P

center = 8.25
half_width = 7.75

F32 = jnp.float32
BF16 = jnp.bfloat16
NT = (((1,), (1,)), ((), ()))
NN = (((1,), (0,)), ((), ()))
CORES = 2
NO_NAME = 255.0 * 128.0


def passed_along(array, axis, by):
    devices = lax.axis_size(axis)
    return lax.ppermute(array, axis, [(i, (i + by) % devices) for i in range(devices)])


def call(kernel, out_shape, scratch=(), vmem=20, flops=0, nbytes=0, **specs):
    return pl.pallas_call(
        kernel,
        out_shape=out_shape,
        **specs,
        scratch_shapes=list(scratch),
        compiler_params=pltpu.CompilerParams(vmem_limit_bytes=vmem * 2**20),
        cost_estimate=pl.CostEstimate(flops=int(flops), bytes_accessed=int(nbytes), transcendentals=0),
    )


def rows_at(t, states, base=0):
    return pl.ds(pl.multiple_of(base + t * states, states), states)


def lane(y):
    return slice(y * 128, (y + 1) * 128)


def block_mask(rows, cols, row_block, col_block):
    row = lax.broadcasted_iota(jnp.int32, (rows, cols), 0) // row_block
    col = lax.broadcasted_iota(jnp.int32, (rows, cols), 1) // col_block
    return row == col


def project(field, proj, states, slots):
    both = lax.dot_general(field, proj, NT, preferred_element_type=F32)
    both = jnp.where(block_mask(*both.shape, states, slots), both, 0.0)
    return jnp.sum(both.reshape(-1, states, both.shape[1]), axis=0)


def folded(terms):
    half = terms.shape[1] // 2
    return jnp.concatenate([terms[:, :half], terms[:, half:]], axis=0).astype(BF16)


def unfolded(block):
    block = block.astype(F32)
    states = block.shape[0] // 2
    return jnp.concatenate([block[:states], block[states:]], axis=1)


def write_terms(message, base, block):
    high, width = block.shape[0], message.shape[1]
    for i in range(block.shape[1] // width):
        message[base + i * high : base + (i + 1) * high, :] = block[:, i * width : (i + 1) * width]


def read_terms(message, base, states, count):
    width, high = message.shape[1], 2 * states
    parts = [message[base + i * high : base + (i + 1) * high, :] for i in range(count // high * states // width)]
    return unfolded(jnp.concatenate(parts, axis=1))


def read_names(message, base, count):
    width = message.shape[1]
    digits = message[base : base + 16, :].astype(F32)
    parts = count // width
    names = [digits[i : i + 1] * 128.0 + digits[parts + i : parts + i + 1] for i in range(parts)]
    return jnp.concatenate(names, axis=1)


def halves_kernel(core, cells, mine, theirs):
    planes, height, width = mine.shape
    rows = width // 128
    first = core[0] == 0
    for z in range(planes):
        for pair in range(height // 16):
            for y in range(rows):
                one = cells[z, 2 * rows * pair + y].astype(F32)
                two = cells[z, 2 * rows * pair + rows + y].astype(F32)
                lower = jnp.concatenate([one[:8], two[:8]], axis=0)
                upper = jnp.concatenate([one[8:], two[8:]], axis=0)
                at = slice(pair * 16, pair * 16 + 16)
                mine[z, at, lane(y)] = jnp.where(first, lower, upper).astype(BF16)
                theirs[z, at, lane(y)] = jnp.where(first, upper, lower).astype(BF16)


def spread_rows(digits, rows_of):
    tiles, slots = digits.shape
    cols = tiles * slots
    to = lax.broadcasted_iota(jnp.int32, (slots, cols), 1) % slots
    pick = jnp.where(lax.broadcasted_iota(jnp.int32, (slots, cols), 0) == to, 1.0, 0.0)
    wide = lax.dot_general(digits.astype(BF16), pick.astype(BF16), NN, preferred_element_type=F32)
    return jnp.sum(jnp.where(rows_of, wide, 0.0), axis=0, keepdims=True)


def first_kernel(sizes, core, *refs):
    states, slots, rows = sizes
    ours, others = refs[0:5], refs[5:10]
    field, proj, potential, names, partial, low, high = refs[10:]
    planes, height, width = field.shape
    half, cols, tiles = planes // 2, proj.shape[1], height // states
    rows_of = block_mask(tiles, cols, 1, slots)
    diagonal = block_mask(tiles, tiles, 1, 1)
    slot = (lax.broadcasted_iota(jnp.int32, (1, cols), 1) % slots).astype(F32)
    digits = []
    for (cells, proj_of, names_of, counts, potential_of), own in ((ours, True), (others, False)):
        start = core[0] * half if own else (1 - core[0]) * half
        found = []
        for z in range(half):
            field[start + z] = cells[z].astype(F32)
            proj[start + z] = proj_of[z]
            potential[start + z] = potential_of[z]
            name = names_of[z].astype(F32)
            top = jnp.floor(name * (1.0 / 128.0))
            count = jnp.broadcast_to(counts[z : z + 1, :].astype(F32), (tiles, tiles))
            count = jnp.sum(jnp.where(diagonal, count, 0.0), axis=1, keepdims=True)
            count = jnp.sum(jnp.where(rows_of, count, 0.0), axis=0, keepdims=True)
            is_used = slot < count
            found.append(jnp.where(is_used, spread_rows(top, rows_of), NO_NAME / 128.0))
            found.append(jnp.where(is_used, spread_rows(name - 128.0 * top, rows_of), 0.0))
        digits.append([jnp.concatenate(found[i::2], axis=1) for i in (0, 1)])
    first = core[0] == 0
    top, bottom = (
        jnp.concatenate([jnp.where(first, a, b), jnp.where(first, b, a)], axis=1)
        for a, b in zip(digits[0], digits[1])
    )
    named = top * 128.0 + bottom
    names[...] = named
    used = jnp.where(named < NO_NAME, 1.0, 0.0)
    terms = []
    for z in range(planes):
        plane = field[z].astype(BF16)
        at = slice(z * cols, (z + 1) * cols)
        terms.append(project(plane, proj[z], states, slots) * used[:, at])
        if z < 2:
            low[z * height : (z + 1) * height, :] = plane
        if z >= planes - 2:
            high[(z - planes + 2) * height : (z - planes + 3) * height, :] = plane
    block = folded(jnp.concatenate(terms, axis=1))
    partial[...] = block
    parts = named.shape[1] // width
    lines = [v[:, i * width : (i + 1) * width] for v in (top, bottom) for i in range(parts)]
    lines = jnp.concatenate(lines + [jnp.zeros((16 - 2 * parts, width), F32)], axis=0).astype(BF16)
    for message in (low, high):
        write_terms(message, 2 * height, block)
        message[2 * height + 4 * states : 2 * height + 4 * states + 16, :] = lines


def same_names(names, own, store, wanted):
    for q in range(0, names.shape[1], 128):
        column = jnp.broadcast_to(names[:, q : q + 128], (128, 128)).T
        for p in range(0, own.shape[1], 128):
            if wanted(q, p):
                store(q, p, jnp.where(column == own[:, p : p + 128], 1.0, 0.0).astype(BF16))


def doubled(terms):
    return jnp.concatenate([terms, terms], axis=0).astype(BF16)


def look_up(strength, names):
    top = jnp.floor(names * (1.0 / 128.0))
    bottom = names - 128.0 * top
    lines, count = strength.shape[0], names.shape[1]
    line = lax.broadcasted_iota(jnp.int32, (lines, count), 0).astype(F32)
    pick = jnp.where(line == top, 1.0, 0.0)
    of_line = lax.dot_general(
        strength, pick, (((0,), (0,)), ((), ())), precision=lax.Precision.HIGHEST, preferred_element_type=F32
    )
    place = lax.broadcasted_iota(jnp.int32, (128, count), 0).astype(F32)
    return jnp.sum(jnp.where(place == bottom, of_line, 0.0), axis=0, keepdims=True)


def local_kernel(sizes, first, *refs):
    states, slots, rows = sizes
    refs = list(refs)
    cur, potential, own = refs[:3]
    rest = refs[3:]
    if first:
        names, strength, base, share, table, weight = rest
        named = names[...]
        mine = jnp.where(named < NO_NAME, named, -1.0)

        def store(q, p, same):
            table[q : q + 128, p : p + 128] = same

        same_names(named, mine, store, lambda q, p: True)
        weight[...] = look_up(strength[...], named)
    else:
        table, prev, base, share = rest
    planes, height, width = cur.shape
    tiles = height // states
    gain = (1.0 if first else 2.0) / half_width
    near, far = -gain * 2.0 / 3.0, gain / 24.0
    terms = doubled(unfolded(own[...]))
    share[...] = lax.dot_general(terms, table[...], NN, preferred_element_type=F32)[:states]

    def tile_step(j, carry):
        here = rows_at(j, states)
        left, right = rows_at((j + tiles - 1) % tiles, states), rows_at((j + 1) % tiles, states)

        def load(z, y):
            if y < 0:
                return cur[z, left, lane(y + rows)]
            if y >= rows:
                return cur[z, right, lane(y - rows)]
            return cur[z, here, lane(y)]

        for y in range(rows):
            mids = [load(z, y) for z in range(planes)]
            for z in range(planes):
                mid = mids[z]
                one = load(z, y - 1) + load(z, y + 1)
                two = load(z, y - 2) + load(z, y + 2)
                one += pltpu.roll(mid, 1, 1) + pltpu.roll(mid, 127, 1)
                two += pltpu.roll(mid, 2, 1) + pltpu.roll(mid, 126, 1)
                for by in (-1, 1):
                    if 0 <= z + by < planes:
                        one += mids[z + by]
                    if 0 <= z + 2 * by < planes:
                        two += mids[z + 2 * by]
                shift = potential[z, pl.ds(j * rows + y, 1), :] + (3.75 - center)
                new = near * one + far * two + shift * mid * gain
                if not first:
                    new = new - prev[z, here, lane(y)]
                base[z, here, lane(y)] = new
        return carry

    lax.fori_loop(0, tiles, tile_step, 0)


def step_kernel(sizes, first, last, *refs):
    states, slots, rows = sizes
    refs = list(refs)
    base, share, below, above, weight, names, proj = refs[:7]
    rest = refs[7:]
    planes, height, width = base.shape
    tiles = height // states
    cols = proj.shape[1]
    count = planes * cols
    reach = (planes + 1) * cols
    gain = (1.0 if first else 2.0) / half_width
    near, far = -gain * 2.0 / 3.0, gain / 24.0
    table = rest.pop(0)
    if last:
        (nxt, applied) = rest
    else:
        (nxt, low, high, partial, applied, rounded) = rest

    named = names[...]
    if first:
        around = [read_names(r, 2 * height + 4 * states, count) for r in (below, above)]
        mine = jnp.where(named < NO_NAME, named, -1.0)

        def store(q, p, same):
            z = p // cols
            table[z, q - z * cols : q - z * cols + 128, p - z * cols : p - z * cols + 128] = same

        def wanted(q, p):
            return 0 <= q // cols - p // cols <= planes

        same_names(jnp.concatenate(around, axis=1), mine, store, wanted)

    terms = [read_terms(r, 2 * height, states, count) for r in (below, above)]
    terms = doubled(jnp.concatenate(terms, axis=1))
    mask = block_mask(height, cols, states, slots)
    for z in range(planes):
        at = slice(z * cols, (z + 1) * cols)
        chosen = lax.dot_general(terms[:, z * cols : z * cols + reach], table[z], NN, preferred_element_type=F32)
        chosen = (chosen[:states] + share[:, at]) * (weight[:, at] * gain)
        spread = jnp.broadcast_to(chosen[None], (tiles, states, cols)).reshape(height, cols)
        spread = jnp.where(mask, spread, 0.0).astype(BF16)
        applied[z] = lax.dot_general(spread, proj[z], NN, preferred_element_type=F32)

    def pair_step(pair, carry):
        here = rows_at(pair, 2 * states)
        for y in range(rows):
            b2, b1 = [below[rows_at(pair, 2 * states, z * height), lane(y)].astype(F32) for z in range(2)]
            a1, a2 = [above[rows_at(pair, 2 * states, z * height), lane(y)].astype(F32) for z in range(2)]
            outer = {0: near * b1 + far * b2, 1: far * b1}
            outer.update({planes - 2: far * a1, planes - 1: near * a1 + far * a2})
            for z in range(planes):
                new = base[z, here, lane(y)] + applied[z, here, lane(y)]
                if z in outer:
                    new += outer[z]
                if last:
                    pairs = nxt.shape[1] // (2 * states)
                    parts = tiles // 2 // pairs
                    slab, plane = divmod(z, planes // CORES)
                    block = (plane * parts + pair // pairs) * CORES + slab
                    nxt[block, rows_at(pair % pairs, 2 * states), lane(y)] = new.astype(BF16)
                else:
                    nxt[z, here, lane(y)] = new
                    rounded[z, here, lane(y)] = new.astype(BF16)
        return carry

    lax.fori_loop(0, tiles // 2, pair_step, 0)
    if not last:
        used = jnp.where(named < NO_NAME, 1.0, 0.0)
        out = []
        for z in range(planes):
            at = slice(z * cols, (z + 1) * cols)
            out.append(project(rounded[z], proj[z], states, slots) * used[:, at])
            if z < 2:
                low[z * height : (z + 1) * height, :] = rounded[z]
            if z >= planes - 2:
                high[(z - planes + 2) * height : (z - planes + 3) * height, :] = rounded[z]
        block = folded(jnp.concatenate(out, axis=1))
        partial[...] = block
        write_terms(low, 2 * height, block)
        write_terms(high, 2 * height, block)


def gram_kernel(states, cells, margin, ordered):
    sources, height, width = cells.shape
    total = jnp.zeros(margin.shape, F32)
    for pair in range(height // (2 * states)):
        both = cells[:, pair * 2 * states : (pair + 1) * 2 * states, :].astype(F32)
        for i in range(2):
            block = both[:, i * states : (i + 1) * states, :].reshape(sources * states, width).astype(BF16)
            ordered[2 * pair + i] = block
            total += lax.dot_general(block, block, NT, preferred_element_type=F32)
    margin[...] = total


def recip(x):
    r = pltpu.reciprocal(x, approx=True)
    r = r * (2.0 - x * r)
    return r * (2.0 - x * r)

def inverse_factor(margin, inverse):
    n = margin.shape[0]
    lanes = lax.broadcasted_iota(jnp.int32, (8, n), 1)
    subs = lax.broadcasted_iota(jnp.int32, (8, n), 0)
    eye = lax.broadcasted_iota(jnp.int32, (n, n), 0) == lax.broadcasted_iota(jnp.int32, (n, n), 1)
    full = margin[...]
    diagonal = jnp.where(eye, full, 0.0)
    across = lax.rsqrt(jnp.sum(diagonal, axis=0, keepdims=True))
    down = lax.rsqrt(jnp.sum(diagonal, axis=1, keepdims=True))
    full = full * down * across
    work = [full[8 * i : 8 * i + 8, :] for i in range(n // 8)]
    for k in range(0, n, 4):
        b, r = divmod(k, 8)
        rows = [work[b][r + p : r + p + 1, :] for p in range(4)]
        cols = [[jnp.broadcast_to(work[i][:, k + p : k + p + 1], (8, n)) for p in range(4)] for i in range(b, n // 8)]
        entry = lambda p, q: jnp.broadcast_to(cols[0][q][r + p : r + p + 1, :], (8, n))
        s = {(p, q): entry(p, q) for p in range(4) for q in range(p + 1)}
        rows = [jnp.where(lanes == k + p, 1.0, jnp.where((lanes >= k) & (lanes < k + 4), 0.0, jnp.broadcast_to(rows[p], (8, n)))) for p in range(4)]
        a, bb, c = s[0, 0], s[1, 0], s[1, 1]
        det = recip(a * c - bb * bb)
        i00, i01, i11 = c * det, -bb * det, a * det
        x = {}
        for q in (2, 3):
            x[0, q] = i00 * s[q, 0] + i01 * s[q, 1]
            x[1, q] = i01 * s[q, 0] + i11 * s[q, 1]
        g22 = s[2, 2] - (s[2, 0] * x[0, 2] + s[2, 1] * x[1, 2])
        g32 = s[3, 2] - (s[3, 0] * x[0, 2] + s[3, 1] * x[1, 2])
        g33 = s[3, 3] - (s[3, 0] * x[0, 3] + s[3, 1] * x[1, 3])
        det2 = recip(g22 * g33 - g32 * g32)
        h00, h01, h11 = g33 * det2, -g32 * det2, g22 * det2
        low2 = rows[2] - (x[0, 2] * rows[0] + x[1, 2] * rows[1])
        low3 = rows[3] - (x[0, 3] * rows[0] + x[1, 3] * rows[1])
        y2 = h00 * low2 + h01 * low3
        y3 = h01 * low2 + h11 * low3
        y0 = i00 * rows[0] + i01 * rows[1] - (x[0, 2] * y2 + x[0, 3] * y3)
        y1 = i01 * rows[0] + i11 * rows[1] - (x[1, 2] * y2 + x[1, 3] * y3)
        inside = (lanes >= k) & (lanes < k + 4)
        for i in range(b, n // 8):
            c4 = cols[i - b]
            if i == b and r == 0:
                c4 = [jnp.where(subs >= 4, v, 0.0) for v in c4]
            elif i == b:
                continue
            change = (c4[0] * y0 + c4[1] * y1) + (c4[2] * y2 + c4[3] * y3)
            work[i] = jnp.where(inside, 0.0, work[i]) - change
        ra = recip(a)
        l10 = bb * ra
        d1 = c - bb * l10
        rg = recip(g22)
        l32 = g32 * rg
        d3 = g33 - g32 * l32
        out = [rows[0] * lax.rsqrt(a), (rows[1] - l10 * rows[0]) * lax.rsqrt(d1), low2 * lax.rsqrt(g22), (low3 - l32 * low2) * lax.rsqrt(d3)]
        for p in range(4):
            inverse[k + p : k + p + 1, :] = (jnp.where(lanes <= k + p, out[p], 0.0) * across)[0:1]

def rotate_kernel(margin, ordered, rotated, inverse):
    inverse_factor(margin, inverse)
    mine = inverse[...].astype(BF16)
    groups, _, states, _ = rotated.shape
    tiles, nstates, width = ordered.shape
    rows = width // 128
    for j in range(tiles):
        new = lax.dot_general(mine, ordered[j], NN, preferred_element_type=F32).astype(BF16)
        new = new.reshape(groups, states, width)
        for y in range(rows):
            rotated[:, j * rows + y, :, :] = new[:, :, lane(y)]


def per_device(states, potential, proj_values, block_list, tile_count, strength):
    local_states, slab_planes, rows_y, cells_x = states.shape
    _, tiles, slots, tile_cells = proj_values.shape
    rows = rows_y // tiles
    ring, groups = lax.axis_size("ring"), lax.axis_size("st")
    total_cells = slab_planes * rows_y * cells_x * ring * CORES
    share_states, planes = local_states // CORES, slab_planes * CORES
    height, cols, count = tiles * share_states, tiles * slots, planes * tiles * slots
    sizes = (share_states, slots, rows)
    shape = (planes, height, tile_cells)

    f32 = lambda s: jax.ShapeDtypeStruct(s, F32)
    bf16 = lambda s: jax.ShapeDtypeStruct(s, BF16)
    whole, scalar = pl.BlockSpec(), pl.BlockSpec(memory_space=pltpu.SMEM)

    def swapped(array):
        return lax.ppermute(array, "core", [(0, 1), (1, 0)])

    core = lax.axis_index("core").astype(jnp.int32).reshape(1)
    proj_own = proj_values.reshape(slab_planes, cols, tile_cells).astype(BF16)
    ours = [proj_own, block_list, tile_count, potential]
    others = [swapped(array) for array in ours]
    piece = bf16((slab_planes, height, tile_cells))
    mine, theirs = call(
        halves_kernel, (piece, piece), in_specs=[scalar, whole], flops=10**7, nbytes=2 * 2**20
    )(core, states.transpose(1, 2, 0, 3))
    got = swapped(theirs)

    def sent(names):
        message = (2 * height + 4 * share_states + (16 if names else 0), tile_cells)
        return [bf16((2 * share_states, count // 2)), bf16(message), bf16(message)]

    field, proj, shift, names, partial, low, high = call(
        lambda *r: first_kernel(sizes, *r),
        [f32(shape), bf16((planes, cols, tile_cells)), f32((planes, rows_y, cells_x)), f32((1, count))] + sent(True),
        in_specs=[scalar] + [whole] * 10,
        flops=10**9, nbytes=8 * 2**20,
    )(core, mine, *ours, got, *others)

    prev, cur = None, field
    for m in range(4):
        first, last = m == 0, m == 3
        below = passed_along(high, "ring", 1)
        above = passed_along(low, "ring", -1)
        outs = [f32(shape), f32((share_states, count))]
        args = [cur, shift, partial]
        args += [names, strength.reshape(-1, 128)] if first else [own_table, prev]
        got = call(
            lambda *r, first=first: local_kernel(sizes, first, *r),
            outs + ([bf16((count, count)), f32((1, count))] if first else []),
            flops=1e9, nbytes=8 * 2**20,
        )(*args)
        if first:
            base, share, own_table, weight = got
        else:
            base, share = got
        args = [base, share, below, above, weight, names, proj] + ([] if first else [table])
        outs = [bf16((planes, (planes + 1) * cols, cols))] if first else []
        scratch = [pltpu.VMEM(shape, F32)]
        if last:
            outs += [bf16((CORES * groups, planes * height // (CORES * groups), tile_cells))]
        else:
            made = sent(False)
            outs += [f32(shape), made[1], made[2], made[0]]
            scratch += [pltpu.VMEM(shape, BF16)]
        got = call(
            lambda *r, first=first, last=last: step_kernel(sizes, first, last, *r),
            outs, scratch=scratch, flops=1e9, nbytes=8 * 2**20,
        )(*args)
        if first:
            table, *got = got
        if last:
            (filtered,) = got
        else:
            prev = cur
            cur, low, high, partial = got

    cells = lax.all_to_all(filtered, ("st", "core"), 0, 0, tiled=True)
    nstates = groups * local_states
    own_tiles = cells.shape[1] // share_states
    part, ordered = call(
        lambda *r: gram_kernel(share_states, *r),
        (f32((nstates, nstates)), bf16((own_tiles, nstates, tile_cells))),
        flops=1e8, nbytes=2**20,
    )(cells)
    everywhere = ("ring", "core", "st")
    devices = ring * CORES * groups
    per = nstates // devices
    total = lax.all_to_all(part.reshape(devices, per, nstates), everywhere, 0, 0, tiled=True)
    total = jnp.sum(total, axis=0, keepdims=True) / total_cells
    margin = lax.all_to_all(jnp.broadcast_to(total, (devices, per, nstates)), everywhere, 0, 0, tiled=True)
    rotated = call(
        rotate_kernel,
        bf16((groups, slab_planes * rows_y // groups, local_states, cells_x)),
        scratch=[pltpu.VMEM((nstates, nstates), F32)],
        flops=2e8, nbytes=2**21,
    )(margin.reshape(nstates, nstates), ordered)
    rotated = lax.all_to_all(rotated, "st", 0, 0, tiled=True)
    return rotated.reshape(slab_planes, rows_y, local_states, cells_x).transpose(2, 0, 1, 3)


def solution(mesh):
    fine = Mesh(mesh.devices.reshape(-1, CORES, mesh.shape["st"]), ("ring", "core", "st"))
    dom = ("ring", "core")
    return jax.shard_map(
        per_device,
        mesh=fine,
        in_specs=(
            P("st", dom, None, None),
            P(dom, None, None),
            P(dom, None, None, None),
            P(dom, None, None),
            P(dom, None),
            P(),
        ),
        out_specs=P("st", dom, None, None),
        check_vma=False,
    )
```

```python
import jax
import jax.numpy as jnp
from jax import lax
from jax.experimental import pallas as pl
from jax.experimental.pallas import tpu as pltpu
from jax.sharding import Mesh, PartitionSpec as P

center = 8.25
half_width = 7.75

F32 = jnp.float32
BF16 = jnp.bfloat16
NT = (((1,), (1,)), ((), ()))
NN = (((1,), (0,)), ((), ()))
CORES = 2
NO_NAME = 255.0 * 128.0


def passed_along(array, axis, by):
    devices = lax.axis_size(axis)
    return lax.ppermute(array, axis, [(i, (i + by) % devices) for i in range(devices)])


def call(kernel, out_shape, scratch=(), vmem=20, flops=0, nbytes=0, **specs):
    return pl.pallas_call(
        kernel,
        out_shape=out_shape,
        **specs,
        scratch_shapes=list(scratch),
        compiler_params=pltpu.CompilerParams(vmem_limit_bytes=vmem * 2**20),
        cost_estimate=pl.CostEstimate(flops=int(flops), bytes_accessed=int(nbytes), transcendentals=0),
    )


def rows_at(t, states, base=0):
    return pl.ds(pl.multiple_of(base + t * states, states), states)


def lane(y):
    return slice(y * 128, (y + 1) * 128)


def block_mask(rows, cols, row_block, col_block):
    row = lax.broadcasted_iota(jnp.int32, (rows, cols), 0) // row_block
    col = lax.broadcasted_iota(jnp.int32, (rows, cols), 1) // col_block
    return row == col


def project(field, proj, states, slots):
    both = lax.dot_general(field, proj, NT, preferred_element_type=F32)
    both = jnp.where(block_mask(*both.shape, states, slots), both, 0.0)
    return jnp.sum(both.reshape(-1, states, both.shape[1]), axis=0)


def folded(terms):
    half = terms.shape[1] // 2
    return jnp.concatenate([terms[:, :half], terms[:, half:]], axis=0).astype(BF16)


def unfolded(block):
    block = block.astype(F32)
    states = block.shape[0] // 2
    return jnp.concatenate([block[:states], block[states:]], axis=1)


def write_terms(message, base, block):
    high, width = block.shape[0], message.shape[1]
    for i in range(block.shape[1] // width):
        message[base + i * high : base + (i + 1) * high, :] = block[:, i * width : (i + 1) * width]


def read_terms(message, base, states, count):
    width, high = message.shape[1], 2 * states
    parts = [message[base + i * high : base + (i + 1) * high, :] for i in range(count // high * states // width)]
    return unfolded(jnp.concatenate(parts, axis=1))


def read_names(message, base, count):
    width = message.shape[1]
    digits = message[base : base + 16, :].astype(F32)
    parts = count // width
    names = [digits[i : i + 1] * 128.0 + digits[parts + i : parts + i + 1] for i in range(parts)]
    return jnp.concatenate(names, axis=1)


def halves_kernel(core, cells, mine, theirs):
    planes, height, width = mine.shape
    rows = width // 128
    first = core[0] == 0
    for z in range(planes):
        for pair in range(height // 16):
            for y in range(rows):
                one = cells[z, 2 * rows * pair + y].astype(F32)
                two = cells[z, 2 * rows * pair + rows + y].astype(F32)
                lower = jnp.concatenate([one[:8], two[:8]], axis=0)
                upper = jnp.concatenate([one[8:], two[8:]], axis=0)
                at = slice(pair * 16, pair * 16 + 16)
                mine[z, at, lane(y)] = jnp.where(first, lower, upper).astype(BF16)
                theirs[z, at, lane(y)] = jnp.where(first, upper, lower).astype(BF16)


def spread_rows(digits, rows_of):
    tiles, slots = digits.shape
    cols = tiles * slots
    to = lax.broadcasted_iota(jnp.int32, (slots, cols), 1) % slots
    pick = jnp.where(lax.broadcasted_iota(jnp.int32, (slots, cols), 0) == to, 1.0, 0.0)
    wide = lax.dot_general(digits.astype(BF16), pick.astype(BF16), NN, preferred_element_type=F32)
    return jnp.sum(jnp.where(rows_of, wide, 0.0), axis=0, keepdims=True)


def first_kernel(sizes, core, *refs):
    states, slots, rows = sizes
    ours, others = refs[0:5], refs[5:10]
    field, proj, potential, names, partial, low, high = refs[10:]
    planes, height, width = field.shape
    half, cols, tiles = planes // 2, proj.shape[1], height // states
    rows_of = block_mask(tiles, cols, 1, slots)
    diagonal = block_mask(tiles, tiles, 1, 1)
    slot = (lax.broadcasted_iota(jnp.int32, (1, cols), 1) % slots).astype(F32)
    digits = []
    for (cells, proj_of, names_of, counts, potential_of), own in ((ours, True), (others, False)):
        start = core[0] * half if own else (1 - core[0]) * half
        found = []
        for z in range(half):
            field[start + z] = cells[z].astype(F32)
            proj[start + z] = proj_of[z]
            potential[start + z] = potential_of[z]
            name = names_of[z].astype(F32)
            top = jnp.floor(name * (1.0 / 128.0))
            count = jnp.broadcast_to(counts[z : z + 1, :].astype(F32), (tiles, tiles))
            count = jnp.sum(jnp.where(diagonal, count, 0.0), axis=1, keepdims=True)
            count = jnp.sum(jnp.where(rows_of, count, 0.0), axis=0, keepdims=True)
            is_used = slot < count
            found.append(jnp.where(is_used, spread_rows(top, rows_of), NO_NAME / 128.0))
            found.append(jnp.where(is_used, spread_rows(name - 128.0 * top, rows_of), 0.0))
        digits.append([jnp.concatenate(found[i::2], axis=1) for i in (0, 1)])
    first = core[0] == 0
    top, bottom = (
        jnp.concatenate([jnp.where(first, a, b), jnp.where(first, b, a)], axis=1)
        for a, b in zip(digits[0], digits[1])
    )
    named = top * 128.0 + bottom
    names[...] = named
    used = jnp.where(named < NO_NAME, 1.0, 0.0)
    terms = []
    for z in range(planes):
        plane = field[z].astype(BF16)
        at = slice(z * cols, (z + 1) * cols)
        terms.append(project(plane, proj[z], states, slots) * used[:, at])
        if z < 2:
            low[z * height : (z + 1) * height, :] = plane
        if z >= planes - 2:
            high[(z - planes + 2) * height : (z - planes + 3) * height, :] = plane
    block = folded(jnp.concatenate(terms, axis=1))
    partial[...] = block
    parts = named.shape[1] // width
    lines = [v[:, i * width : (i + 1) * width] for v in (top, bottom) for i in range(parts)]
    lines = jnp.concatenate(lines + [jnp.zeros((16 - 2 * parts, width), F32)], axis=0).astype(BF16)
    for message in (low, high):
        write_terms(message, 2 * height, block)
        message[2 * height + 4 * states : 2 * height + 4 * states + 16, :] = lines


def same_names(names, own, store, wanted):
    for q in range(0, names.shape[1], 128):
        column = jnp.broadcast_to(names[:, q : q + 128], (128, 128)).T
        for p in range(0, own.shape[1], 128):
            if wanted(q, p):
                store(q, p, jnp.where(column == own[:, p : p + 128], 1.0, 0.0).astype(BF16))


def doubled(terms):
    return jnp.concatenate([terms, terms], axis=0).astype(BF16)


def look_up(strength, names):
    top = jnp.floor(names * (1.0 / 128.0))
    bottom = names - 128.0 * top
    lines, count = strength.shape[0], names.shape[1]
    line = lax.broadcasted_iota(jnp.int32, (lines, count), 0).astype(F32)
    pick = jnp.where(line == top, 1.0, 0.0)
    of_line = lax.dot_general(
        strength, pick, (((0,), (0,)), ((), ())), precision=lax.Precision.HIGHEST, preferred_element_type=F32
    )
    place = lax.broadcasted_iota(jnp.int32, (128, count), 0).astype(F32)
    return jnp.sum(jnp.where(place == bottom, of_line, 0.0), axis=0, keepdims=True)


def local_kernel(sizes, first, *refs):
    states, slots, rows = sizes
    refs = list(refs)
    cur, potential, own = refs[:3]
    rest = refs[3:]
    if first:
        names, strength, base, share, table, weight = rest
        named = names[...]
        mine = jnp.where(named < NO_NAME, named, -1.0)

        def store(q, p, same):
            table[q : q + 128, p : p + 128] = same

        same_names(named, mine, store, lambda q, p: True)
        weight[...] = look_up(strength[...], named)
    else:
        table, prev, base, share = rest
    planes, height, width = cur.shape
    tiles = height // states
    gain = (1.0 if first else 2.0) / half_width
    near, far = -gain * 2.0 / 3.0, gain / 24.0
    terms = doubled(unfolded(own[...]))
    share[...] = lax.dot_general(terms, table[...], NN, preferred_element_type=F32)[:states]

    def tile_step(j, carry):
        here = rows_at(j, states)
        left, right = rows_at((j + tiles - 1) % tiles, states), rows_at((j + 1) % tiles, states)

        def load(z, y):
            if y < 0:
                return cur[z, left, lane(y + rows)]
            if y >= rows:
                return cur[z, right, lane(y - rows)]
            return cur[z, here, lane(y)]

        for y in range(rows):
            mids = [load(z, y) for z in range(planes)]
            for z in range(planes):
                mid = mids[z]
                one = load(z, y - 1) + load(z, y + 1)
                two = load(z, y - 2) + load(z, y + 2)
                one += pltpu.roll(mid, 1, 1) + pltpu.roll(mid, 127, 1)
                two += pltpu.roll(mid, 2, 1) + pltpu.roll(mid, 126, 1)
                for by in (-1, 1):
                    if 0 <= z + by < planes:
                        one += mids[z + by]
                    if 0 <= z + 2 * by < planes:
                        two += mids[z + 2 * by]
                shift = potential[z, pl.ds(j * rows + y, 1), :] + (3.75 - center)
                new = near * one + far * two + shift * mid * gain
                if not first:
                    new = new - prev[z, here, lane(y)]
                base[z, here, lane(y)] = new
        return carry

    lax.fori_loop(0, tiles, tile_step, 0)


def turn_kernel(sizes, early, core, *refs):
    inputs, refs = refs[:5], refs[5:]
    made, refs = ([], refs) if early else (refs[:4], refs[4:])

    @pl.when((core[0] != 0) if early else (core[0] == 0))
    def _():
        local_kernel(sizes, True, *inputs, *refs)

    if not early:

        @pl.when(core[0] != 0)
        def _():
            for ready, out in zip(made, refs):
                out[...] = ready[...]


def step_kernel(sizes, first, last, *refs):
    states, slots, rows = sizes
    refs = list(refs)
    base, share, below, above, weight, names, proj = refs[:7]
    rest = refs[7:]
    planes, height, width = base.shape
    tiles = height // states
    cols = proj.shape[1]
    count = planes * cols
    reach = (planes + 1) * cols
    gain = (1.0 if first else 2.0) / half_width
    near, far = -gain * 2.0 / 3.0, gain / 24.0
    table = rest.pop(0)
    if last:
        (nxt, applied) = rest
    else:
        (nxt, low, high, partial, applied, rounded) = rest

    named = names[...]
    if first:
        around = [read_names(r, 2 * height + 4 * states, count) for r in (below, above)]
        mine = jnp.where(named < NO_NAME, named, -1.0)

        def store(q, p, same):
            z = p // cols
            table[z, q - z * cols : q - z * cols + 128, p - z * cols : p - z * cols + 128] = same

        def wanted(q, p):
            return 0 <= q // cols - p // cols <= planes

        same_names(jnp.concatenate(around, axis=1), mine, store, wanted)

    terms = [read_terms(r, 2 * height, states, count) for r in (below, above)]
    terms = doubled(jnp.concatenate(terms, axis=1))
    mask = block_mask(height, cols, states, slots)
    for z in range(planes):
        at = slice(z * cols, (z + 1) * cols)
        chosen = lax.dot_general(terms[:, z * cols : z * cols + reach], table[z], NN, preferred_element_type=F32)
        chosen = (chosen[:states] + share[:, at]) * (weight[:, at] * gain)
        spread = jnp.broadcast_to(chosen[None], (tiles, states, cols)).reshape(height, cols)
        spread = jnp.where(mask, spread, 0.0).astype(BF16)
        applied[z] = lax.dot_general(spread, proj[z], NN, preferred_element_type=F32)

    def pair_step(pair, carry):
        here = rows_at(pair, 2 * states)
        for y in range(rows):
            b2, b1 = [below[rows_at(pair, 2 * states, z * height), lane(y)].astype(F32) for z in range(2)]
            a1, a2 = [above[rows_at(pair, 2 * states, z * height), lane(y)].astype(F32) for z in range(2)]
            outer = {0: near * b1 + far * b2, 1: far * b1}
            outer.update({planes - 2: far * a1, planes - 1: near * a1 + far * a2})
            for z in range(planes):
                new = base[z, here, lane(y)] + applied[z, here, lane(y)]
                if z in outer:
                    new += outer[z]
                if last:
                    pairs = nxt.shape[1] // (2 * states)
                    parts = tiles // 2 // pairs
                    slab, plane = divmod(z, planes // CORES)
                    block = (plane * parts + pair // pairs) * CORES + slab
                    nxt[block, rows_at(pair % pairs, 2 * states), lane(y)] = new.astype(BF16)
                else:
                    nxt[z, here, lane(y)] = new
                    rounded[z, here, lane(y)] = new.astype(BF16)
        return carry

    lax.fori_loop(0, tiles // 2, pair_step, 0)
    if not last:
        used = jnp.where(named < NO_NAME, 1.0, 0.0)
        out = []
        for z in range(planes):
            at = slice(z * cols, (z + 1) * cols)
            out.append(project(rounded[z], proj[z], states, slots) * used[:, at])
            if z < 2:
                low[z * height : (z + 1) * height, :] = rounded[z]
            if z >= planes - 2:
                high[(z - planes + 2) * height : (z - planes + 3) * height, :] = rounded[z]
        block = folded(jnp.concatenate(out, axis=1))
        partial[...] = block
        write_terms(low, 2 * height, block)
        write_terms(high, 2 * height, block)


def gram_kernel(states, cells, margin, ordered):
    sources, height, width = cells.shape
    total = jnp.zeros(margin.shape, F32)
    for pair in range(height // (2 * states)):
        both = cells[:, pair * 2 * states : (pair + 1) * 2 * states, :].astype(F32)
        for i in range(2):
            block = both[:, i * states : (i + 1) * states, :].reshape(sources * states, width).astype(BF16)
            ordered[2 * pair + i] = block
            total += lax.dot_general(block, block, NT, preferred_element_type=F32)
    margin[...] = total


def recip(x):
    r = pltpu.reciprocal(x, approx=True)
    r = r * (2.0 - x * r)
    return r * (2.0 - x * r)

def inverse_factor(margin, inverse):
    n = margin.shape[0]
    lanes = lax.broadcasted_iota(jnp.int32, (8, n), 1)
    subs = lax.broadcasted_iota(jnp.int32, (8, n), 0)
    eye = lax.broadcasted_iota(jnp.int32, (n, n), 0) == lax.broadcasted_iota(jnp.int32, (n, n), 1)
    full = margin[...]
    diagonal = jnp.where(eye, full, 0.0)
    across = lax.rsqrt(jnp.sum(diagonal, axis=0, keepdims=True))
    down = lax.rsqrt(jnp.sum(diagonal, axis=1, keepdims=True))
    full = full * down * across
    work = [full[8 * i : 8 * i + 8, :] for i in range(n // 8)]
    for k in range(0, n, 4):
        b, r = divmod(k, 8)
        rows = [work[b][r + p : r + p + 1, :] for p in range(4)]
        cols = [[jnp.broadcast_to(work[i][:, k + p : k + p + 1], (8, n)) for p in range(4)] for i in range(b, n // 8)]
        entry = lambda p, q: jnp.broadcast_to(cols[0][q][r + p : r + p + 1, :], (8, n))
        s = {(p, q): entry(p, q) for p in range(4) for q in range(p + 1)}
        rows = [jnp.where(lanes == k + p, 1.0, jnp.where((lanes >= k) & (lanes < k + 4), 0.0, jnp.broadcast_to(rows[p], (8, n)))) for p in range(4)]
        a, bb, c = s[0, 0], s[1, 0], s[1, 1]
        det = recip(a * c - bb * bb)
        i00, i01, i11 = c * det, -bb * det, a * det
        x = {}
        for q in (2, 3):
            x[0, q] = i00 * s[q, 0] + i01 * s[q, 1]
            x[1, q] = i01 * s[q, 0] + i11 * s[q, 1]
        g22 = s[2, 2] - (s[2, 0] * x[0, 2] + s[2, 1] * x[1, 2])
        g32 = s[3, 2] - (s[3, 0] * x[0, 2] + s[3, 1] * x[1, 2])
        g33 = s[3, 3] - (s[3, 0] * x[0, 3] + s[3, 1] * x[1, 3])
        det2 = recip(g22 * g33 - g32 * g32)
        h00, h01, h11 = g33 * det2, -g32 * det2, g22 * det2
        low2 = rows[2] - (x[0, 2] * rows[0] + x[1, 2] * rows[1])
        low3 = rows[3] - (x[0, 3] * rows[0] + x[1, 3] * rows[1])
        y2 = h00 * low2 + h01 * low3
        y3 = h01 * low2 + h11 * low3
        y0 = i00 * rows[0] + i01 * rows[1] - (x[0, 2] * y2 + x[0, 3] * y3)
        y1 = i01 * rows[0] + i11 * rows[1] - (x[1, 2] * y2 + x[1, 3] * y3)
        inside = (lanes >= k) & (lanes < k + 4)
        for i in range(b, n // 8):
            c4 = cols[i - b]
            if i == b and r == 0:
                c4 = [jnp.where(subs >= 4, v, 0.0) for v in c4]
            elif i == b:
                continue
            change = (c4[0] * y0 + c4[1] * y1) + (c4[2] * y2 + c4[3] * y3)
            work[i] = jnp.where(inside, 0.0, work[i]) - change
        ra = recip(a)
        l10 = bb * ra
        d1 = c - bb * l10
        rg = recip(g22)
        l32 = g32 * rg
        d3 = g33 - g32 * l32
        out = [rows[0] * lax.rsqrt(a), (rows[1] - l10 * rows[0]) * lax.rsqrt(d1), low2 * lax.rsqrt(g22), (low3 - l32 * low2) * lax.rsqrt(d3)]
        for p in range(4):
            inverse[k + p : k + p + 1, :] = (jnp.where(lanes <= k + p, out[p], 0.0) * across)[0:1]

def rotate_kernel(margin, ordered, rotated, inverse):
    inverse_factor(margin, inverse)
    mine = inverse[...].astype(BF16)
    groups, _, states, _ = rotated.shape
    tiles, nstates, width = ordered.shape
    rows = width // 128
    for j in range(tiles):
        new = lax.dot_general(mine, ordered[j], NN, preferred_element_type=F32).astype(BF16)
        new = new.reshape(groups, states, width)
        for y in range(rows):
            rotated[:, j * rows + y, :, :] = new[:, :, lane(y)]


def per_device(states, potential, proj_values, block_list, tile_count, strength):
    local_states, slab_planes, rows_y, cells_x = states.shape
    _, tiles, slots, tile_cells = proj_values.shape
    rows = rows_y // tiles
    ring, groups = lax.axis_size("ring"), lax.axis_size("st")
    total_cells = slab_planes * rows_y * cells_x * ring * CORES
    share_states, planes = local_states // CORES, slab_planes * CORES
    height, cols, count = tiles * share_states, tiles * slots, planes * tiles * slots
    sizes = (share_states, slots, rows)
    shape = (planes, height, tile_cells)

    f32 = lambda s: jax.ShapeDtypeStruct(s, F32)
    bf16 = lambda s: jax.ShapeDtypeStruct(s, BF16)
    whole, scalar = pl.BlockSpec(), pl.BlockSpec(memory_space=pltpu.SMEM)

    def swapped(array):
        return lax.ppermute(array, "core", [(0, 1), (1, 0)])

    core = lax.axis_index("core").astype(jnp.int32).reshape(1)
    proj_own = proj_values.reshape(slab_planes, cols, tile_cells).astype(BF16)
    ours = [proj_own, block_list, tile_count, potential]
    others = [swapped(array) for array in ours]
    piece = bf16((slab_planes, height, tile_cells))
    mine, theirs = call(
        halves_kernel, (piece, piece), in_specs=[scalar, whole], flops=10**7, nbytes=2 * 2**20
    )(core, states.transpose(1, 2, 0, 3))
    got = swapped(theirs)

    def sent(names):
        message = (2 * height + 4 * share_states + (16 if names else 0), tile_cells)
        return [bf16((2 * share_states, count // 2)), bf16(message), bf16(message)]

    field, proj, shift, names, partial, low, high = call(
        lambda *r: first_kernel(sizes, *r),
        [f32(shape), bf16((planes, cols, tile_cells)), f32((planes, rows_y, cells_x)), f32((1, count))] + sent(True),
        in_specs=[scalar] + [whole] * 10,
        flops=10**9, nbytes=8 * 2**20,
    )(core, mine, *ours, got, *others)

    prev, cur = None, field
    for m in range(4):
        first, last = m == 0, m == 3
        outs = [f32(shape), f32((share_states, count))]
        args = [cur, shift, partial]
        if first:
            args = [core] + args + [names, strength.reshape(-1, 128)]
            outs += [bf16((count, count)), f32((1, count))]
            made = call(
                lambda *r: turn_kernel(sizes, True, *r), outs,
                in_specs=[scalar] + [whole] * 5, flops=1e9, nbytes=8 * 2**20,
            )(*args)
            low, high, *made = lax.optimization_barrier((low, high, *made))
        below = passed_along(high, "ring", 1)
        above = passed_along(low, "ring", -1)
        if first:
            base, share, own_table, weight = call(
                lambda *r: turn_kernel(sizes, False, *r), outs,
                in_specs=[scalar] + [whole] * 9, flops=1e9, nbytes=8 * 2**20,
            )(*args, *made)
        else:
            base, share = call(
                lambda *r: local_kernel(sizes, False, *r), outs, flops=1e9, nbytes=8 * 2**20
            )(*args, own_table, prev)
        args = [base, share, below, above, weight, names, proj] + ([] if first else [table])
        outs = [bf16((planes, (planes + 1) * cols, cols))] if first else []
        scratch = [pltpu.VMEM(shape, F32)]
        if last:
            outs += [bf16((CORES * groups, planes * height // (CORES * groups), tile_cells))]
        else:
            made = sent(False)
            outs += [f32(shape), made[1], made[2], made[0]]
            scratch += [pltpu.VMEM(shape, BF16)]
        got = call(
            lambda *r, first=first, last=last: step_kernel(sizes, first, last, *r),
            outs, scratch=scratch, flops=1e9, nbytes=8 * 2**20,
        )(*args)
        if first:
            table, *got = got
        if last:
            (filtered,) = got
        else:
            prev = cur
            cur, low, high, partial = got

    cells = lax.all_to_all(filtered, ("st", "core"), 0, 0, tiled=True)
    nstates = groups * local_states
    own_tiles = cells.shape[1] // share_states
    part, ordered = call(
        lambda *r: gram_kernel(share_states, *r),
        (f32((nstates, nstates)), bf16((own_tiles, nstates, tile_cells))),
        flops=1e8, nbytes=2**20,
    )(cells)
    everywhere = ("ring", "core", "st")
    devices = ring * CORES * groups
    per = nstates // devices
    total = lax.all_to_all(part.reshape(devices, per, nstates), everywhere, 0, 0, tiled=True)
    total = jnp.sum(total, axis=0, keepdims=True) / total_cells
    margin = lax.all_to_all(jnp.broadcast_to(total, (devices, per, nstates)), everywhere, 0, 0, tiled=True)
    rotated = call(
        rotate_kernel,
        bf16((groups, slab_planes * rows_y // groups, local_states, cells_x)),
        scratch=[pltpu.VMEM((nstates, nstates), F32)],
        flops=2e8, nbytes=2**21,
    )(margin.reshape(nstates, nstates), ordered)
    rotated = lax.all_to_all(rotated, "st", 0, 0, tiled=True)
    return rotated.reshape(slab_planes, rows_y, local_states, cells_x).transpose(2, 0, 1, 3)


def solution(mesh):
    fine = Mesh(mesh.devices.reshape(-1, CORES, mesh.shape["st"]), ("ring", "core", "st"))
    dom = ("ring", "core")
    return jax.shard_map(
        per_device,
        mesh=fine,
        in_specs=(
            P("st", dom, None, None),
            P(dom, None, None),
            P(dom, None, None, None),
            P(dom, None, None),
            P(dom, None),
            P(),
        ),
        out_specs=P("st", dom, None, None),
        check_vma=False,
    )
```

```python
import jax
import jax.numpy as jnp
from jax import lax
from jax.experimental import pallas as pl
from jax.experimental.pallas import tpu as pltpu
from jax.sharding import Mesh, PartitionSpec as P

center = 8.25
half_width = 7.75

F32 = jnp.float32
BF16 = jnp.bfloat16
F8 = jnp.float8_e4m3fn
NT = (((1,), (1,)), ((), ()))
NN = (((1,), (0,)), ((), ()))
CORES = 2
NO_NAME = 255.0 * 128.0


def passed_along(array, axis, by):
    devices = lax.axis_size(axis)
    return lax.ppermute(array, axis, [(i, (i + by) % devices) for i in range(devices)])


def call(kernel, out_shape, scratch=(), vmem=20, flops=0, nbytes=0, **specs):
    return pl.pallas_call(
        kernel,
        out_shape=out_shape,
        **specs,
        scratch_shapes=list(scratch),
        compiler_params=pltpu.CompilerParams(vmem_limit_bytes=vmem * 2**20),
        cost_estimate=pl.CostEstimate(flops=int(flops), bytes_accessed=int(nbytes), transcendentals=0),
    )


def rows_at(t, states, base=0):
    return pl.ds(pl.multiple_of(base + t * states, states), states)


def lane(y):
    return slice(y * 128, (y + 1) * 128)


def block_mask(rows, cols, row_block, col_block):
    row = lax.broadcasted_iota(jnp.int32, (rows, cols), 0) // row_block
    col = lax.broadcasted_iota(jnp.int32, (rows, cols), 1) // col_block
    return row == col


def project(field, proj, states, slots):
    both = lax.dot_general(field, proj, NT, preferred_element_type=F32)
    both = jnp.where(block_mask(*both.shape, states, slots), both, 0.0)
    return jnp.sum(both.reshape(-1, states, both.shape[1]), axis=0)


def folded(terms):
    half = terms.shape[1] // 2
    return jnp.concatenate([terms[:, :half], terms[:, half:]], axis=0).astype(BF16)


def unfolded(block):
    block = block.astype(F32)
    states = block.shape[0] // 2
    return jnp.concatenate([block[:states], block[states:]], axis=1)


def write_terms(message, base, block):
    high, width = block.shape[0], message.shape[1]
    for i in range(block.shape[1] // width):
        message[base + i * high : base + (i + 1) * high, :] = block[:, i * width : (i + 1) * width]


def read_terms(message, base, states, count):
    width, high = message.shape[1], 2 * states
    parts = [message[base + i * high : base + (i + 1) * high, :] for i in range(count // high * states // width)]
    return unfolded(jnp.concatenate(parts, axis=1))


def read_names(message, base, count):
    width = message.shape[1]
    digits = message[base : base + 16, :].astype(F32)
    parts = count // width
    names = [digits[i : i + 1] * 128.0 + digits[parts + i : parts + i + 1] for i in range(parts)]
    return jnp.concatenate(names, axis=1)


def halves_kernel(core, cells, mine, theirs):
    planes, height, width = mine.shape
    rows = width // 128
    first = core[0] == 0
    for z in range(planes):
        for pair in range(height // 16):
            for y in range(rows):
                one = cells[z, 2 * rows * pair + y].astype(F32)
                two = cells[z, 2 * rows * pair + rows + y].astype(F32)
                lower = jnp.concatenate([one[:8], two[:8]], axis=0)
                upper = jnp.concatenate([one[8:], two[8:]], axis=0)
                at = slice(pair * 16, pair * 16 + 16)
                mine[z, at, lane(y)] = jnp.where(first, lower, upper).astype(BF16)
                theirs[z, at, lane(y)] = jnp.where(first, upper, lower).astype(BF16)


def spread_rows(digits, rows_of):
    tiles, slots = digits.shape
    cols = tiles * slots
    to = lax.broadcasted_iota(jnp.int32, (slots, cols), 1) % slots
    pick = jnp.where(lax.broadcasted_iota(jnp.int32, (slots, cols), 0) == to, 1.0, 0.0)
    wide = lax.dot_general(digits.astype(BF16), pick.astype(BF16), NN, preferred_element_type=F32)
    return jnp.sum(jnp.where(rows_of, wide, 0.0), axis=0, keepdims=True)


def first_kernel(sizes, core, *refs):
    states, slots, rows = sizes
    ours, others = refs[0:5], refs[5:10]
    field, proj, potential, names, partial, low, high = refs[10:]
    planes, height, width = field.shape
    half, cols, tiles = planes // 2, proj.shape[1], height // states
    rows_of = block_mask(tiles, cols, 1, slots)
    diagonal = block_mask(tiles, tiles, 1, 1)
    slot = (lax.broadcasted_iota(jnp.int32, (1, cols), 1) % slots).astype(F32)
    digits = []
    for (cells, proj_of, names_of, counts, potential_of), own in ((ours, True), (others, False)):
        start = core[0] * half if own else (1 - core[0]) * half
        found = []
        for z in range(half):
            field[start + z] = cells[z].astype(F32)
            proj[start + z] = proj_of[z]
            potential[start + z] = potential_of[z]
            name = names_of[z].astype(F32)
            top = jnp.floor(name * (1.0 / 128.0))
            count = jnp.broadcast_to(counts[z : z + 1, :].astype(F32), (tiles, tiles))
            count = jnp.sum(jnp.where(diagonal, count, 0.0), axis=1, keepdims=True)
            count = jnp.sum(jnp.where(rows_of, count, 0.0), axis=0, keepdims=True)
            is_used = slot < count
            found.append(jnp.where(is_used, spread_rows(top, rows_of), NO_NAME / 128.0))
            found.append(jnp.where(is_used, spread_rows(name - 128.0 * top, rows_of), 0.0))
        digits.append([jnp.concatenate(found[i::2], axis=1) for i in (0, 1)])
    first = core[0] == 0
    top, bottom = (
        jnp.concatenate([jnp.where(first, a, b), jnp.where(first, b, a)], axis=1)
        for a, b in zip(digits[0], digits[1])
    )
    named = top * 128.0 + bottom
    names[...] = named
    used = jnp.where(named < NO_NAME, 1.0, 0.0)
    terms = []
    for z in range(planes):
        plane = field[z].astype(BF16)
        at = slice(z * cols, (z + 1) * cols)
        terms.append(project(plane, proj[z], states, slots) * used[:, at])
        if z < 2:
            low[z * height : (z + 1) * height, :] = plane
        if z >= planes - 2:
            high[(z - planes + 2) * height : (z - planes + 3) * height, :] = plane
    block = folded(jnp.concatenate(terms, axis=1))
    partial[...] = block
    parts = named.shape[1] // width
    lines = [v[:, i * width : (i + 1) * width] for v in (top, bottom) for i in range(parts)]
    lines = jnp.concatenate(lines + [jnp.zeros((16 - 2 * parts, width), F32)], axis=0).astype(BF16)
    for message in (low, high):
        write_terms(message, 2 * height, block)
        message[2 * height + 4 * states : 2 * height + 4 * states + 16, :] = lines


def same_names(names, own, store, wanted):
    for q in range(0, names.shape[1], 128):
        column = jnp.broadcast_to(names[:, q : q + 128], (128, 128)).T
        for p in range(0, own.shape[1], 128):
            if wanted(q, p):
                store(q, p, jnp.where(column == own[:, p : p + 128], 1.0, 0.0))


def doubled(terms):
    return jnp.concatenate([terms, terms], axis=0).astype(BF16)


def look_up(strength, names):
    top = jnp.floor(names * (1.0 / 128.0))
    bottom = names - 128.0 * top
    lines, count = strength.shape[0], names.shape[1]
    line = lax.broadcasted_iota(jnp.int32, (lines, count), 0).astype(F32)
    pick = jnp.where(line == top, 1.0, 0.0)
    of_line = lax.dot_general(
        strength, pick, (((0,), (0,)), ((), ())), precision=lax.Precision.HIGHEST, preferred_element_type=F32
    )
    place = lax.broadcasted_iota(jnp.int32, (128, count), 0).astype(F32)
    return jnp.sum(jnp.where(place == bottom, of_line, 0.0), axis=0, keepdims=True)


def applied_to(chosen, proj, tiles, mask):
    spread = jnp.broadcast_to(chosen[None], (tiles,) + chosen.shape).reshape(mask.shape)
    spread = jnp.where(mask, spread, 0.0).astype(BF16)
    return lax.dot_general(spread, proj, NN, preferred_element_type=F32)


def inner_planes(planes):
    return range(2, planes - 2)


def local_kernel(sizes, first, *refs):
    states, slots, rows = sizes
    refs = list(refs)
    if first:
        cur, potential, own, proj, names, strength, base, share, inner, table, weight, square = refs
        named = names[...]
        mine = jnp.where(named < NO_NAME, named, -1.0)

        def store(q, p, same):
            table[q : q + 128, p : p + 128] = same.astype(BF16)

        same_names(named, mine, store, lambda q, p: True)
        weight[...] = look_up(strength[...], named)
    else:
        outer, chosen, done, table, prev, potential, own, proj, cur, base, share, inner = refs
    planes, height, width = cur.shape
    tiles, cols = height // states, proj.shape[1]
    gain = (1.0 if first else 2.0) / half_width
    near, far = -gain * 2.0 / 3.0, gain / 24.0
    terms = doubled(unfolded(own[...]))
    share[...] = lax.dot_general(terms, table[...], NN, preferred_element_type=F32)[:states]
    if first:
        same_tile = block_mask(cols, cols, slots, slots)
        for i, z in enumerate(inner_planes(planes)):
            products = lax.dot_general(proj[z], proj[z], NT, preferred_element_type=F32)
            square[i] = jnp.where(same_tile, products, 0.0).astype(BF16)
    else:
        mask = block_mask(height, cols, states, slots)
        for z in range(planes):
            if z in inner_planes(planes):
                cur[z] = done[z] + applied_to(chosen[:, z * cols : (z + 1) * cols], proj[z], tiles, mask)
            else:
                cur[z] = outer[z if z < 2 else z - planes + 4]

    def tile_step(j, carry):
        here = rows_at(j, states)
        left, right = rows_at((j + tiles - 1) % tiles, states), rows_at((j + 1) % tiles, states)

        def load(z, y):
            if y < 0:
                return cur[z, left, lane(y + rows)]
            if y >= rows:
                return cur[z, right, lane(y - rows)]
            return cur[z, here, lane(y)]

        for y in range(rows):
            mids = [load(z, y) for z in range(planes)]
            for z in range(planes):
                mid = mids[z]
                one = load(z, y - 1) + load(z, y + 1)
                two = load(z, y - 2) + load(z, y + 2)
                one += pltpu.roll(mid, 1, 1) + pltpu.roll(mid, 127, 1)
                two += pltpu.roll(mid, 2, 1) + pltpu.roll(mid, 126, 1)
                for by in (-1, 1):
                    if 0 <= z + by < planes:
                        one += mids[z + by]
                    if 0 <= z + 2 * by < planes:
                        two += mids[z + 2 * by]
                shift = potential[z, pl.ds(j * rows + y, 1), :] + (3.75 - center)
                new = near * one + far * two + shift * mid * gain
                if not first:
                    new = new - prev[z, here, lane(y)]
                base[z, here, lane(y)] = new
        return carry

    lax.fori_loop(0, tiles, tile_step, 0)
    for i, z in enumerate(inner_planes(planes)):
        inner[:, i * cols : (i + 1) * cols] = project(base[z].astype(BF16), proj[z], states, slots)


def turn_kernel(sizes, early, core, *refs):
    inputs, refs = refs[:6], refs[6:]
    made, refs = ([], refs) if early else (refs[:6], refs[6:])

    @pl.when((core[0] != 0) if early else (core[0] == 0))
    def _():
        local_kernel(sizes, True, *inputs, *refs)

    if not early:

        @pl.when(core[0] != 0)
        def _():
            for ready, out in zip(made, refs):
                out[...] = ready[...]


def in_pieces(terms):
    largest = jnp.maximum(jnp.max(jnp.abs(terms), axis=1, keepdims=True), 1e-30)
    rest = terms * (240.0 / largest)
    pieces = []
    for _ in range(3):
        pieces.append(rest.astype(F8).astype(F32))
        rest = rest - pieces[-1]
    return jnp.concatenate(pieces + [jnp.zeros_like(terms)], axis=0).astype(F8), largest * (1.0 / 240.0)


def step_kernel(sizes, first, last, *refs):
    states, slots, rows = sizes
    refs = list(refs)
    base, share, below, above, weight, names, proj, inner, square = refs[:9]
    rest = refs[9:]
    planes, height, width = base.shape
    tiles = height // states
    cols = proj.shape[1]
    count = planes * cols
    reach = (planes + 1) * cols
    gain = (1.0 if first else 2.0) / half_width
    near, far = -gain * 2.0 / 3.0, gain / 24.0
    table = rest.pop(0)
    if last:
        (nxt, applied) = rest
    else:
        (nxt, low, high, partial, selected, applied) = rest

    named = names[...]
    if first:
        around = [read_names(r, 2 * height + 4 * states, count) for r in (below, above)]
        mine = jnp.where(named < NO_NAME, named, -1.0)

        def store(q, p, same):
            z = p // cols
            table[z, q - z * cols : q - z * cols + 128, p - z * cols : p - z * cols + 128] = same.astype(F8)

        def wanted(q, p):
            return 0 <= q // cols - p // cols <= planes

        same_names(jnp.concatenate(around, axis=1), mine, store, wanted)

    terms = [read_terms(r, 2 * height, states, count) for r in (below, above)]
    terms, scale = in_pieces(jnp.concatenate(terms, axis=1))
    mask = block_mask(height, cols, states, slots)
    used = jnp.where(named < NO_NAME, 1.0, 0.0)
    out = [None] * planes
    for z in range(planes):
        at = slice(z * cols, (z + 1) * cols)
        chosen = lax.dot_general(terms[:, z * cols : z * cols + reach], table[z], NN, preferred_element_type=F32)
        chosen = (chosen[:states] + chosen[states : 2 * states] + chosen[2 * states : 3 * states]) * scale
        chosen = (chosen + share[:, at]) * (weight[:, at] * gain)
        if not last:
            selected[:, at] = chosen
        if last or z not in inner_planes(planes):
            applied[z] = applied_to(chosen, proj[z], tiles, mask)
        else:
            i = z - inner_planes(planes)[0]
            of_chosen = lax.dot_general(doubled(chosen), square[i], NN, preferred_element_type=F32)
            out[z] = (inner[:, i * cols : (i + 1) * cols] + of_chosen[:states]) * used[:, at]

    def pair_step(pair, carry):
        here = rows_at(pair, 2 * states)
        for y in range(rows):
            b2, b1 = [below[rows_at(pair, 2 * states, z * height), lane(y)].astype(F32) for z in range(2)]
            a1, a2 = [above[rows_at(pair, 2 * states, z * height), lane(y)].astype(F32) for z in range(2)]
            outer = {0: near * b1 + far * b2, 1: far * b1}
            outer.update({planes - 2: far * a1, planes - 1: near * a1 + far * a2})
            for z in range(planes):
                if not last and z not in outer:
                    continue
                new = base[z, here, lane(y)] + applied[z, here, lane(y)]
                if z in outer:
                    new += outer[z]
                if last:
                    pairs = nxt.shape[1] // (2 * states)
                    parts = tiles // 2 // pairs
                    slab, plane = divmod(z, planes // CORES)
                    block = (plane * parts + pair // pairs) * CORES + slab
                    nxt[block, rows_at(pair % pairs, 2 * states), lane(y)] = new.astype(BF16)
                else:
                    i = z if z < 2 else z - planes + 4
                    nxt[i, here, lane(y)] = new
                    message = low if i < 2 else high
                    message[rows_at(pair, 2 * states, i % 2 * height), lane(y)] = new.astype(BF16)
        return carry

    lax.fori_loop(0, tiles // 2, pair_step, 0)
    if not last:
        for z in range(planes):
            if z in inner_planes(planes):
                continue
            i = z if z < 2 else z - planes + 4
            plane = (low if i < 2 else high)[i % 2 * height : (i % 2 + 1) * height, :]
            out[z] = project(plane, proj[z], states, slots) * used[:, z * cols : (z + 1) * cols]
        block = folded(jnp.concatenate(out, axis=1))
        partial[...] = block
        write_terms(low, 2 * height, block)
        write_terms(high, 2 * height, block)


def gram_kernel(states, cells, margin, ordered):
    sources, height, width = cells.shape
    total = jnp.zeros(margin.shape, F32)
    for pair in range(height // (2 * states)):
        both = cells[:, pair * 2 * states : (pair + 1) * 2 * states, :].astype(F32)
        for i in range(2):
            block = both[:, i * states : (i + 1) * states, :].reshape(sources * states, width).astype(BF16)
            ordered[2 * pair + i] = block
            total += lax.dot_general(block, block, NT, preferred_element_type=F32)
    margin[...] = total


def recip(x):
    r = pltpu.reciprocal(x, approx=True)
    r = r * (2.0 - x * r)
    return r * (2.0 - x * r)

def inverse_factor(margin, inverse):
    n = margin.shape[0]
    lanes = lax.broadcasted_iota(jnp.int32, (8, n), 1)
    subs = lax.broadcasted_iota(jnp.int32, (8, n), 0)
    eye = lax.broadcasted_iota(jnp.int32, (n, n), 0) == lax.broadcasted_iota(jnp.int32, (n, n), 1)
    full = margin[...]
    diagonal = jnp.where(eye, full, 0.0)
    across = lax.rsqrt(jnp.sum(diagonal, axis=0, keepdims=True))
    down = lax.rsqrt(jnp.sum(diagonal, axis=1, keepdims=True))
    full = full * down * across
    work = [full[8 * i : 8 * i + 8, :] for i in range(n // 8)]
    for k in range(0, n, 4):
        b, r = divmod(k, 8)
        rows = [work[b][r + p : r + p + 1, :] for p in range(4)]
        cols = [[jnp.broadcast_to(work[i][:, k + p : k + p + 1], (8, n)) for p in range(4)] for i in range(b, n // 8)]
        entry = lambda p, q: jnp.broadcast_to(cols[0][q][r + p : r + p + 1, :], (8, n))
        s = {(p, q): entry(p, q) for p in range(4) for q in range(p + 1)}
        rows = [jnp.where(lanes == k + p, 1.0, jnp.where((lanes >= k) & (lanes < k + 4), 0.0, jnp.broadcast_to(rows[p], (8, n)))) for p in range(4)]
        a, bb, c = s[0, 0], s[1, 0], s[1, 1]
        det = recip(a * c - bb * bb)
        i00, i01, i11 = c * det, -bb * det, a * det
        x = {}
        for q in (2, 3):
            x[0, q] = i00 * s[q, 0] + i01 * s[q, 1]
            x[1, q] = i01 * s[q, 0] + i11 * s[q, 1]
        g22 = s[2, 2] - (s[2, 0] * x[0, 2] + s[2, 1] * x[1, 2])
        g32 = s[3, 2] - (s[3, 0] * x[0, 2] + s[3, 1] * x[1, 2])
        g33 = s[3, 3] - (s[3, 0] * x[0, 3] + s[3, 1] * x[1, 3])
        det2 = recip(g22 * g33 - g32 * g32)
        h00, h01, h11 = g33 * det2, -g32 * det2, g22 * det2
        low2 = rows[2] - (x[0, 2] * rows[0] + x[1, 2] * rows[1])
        low3 = rows[3] - (x[0, 3] * rows[0] + x[1, 3] * rows[1])
        y2 = h00 * low2 + h01 * low3
        y3 = h01 * low2 + h11 * low3
        y0 = i00 * rows[0] + i01 * rows[1] - (x[0, 2] * y2 + x[0, 3] * y3)
        y1 = i01 * rows[0] + i11 * rows[1] - (x[1, 2] * y2 + x[1, 3] * y3)
        inside = (lanes >= k) & (lanes < k + 4)
        for i in range(b, n // 8):
            c4 = cols[i - b]
            if i == b and r == 0:
                c4 = [jnp.where(subs >= 4, v, 0.0) for v in c4]
            elif i == b:
                continue
            change = (c4[0] * y0 + c4[1] * y1) + (c4[2] * y2 + c4[3] * y3)
            work[i] = jnp.where(inside, 0.0, work[i]) - change
        ra = recip(a)
        l10 = bb * ra
        d1 = c - bb * l10
        rg = recip(g22)
        l32 = g32 * rg
        d3 = g33 - g32 * l32
        out = [rows[0] * lax.rsqrt(a), (rows[1] - l10 * rows[0]) * lax.rsqrt(d1), low2 * lax.rsqrt(g22), (low3 - l32 * low2) * lax.rsqrt(d3)]
        for p in range(4):
            inverse[k + p : k + p + 1, :] = (jnp.where(lanes <= k + p, out[p], 0.0) * across)[0:1]

def rotate_kernel(margin, ordered, rotated, inverse):
    inverse_factor(margin, inverse)
    mine = inverse[...].astype(BF16)
    groups, _, states, _ = rotated.shape
    tiles, nstates, width = ordered.shape
    rows = width // 128
    for j in range(tiles):
        new = lax.dot_general(mine, ordered[j], NN, preferred_element_type=F32).astype(BF16)
        new = new.reshape(groups, states, width)
        for y in range(rows):
            rotated[:, j * rows + y, :, :] = new[:, :, lane(y)]


def per_device(states, potential, proj_values, block_list, tile_count, strength):
    local_states, slab_planes, rows_y, cells_x = states.shape
    _, tiles, slots, tile_cells = proj_values.shape
    rows = rows_y // tiles
    ring, groups = lax.axis_size("ring"), lax.axis_size("st")
    total_cells = slab_planes * rows_y * cells_x * ring * CORES
    share_states, planes = local_states // CORES, slab_planes * CORES
    height, cols, count = tiles * share_states, tiles * slots, planes * tiles * slots
    sizes = (share_states, slots, rows)
    shape = (planes, height, tile_cells)

    f32 = lambda s: jax.ShapeDtypeStruct(s, F32)
    bf16 = lambda s: jax.ShapeDtypeStruct(s, BF16)
    whole, scalar = pl.BlockSpec(), pl.BlockSpec(memory_space=pltpu.SMEM)

    def swapped(array):
        return lax.ppermute(array, "core", [(0, 1), (1, 0)])

    core = lax.axis_index("core").astype(jnp.int32).reshape(1)
    proj_own = proj_values.reshape(slab_planes, cols, tile_cells).astype(BF16)
    ours = [proj_own, block_list, tile_count, potential]
    others = [swapped(array) for array in ours]
    piece = bf16((slab_planes, height, tile_cells))
    mine, theirs = call(
        halves_kernel, (piece, piece), in_specs=[scalar, whole], flops=10**7, nbytes=2 * 2**20
    )(core, states.transpose(1, 2, 0, 3))
    got = swapped(theirs)

    def sent(names):
        message = (2 * height + 4 * share_states + (16 if names else 0), tile_cells)
        return [bf16((2 * share_states, count // 2)), bf16(message), bf16(message)]

    field, proj, shift, names, partial, low, high = call(
        lambda *r: first_kernel(sizes, *r),
        [f32(shape), bf16((planes, cols, tile_cells)), f32((planes, rows_y, cells_x)), f32((1, count))] + sent(True),
        in_specs=[scalar] + [whole] * 10,
        flops=10**9, nbytes=8 * 2**20,
    )(core, mine, *ours, got, *others)

    inside = len(inner_planes(planes))
    prev, cur, outer = None, field, None
    for m in range(4):
        first, last = m == 0, m == 3
        outs = [f32(shape), f32((share_states, count)), f32((share_states, inside * cols))]
        if first:
            args = [core, cur, shift, partial, proj, names, strength.reshape(-1, 128)]
            outs += [bf16((count, count)), f32((1, count)), bf16((inside, cols, cols))]
            made = call(
                lambda *r: turn_kernel(sizes, True, *r), outs,
                in_specs=[scalar] + [whole] * 6, flops=1e9, nbytes=8 * 2**20,
            )(*args)
            low, high, *made = lax.optimization_barrier((low, high, *made))
        below = passed_along(high, "ring", 1)
        above = passed_along(low, "ring", -1)
        if first:
            base, share, inner, own_table, weight, square = call(
                lambda *r: turn_kernel(sizes, False, *r), outs,
                in_specs=[scalar] + [whole] * 12, flops=1e9, nbytes=8 * 2**20,
            )(*args, *made)
        else:
            after, base, share, inner = call(
                lambda *r: local_kernel(sizes, False, *r), [f32(shape)] + outs, flops=1e9, nbytes=8 * 2**20
            )(outer, chosen, base, own_table, prev, shift, partial, proj)
            prev, cur = cur, after
        args = [base, share, below, above, weight, names, proj, inner, square] + ([] if first else [table])
        outs = [jax.ShapeDtypeStruct((planes, (planes + 1) * cols, cols), F8)] if first else []
        if last:
            outs += [bf16((CORES * groups, planes * height // (CORES * groups), tile_cells))]
        else:
            made = sent(False)
            outs += [f32((4, height, tile_cells)), made[1], made[2], made[0], f32((share_states, count))]
        got = call(
            lambda *r, first=first, last=last: step_kernel(sizes, first, last, *r),
            outs, scratch=[pltpu.VMEM(shape, F32)], flops=1e9, nbytes=8 * 2**20,
        )(*args)
        if first:
            table, *got = got
        if last:
            (filtered,) = got
        else:
            outer, low, high, partial, chosen = got
            prev = cur

    cells = lax.all_to_all(filtered, ("st", "core"), 0, 0, tiled=True)
    nstates = groups * local_states
    own_tiles = cells.shape[1] // share_states
    part, ordered = call(
        lambda *r: gram_kernel(share_states, *r),
        (f32((nstates, nstates)), bf16((own_tiles, nstates, tile_cells))),
        flops=1e8, nbytes=2**20,
    )(cells)
    everywhere = ("ring", "core", "st")
    devices = ring * CORES * groups
    per = nstates // devices
    total = lax.all_to_all(part.reshape(devices, per, nstates), everywhere, 0, 0, tiled=True)
    total = jnp.sum(total, axis=0, keepdims=True) / total_cells
    margin = lax.all_to_all(jnp.broadcast_to(total, (devices, per, nstates)), everywhere, 0, 0, tiled=True)
    rotated = call(
        rotate_kernel,
        bf16((groups, slab_planes * rows_y // groups, local_states, cells_x)),
        scratch=[pltpu.VMEM((nstates, nstates), F32)],
        flops=2e8, nbytes=2**21,
    )(margin.reshape(nstates, nstates), ordered)
    rotated = lax.all_to_all(rotated, "st", 0, 0, tiled=True)
    return rotated.reshape(slab_planes, rows_y, local_states, cells_x).transpose(2, 0, 1, 3)


def solution(mesh):
    fine = Mesh(mesh.devices.reshape(-1, CORES, mesh.shape["st"]), ("ring", "core", "st"))
    dom = ("ring", "core")
    return jax.shard_map(
        per_device,
        mesh=fine,
        in_specs=(
            P("st", dom, None, None),
            P(dom, None, None),
            P(dom, None, None, None),
            P(dom, None, None),
            P(dom, None),
            P(),
        ),
        out_specs=P("st", dom, None, None),
        check_vma=False,
    )
```

```python
import jax
import jax.numpy as jnp
from jax import lax
from jax.experimental import pallas as pl
from jax.experimental.pallas import tpu as pltpu
from jax.sharding import Mesh, PartitionSpec as P

center = 8.25
half_width = 7.75

F32 = jnp.float32
BF16 = jnp.bfloat16
F8 = jnp.float8_e4m3fn
NT = (((1,), (1,)), ((), ()))
NN = (((1,), (0,)), ((), ()))
CORES = 2
NO_NAME = 255.0 * 128.0


def passed_along(array, axis, by):
    devices = lax.axis_size(axis)
    return lax.ppermute(array, axis, [(i, (i + by) % devices) for i in range(devices)])


def call(kernel, out_shape, scratch=(), vmem=20, flops=0, nbytes=0, **specs):
    return pl.pallas_call(
        kernel,
        out_shape=out_shape,
        **specs,
        scratch_shapes=list(scratch),
        compiler_params=pltpu.CompilerParams(vmem_limit_bytes=vmem * 2**20),
        cost_estimate=pl.CostEstimate(flops=int(flops), bytes_accessed=int(nbytes), transcendentals=0),
    )


def rows_at(t, states, base=0):
    return pl.ds(pl.multiple_of(base + t * states, states), states)


def lane(y):
    return slice(y * 128, (y + 1) * 128)


def block_mask(rows, cols, row_block, col_block):
    row = lax.broadcasted_iota(jnp.int32, (rows, cols), 0) // row_block
    col = lax.broadcasted_iota(jnp.int32, (rows, cols), 1) // col_block
    return row == col


def project(field, proj, states, slots):
    return of_tiles(lax.dot_general(field, proj, NT, preferred_element_type=F32), states, slots)


def of_tiles(both, states, slots):
    both = jnp.where(block_mask(*both.shape, states, slots), both, 0.0)
    return jnp.sum(both.reshape(-1, states, both.shape[1]), axis=0)


def folded(terms):
    half = terms.shape[1] // 2
    return jnp.concatenate([terms[:, :half], terms[:, half:]], axis=0).astype(BF16)


def unfolded(block):
    block = block.astype(F32)
    states = block.shape[0] // 2
    return jnp.concatenate([block[:states], block[states:]], axis=1)


def write_terms(message, base, block):
    high, width = block.shape[0], message.shape[1]
    for i in range(block.shape[1] // width):
        message[base + i * high : base + (i + 1) * high, :] = block[:, i * width : (i + 1) * width]


def read_terms(message, base, states, count):
    width, high = message.shape[1], 2 * states
    parts = [message[base + i * high : base + (i + 1) * high, :] for i in range(count // high * states // width)]
    return unfolded(jnp.concatenate(parts, axis=1))


def read_names(message, base, count):
    width = message.shape[1]
    digits = message[base : base + 16, :].astype(F32)
    parts = count // width
    names = [digits[i : i + 1] * 128.0 + digits[parts + i : parts + i + 1] for i in range(parts)]
    return jnp.concatenate(names, axis=1)


def halves_kernel(core, cells, mine, theirs):
    planes, height, width = mine.shape
    rows = width // 128
    first = core[0] == 0
    for z in range(planes):
        for pair in range(height // 16):
            for y in range(rows):
                one = cells[z, 2 * rows * pair + y].astype(F32)
                two = cells[z, 2 * rows * pair + rows + y].astype(F32)
                lower = jnp.concatenate([one[:8], two[:8]], axis=0)
                upper = jnp.concatenate([one[8:], two[8:]], axis=0)
                at = slice(pair * 16, pair * 16 + 16)
                mine[z, at, lane(y)] = jnp.where(first, lower, upper).astype(BF16)
                theirs[z, at, lane(y)] = jnp.where(first, upper, lower).astype(BF16)


def spread_rows(digits, rows_of):
    tiles, slots = digits.shape
    cols = tiles * slots
    to = lax.broadcasted_iota(jnp.int32, (slots, cols), 1) % slots
    pick = jnp.where(lax.broadcasted_iota(jnp.int32, (slots, cols), 0) == to, 1.0, 0.0)
    wide = lax.dot_general(digits.astype(BF16), pick.astype(BF16), NN, preferred_element_type=F32)
    return jnp.sum(jnp.where(rows_of, wide, 0.0), axis=0, keepdims=True)


def first_kernel(sizes, core, *refs):
    states, slots, rows = sizes
    ours, others = refs[0:4], refs[4:8]
    names, partial, low, high = refs[8:]
    half, height, width = ours[0].shape
    planes, cols, tiles = CORES * half, ours[1].shape[1], height // states
    rows_of = block_mask(tiles, cols, 1, slots)
    diagonal = block_mask(tiles, tiles, 1, 1)
    slot = (lax.broadcasted_iota(jnp.int32, (1, cols), 1) % slots).astype(F32)
    digits, terms = [], []
    for cells, proj_of, names_of, counts in (ours, others):
        found = []
        for z in range(half):
            terms.append(project(cells[z], proj_of[z], states, slots))
            name = names_of[z].astype(F32)
            top = jnp.floor(name * (1.0 / 128.0))
            count = jnp.broadcast_to(counts[z : z + 1, :].astype(F32), (tiles, tiles))
            count = jnp.sum(jnp.where(diagonal, count, 0.0), axis=1, keepdims=True)
            count = jnp.sum(jnp.where(rows_of, count, 0.0), axis=0, keepdims=True)
            is_used = slot < count
            found.append(jnp.where(is_used, spread_rows(top, rows_of), NO_NAME / 128.0))
            found.append(jnp.where(is_used, spread_rows(name - 128.0 * top, rows_of), 0.0))
        digits.append([jnp.concatenate(found[i::2], axis=1) for i in (0, 1)])
    first = core[0] == 0
    top, bottom = (
        jnp.concatenate([jnp.where(first, a, b), jnp.where(first, b, a)], axis=1)
        for a, b in zip(digits[0], digits[1])
    )
    named = top * 128.0 + bottom
    names[...] = named
    used = jnp.where(named < NO_NAME, 1.0, 0.0)
    mine, theirs = ours[0], others[0]
    for z in range(2):
        at = slice(z * height, (z + 1) * height)
        low[at, :] = jnp.where(first, mine[z], theirs[z])
        high[at, :] = jnp.where(first, theirs[half - 2 + z], mine[half - 2 + z])
    terms = [jnp.where(first, terms[z], terms[(z + half) % planes]) for z in range(planes)]
    terms = [terms[z] * used[:, z * cols : (z + 1) * cols] for z in range(planes)]
    block = folded(jnp.concatenate(terms, axis=1))
    partial[...] = block
    parts = named.shape[1] // width
    lines = [v[:, i * width : (i + 1) * width] for v in (top, bottom) for i in range(parts)]
    lines = jnp.concatenate(lines + [jnp.zeros((16 - 2 * parts, width), F32)], axis=0).astype(BF16)
    for message in (low, high):
        write_terms(message, 2 * height, block)
        message[2 * height + 4 * states : 2 * height + 4 * states + 16, :] = lines


def same_names(names, own, store, wanted):
    for q in range(0, names.shape[1], 128):
        column = jnp.broadcast_to(names[:, q : q + 128], (128, 128)).T
        for p in range(0, own.shape[1], 128):
            if wanted(q, p):
                store(q, p, jnp.where(column == own[:, p : p + 128], 1.0, 0.0))


def doubled(terms):
    return jnp.concatenate([terms, terms], axis=0).astype(BF16)


def in_pieces(terms):
    largest = jnp.maximum(jnp.max(jnp.abs(terms), axis=1, keepdims=True), 1e-30)
    rest = terms * (240.0 / largest)
    pieces = []
    for _ in range(3):
        pieces.append(rest.astype(F8).astype(F32))
        rest = rest - pieces[-1]
    return jnp.concatenate(pieces + [jnp.zeros_like(terms)], axis=0).astype(F8), largest * (1.0 / 240.0)


def from_pieces(sums, scale):
    states = scale.shape[0]
    return (sums[:states] + sums[states : 2 * states] + sums[2 * states : 3 * states]) * scale


def look_up(strength, names):
    top = jnp.floor(names * (1.0 / 128.0))
    bottom = names - 128.0 * top
    lines, count = strength.shape[0], names.shape[1]
    line = lax.broadcasted_iota(jnp.int32, (lines, count), 0).astype(F32)
    pick = jnp.where(line == top, 1.0, 0.0)
    of_line = lax.dot_general(
        strength, pick, (((0,), (0,)), ((), ())), precision=lax.Precision.HIGHEST, preferred_element_type=F32
    )
    place = lax.broadcasted_iota(jnp.int32, (128, count), 0).astype(F32)
    return jnp.sum(jnp.where(place == bottom, of_line, 0.0), axis=0, keepdims=True)


def applied_to(chosen, proj, tiles, mask):
    spread = jnp.broadcast_to(chosen[None], (tiles,) + chosen.shape).reshape(mask.shape)
    spread = jnp.where(mask, spread, 0.0).astype(BF16)
    return lax.dot_general(spread, proj, NN, preferred_element_type=F32)


def inner_planes(planes):
    return range(2, planes - 2)


def local_kernel(sizes, first, *refs):
    states, slots, rows = sizes
    refs = list(refs)
    if first:
        core, own, names, strength = refs[0], refs[7], refs[8], refs[9]
        cur, potential, proj, base, share, inner, table, weight, square, turned = refs[10:]
        half = refs[1].shape[0]
        for start, (cells, values, proj_of) in ((core[0] * half, refs[1:4]), ((1 - core[0]) * half, refs[4:7])):
            for z in range(half):
                cur[start + z] = cells[z].astype(F32)
                potential[start + z] = values[z]
                proj[start + z] = proj_of[z]
        named = names[...]
        mine = jnp.where(named < NO_NAME, named, -1.0)

        def store(q, p, same):
            table[q : q + 128, p : p + 128] = same.astype(F8)

        same_names(named, mine, store, lambda q, p: True)
        weight[...] = look_up(strength[...], named)
    else:
        outer, chosen, done, table, prev, potential, own, proj, cur, base, share, inner = refs
    planes, height, width = cur.shape
    tiles, cols = height // states, proj.shape[1]
    gain = (1.0 if first else 2.0) / half_width
    near, far = -gain * 2.0 / 3.0, gain / 24.0
    terms, scale = in_pieces(unfolded(own[...]))
    share[...] = from_pieces(lax.dot_general(terms, table[...], NN, preferred_element_type=F32), scale)
    if first:
        same_tile = block_mask(cols, cols, slots, slots)
        for i, z in enumerate(inner_planes(planes)):
            products = lax.dot_general(proj[z], proj[z], NT, preferred_element_type=F32)
            square[i] = jnp.where(same_tile, products, 0.0).astype(BF16)
        for i, z in enumerate((0, 1, planes - 2, planes - 1)):
            turned[i] = proj[z].astype(F32).T.astype(BF16)
    else:
        mask = block_mask(height, cols, states, slots)
        for z in range(planes):
            if z in inner_planes(planes):
                cur[z] = done[z] + applied_to(chosen[:, z * cols : (z + 1) * cols], proj[z], tiles, mask)
            else:
                cur[z] = outer[z if z < 2 else z - planes + 4]

    def tile_step(j, carry):
        here = rows_at(j, states)
        left, right = rows_at((j + tiles - 1) % tiles, states), rows_at((j + 1) % tiles, states)

        def load(z, y):
            if y < 0:
                return cur[z, left, lane(y + rows)]
            if y >= rows:
                return cur[z, right, lane(y - rows)]
            return cur[z, here, lane(y)]

        for y in range(rows):
            mids = [load(z, y) for z in range(planes)]
            for z in range(planes):
                mid = mids[z]
                one = load(z, y - 1) + load(z, y + 1)
                two = load(z, y - 2) + load(z, y + 2)
                one += pltpu.roll(mid, 1, 1) + pltpu.roll(mid, 127, 1)
                two += pltpu.roll(mid, 2, 1) + pltpu.roll(mid, 126, 1)
                for by in (-1, 1):
                    if 0 <= z + by < planes:
                        one += mids[z + by]
                    if 0 <= z + 2 * by < planes:
                        two += mids[z + 2 * by]
                shift = potential[z, pl.ds(j * rows + y, 1), :] + (3.75 - center)
                new = near * one + far * two + shift * mid * gain
                if not first:
                    new = new - prev[z, here, lane(y)]
                base[z, here, lane(y)] = new
        return carry

    lax.fori_loop(0, tiles, tile_step, 0)
    for i, z in enumerate(inner_planes(planes)):
        inner[:, i * cols : (i + 1) * cols] = project(base[z].astype(BF16), proj[z], states, slots)


def turn_kernel(sizes, early, core, *refs):
    inputs, refs = refs[:9], refs[9:]
    made, refs = ([], refs) if early else (refs[:10], refs[10:])

    @pl.when((core[0] != 0) if early else (core[0] == 0))
    def _():
        local_kernel(sizes, True, core, *inputs, *refs)

    if not early:

        @pl.when(core[0] != 0)
        def _():
            for ready, out in zip(made, refs):
                out[...] = ready[...]


def step_kernel(sizes, first, last, *refs):
    states, slots, rows = sizes
    refs = list(refs)
    base, share, below, above, weight, names, proj, inner, square, turned = refs[:10]
    rest = refs[10:]
    planes, height, width = base.shape
    tiles = height // states
    cols = proj.shape[1]
    count = planes * cols
    reach = (planes + 1) * cols
    gain = (1.0 if first else 2.0) / half_width
    near, far = -gain * 2.0 / 3.0, gain / 24.0
    table = rest.pop(0)
    if last:
        (nxt, applied) = rest
    else:
        (nxt, low, high, partial, selected, applied) = rest

    named = names[...]
    if first:
        around = [read_names(r, 2 * height + 4 * states, count) for r in (below, above)]
        mine = jnp.where(named < NO_NAME, named, -1.0)

        def store(q, p, same):
            z = p // cols
            table[z, q - z * cols : q - z * cols + 128, p - z * cols : p - z * cols + 128] = same.astype(F8)

        def wanted(q, p):
            return 0 <= q // cols - p // cols <= planes

        same_names(jnp.concatenate(around, axis=1), mine, store, wanted)

    terms = [read_terms(r, 2 * height, states, count) for r in (below, above)]
    terms, scale = in_pieces(jnp.concatenate(terms, axis=1))
    mask = block_mask(height, cols, states, slots)
    used = jnp.where(named < NO_NAME, 1.0, 0.0)
    out = [None] * planes
    for z in range(planes):
        at = slice(z * cols, (z + 1) * cols)
        chosen = lax.dot_general(terms[:, z * cols : z * cols + reach], table[z], NN, preferred_element_type=F32)
        chosen = from_pieces(chosen, scale)
        chosen = (chosen + share[:, at]) * (weight[:, at] * gain)
        if not last:
            selected[:, at] = chosen
        if last or z not in inner_planes(planes):
            applied[z] = applied_to(chosen, proj[z], tiles, mask)
        else:
            i = z - inner_planes(planes)[0]
            of_chosen = lax.dot_general(doubled(chosen), square[i], NN, preferred_element_type=F32)
            out[z] = (inner[:, i * cols : (i + 1) * cols] + of_chosen[:states]) * used[:, at]

    def pair_step(pair, carry):
        here = rows_at(pair, 2 * states)
        for y in range(rows):
            b2, b1 = [below[rows_at(pair, 2 * states, z * height), lane(y)].astype(F32) for z in range(2)]
            a1, a2 = [above[rows_at(pair, 2 * states, z * height), lane(y)].astype(F32) for z in range(2)]
            outer = {0: near * b1 + far * b2, 1: far * b1}
            outer.update({planes - 2: far * a1, planes - 1: near * a1 + far * a2})
            for z in range(planes):
                if not last and z not in outer:
                    continue
                new = base[z, here, lane(y)] + applied[z, here, lane(y)]
                if z in outer:
                    new += outer[z]
                if last:
                    pairs = nxt.shape[1] // (2 * states)
                    parts = tiles // 2 // pairs
                    slab, plane = divmod(z, planes // CORES)
                    block = (plane * parts + pair // pairs) * CORES + slab
                    nxt[block, rows_at(pair % pairs, 2 * states), lane(y)] = new.astype(BF16)
                else:
                    i = z if z < 2 else z - planes + 4
                    nxt[i, here, lane(y)] = new
                    message = low if i < 2 else high
                    message[rows_at(pair, 2 * states, i % 2 * height), lane(y)] = new.astype(BF16)
        return carry

    lax.fori_loop(0, tiles // 2, pair_step, 0)
    if not last:
        for z in range(planes):
            if z in inner_planes(planes):
                continue
            i = z if z < 2 else z - planes + 4
            plane = (low if i < 2 else high)[i % 2 * height : (i % 2 + 1) * height, :]
            both = lax.dot_general(plane, turned[i], NN, preferred_element_type=F32)
            out[z] = of_tiles(both, states, slots) * used[:, z * cols : (z + 1) * cols]
        block = folded(jnp.concatenate(out, axis=1))
        partial[...] = block
        write_terms(low, 2 * height, block)
        write_terms(high, 2 * height, block)


def gram_kernel(states, cells, margin, ordered):
    sources, height, width = cells.shape
    total = jnp.zeros(margin.shape, F32)
    for pair in range(height // (2 * states)):
        both = cells[:, pair * 2 * states : (pair + 1) * 2 * states, :].astype(F32)
        for i in range(2):
            block = both[:, i * states : (i + 1) * states, :].reshape(sources * states, width).astype(BF16)
            ordered[2 * pair + i] = block
            total += lax.dot_general(block, block, NT, preferred_element_type=F32)
    margin[...] = total


def recip(x):
    r = pltpu.reciprocal(x, approx=True)
    r = r * (2.0 - x * r)
    return r

def inverse_factor(margin, inverse):
    n = margin.shape[0]
    lanes = lax.broadcasted_iota(jnp.int32, (8, n), 1)
    eye = lax.broadcasted_iota(jnp.int32, (n, n), 0) == lax.broadcasted_iota(jnp.int32, (n, n), 1)
    full = margin[...]
    diagonal = jnp.where(eye, full, 0.0)
    across = lax.rsqrt(jnp.sum(diagonal, axis=0, keepdims=True))
    down = lax.rsqrt(jnp.sum(diagonal, axis=1, keepdims=True))
    full = full * down * across
    work = [full[8 * i : 8 * i + 8, :] for i in range(n // 8)]
    for k in range(0, n, 8):
        b = k // 8
        wide = [jnp.broadcast_to(work[b][:, k + p : k + p + 1], (8, n)) for p in range(8)]
        s = {(q, p): jnp.broadcast_to(wide[p][q : q + 1, :], (8, n)) for p in range(8) for q in range(p, 8)}
        inside = (lanes >= k) & (lanes < k + 8)
        rows = [
            jnp.where(lanes == k + p, 1.0, jnp.where(inside, 0.0, jnp.broadcast_to(work[b][p : p + 1, :], (8, n))))
            for p in range(8)
        ]
        solved, x = [None] * 8, {}
        for p in range(0, 8, 2):
            a, bb, c = s[p, p], s[p + 1, p], s[p + 1, p + 1]
            det = recip(a * c - bb * bb)
            i00, i01, i11 = c * det, -bb * det, a * det
            for q in range(p + 2, 8):
                x[p, q] = i00 * s[q, p] + i01 * s[q, p + 1]
                x[p + 1, q] = i01 * s[q, p] + i11 * s[q, p + 1]
            for q in range(p + 2, 8):
                for w in range(p + 2, q + 1):
                    s[q, w] = s[q, w] - (s[q, p] * x[p, w] + s[q, p + 1] * x[p + 1, w])
                rows[q] = rows[q] - (x[p, q] * rows[p] + x[p + 1, q] * rows[p + 1])
            solved[p] = i00 * rows[p] + i01 * rows[p + 1]
            solved[p + 1] = i01 * rows[p] + i11 * rows[p + 1]
            ratio = bb * recip(a)
            out = [rows[p] * lax.rsqrt(a), (rows[p + 1] - ratio * rows[p]) * lax.rsqrt(c - bb * ratio)]
            for i in range(2):
                kept = jnp.where(lanes <= k + p + i, out[i], 0.0) * across
                inverse[k + p + i : k + p + i + 1, :] = kept[0:1]
        for p in (4, 2, 0):
            for q in range(p + 2, 8):
                solved[p] = solved[p] - x[p, q] * solved[q]
                solved[p + 1] = solved[p + 1] - x[p + 1, q] * solved[q]
        for i in range(b + 1, n // 8):
            column = [jnp.broadcast_to(work[i][:, k + p : k + p + 1], (8, n)) * solved[p] for p in range(8)]
            change = ((column[0] + column[1]) + (column[2] + column[3])) + ((column[4] + column[5]) + (column[6] + column[7]))
            work[i] = jnp.where(inside, 0.0, work[i]) - change

def rotate_kernel(margin, ordered, rotated, inverse):
    inverse_factor(margin, inverse)
    mine = inverse[...].astype(BF16)
    groups, _, states, _ = rotated.shape
    tiles, nstates, width = ordered.shape
    rows = width // 128
    for j in range(tiles):
        new = lax.dot_general(mine, ordered[j], NN, preferred_element_type=F32).astype(BF16)
        new = new.reshape(groups, states, width)
        for y in range(rows):
            rotated[:, j * rows + y, :, :] = new[:, :, lane(y)]


def per_device(states, potential, proj_values, block_list, tile_count, strength):
    local_states, slab_planes, rows_y, cells_x = states.shape
    _, tiles, slots, tile_cells = proj_values.shape
    rows = rows_y // tiles
    ring, groups = lax.axis_size("ring"), lax.axis_size("st")
    total_cells = slab_planes * rows_y * cells_x * ring * CORES
    share_states, planes = local_states // CORES, slab_planes * CORES
    height, cols, count = tiles * share_states, tiles * slots, planes * tiles * slots
    sizes = (share_states, slots, rows)
    shape = (planes, height, tile_cells)

    f32 = lambda s: jax.ShapeDtypeStruct(s, F32)
    bf16 = lambda s: jax.ShapeDtypeStruct(s, BF16)
    whole, scalar = pl.BlockSpec(), pl.BlockSpec(memory_space=pltpu.SMEM)

    def swapped(array):
        return lax.ppermute(array, "core", [(0, 1), (1, 0)])

    core = lax.axis_index("core").astype(jnp.int32).reshape(1)
    proj_own = proj_values.reshape(slab_planes, cols, tile_cells).astype(BF16)
    ours = [proj_own, block_list, tile_count]
    others = [swapped(array) for array in ours]
    potential_others = swapped(potential)
    piece = bf16((slab_planes, height, tile_cells))
    mine, theirs = call(
        halves_kernel, (piece, piece), in_specs=[scalar, whole], flops=10**7, nbytes=2 * 2**20
    )(core, states.transpose(1, 2, 0, 3))
    got = swapped(theirs)

    def sent(names):
        message = (2 * height + 4 * share_states + (16 if names else 0), tile_cells)
        return [bf16((2 * share_states, count // 2)), bf16(message), bf16(message)]

    names, partial, low, high = call(
        lambda *r: first_kernel(sizes, *r),
        [f32((1, count))] + sent(True),
        in_specs=[scalar] + [whole] * 8,
        flops=10**9, nbytes=8 * 2**20,
    )(core, mine, *ours, got, *others)

    inside = len(inner_planes(planes))
    prev = cur = outer = None
    for m in range(4):
        first, last = m == 0, m == 3
        outs = [f32(shape), f32((share_states, count)), f32((share_states, inside * cols))]
        if first:
            args = [core, mine, potential, ours[0], got, potential_others, others[0]]
            args += [partial, names, strength.reshape(-1, 128)]
            outs = [f32(shape), f32((planes, rows_y, cells_x)), bf16((planes, cols, tile_cells))] + outs
            outs += [jax.ShapeDtypeStruct((count, count), F8), f32((1, count)), bf16((inside, cols, cols)), bf16((4, tile_cells, cols))]
            made = call(
                lambda *r: turn_kernel(sizes, True, *r), outs,
                in_specs=[scalar] + [whole] * 9, flops=1e9, nbytes=8 * 2**20,
            )(*args)
            low, high, *made = lax.optimization_barrier((low, high, *made))
        below = passed_along(high, "ring", 1)
        above = passed_along(low, "ring", -1)
        if first:
            cur, shift, proj, base, share, inner, own_table, weight, square, turned = call(
                lambda *r: turn_kernel(sizes, False, *r), outs,
                in_specs=[scalar] + [whole] * 19, flops=1e9, nbytes=8 * 2**20,
            )(*args, *made)
        else:
            after, base, share, inner = call(
                lambda *r: local_kernel(sizes, False, *r), [f32(shape)] + outs, flops=1e9, nbytes=8 * 2**20
            )(outer, chosen, base, own_table, prev, shift, partial, proj)
            prev, cur = cur, after
        args = [base, share, below, above, weight, names, proj, inner, square, turned] + ([] if first else [table])
        outs = [jax.ShapeDtypeStruct((planes, (planes + 1) * cols, cols), F8)] if first else []
        if last:
            outs += [bf16((CORES * groups, planes * height // (CORES * groups), tile_cells))]
        else:
            made = sent(False)
            outs += [f32((4, height, tile_cells)), made[1], made[2], made[0], f32((share_states, count))]
        got = call(
            lambda *r, first=first, last=last: step_kernel(sizes, first, last, *r),
            outs, scratch=[pltpu.VMEM(shape, F32)], flops=1e9, nbytes=8 * 2**20,
        )(*args)
        if first:
            table, *got = got
        if last:
            (filtered,) = got
        else:
            outer, low, high, partial, chosen = got
            prev = cur

    cells = lax.all_to_all(filtered, ("st", "core"), 0, 0, tiled=True)
    nstates = groups * local_states
    own_tiles = cells.shape[1] // share_states
    part, ordered = call(
        lambda *r: gram_kernel(share_states, *r),
        (f32((nstates, nstates)), bf16((own_tiles, nstates, tile_cells))),
        flops=1e8, nbytes=2**20,
    )(cells)
    everywhere = ("ring", "core", "st")
    devices = ring * CORES * groups
    per = nstates // devices
    total = lax.all_to_all(part.reshape(devices, per, nstates), everywhere, 0, 0, tiled=True)
    total = jnp.sum(total, axis=0, keepdims=True) / total_cells
    margin = lax.all_to_all(jnp.broadcast_to(total, (devices, per, nstates)), everywhere, 0, 0, tiled=True)
    rotated = call(
        rotate_kernel,
        bf16((groups, slab_planes * rows_y // groups, local_states, cells_x)),
        scratch=[pltpu.VMEM((nstates, nstates), F32)],
        flops=2e8, nbytes=2**21,
    )(margin.reshape(nstates, nstates), ordered)
    rotated = lax.all_to_all(rotated, "st", 0, 0, tiled=True)
    return rotated.reshape(slab_planes, rows_y, local_states, cells_x).transpose(2, 0, 1, 3)


def solution(mesh):
    fine = Mesh(mesh.devices.reshape(-1, CORES, mesh.shape["st"]), ("ring", "core", "st"))
    dom = ("ring", "core")
    return jax.shard_map(
        per_device,
        mesh=fine,
        in_specs=(
            P("st", dom, None, None),
            P(dom, None, None),
            P(dom, None, None, None),
            P(dom, None, None),
            P(dom, None),
            P(),
        ),
        out_specs=P("st", dom, None, None),
        check_vma=False,
    )
```

```python
import jax
import jax.numpy as jnp
from jax import lax
from jax.experimental import pallas as pl
from jax.experimental.pallas import tpu as pltpu
from jax.sharding import Mesh, PartitionSpec as P

center = 8.25
half_width = 7.75

F32 = jnp.float32
BF16 = jnp.bfloat16
F8 = jnp.float8_e4m3fn
NT = (((1,), (1,)), ((), ()))
NN = (((1,), (0,)), ((), ()))
CORES = 2
NO_NAME = 255.0 * 128.0


def passed_along(array, axis, by):
    devices = lax.axis_size(axis)
    return lax.ppermute(array, axis, [(i, (i + by) % devices) for i in range(devices)])


def call(kernel, out_shape, scratch=(), vmem=12, flops=0, nbytes=0, **specs):
    return pl.pallas_call(
        kernel,
        out_shape=out_shape,
        **specs,
        scratch_shapes=list(scratch),
        compiler_params=pltpu.CompilerParams(vmem_limit_bytes=vmem * 2**20),
        cost_estimate=pl.CostEstimate(flops=int(flops), bytes_accessed=int(nbytes), transcendentals=0),
    )


def rows_at(t, states, base=0):
    return pl.ds(pl.multiple_of(base + t * states, states), states)


def lane(y):
    return slice(y * 128, (y + 1) * 128)


def block_mask(rows, cols, row_block, col_block):
    row = lax.broadcasted_iota(jnp.int32, (rows, cols), 0) // row_block
    col = lax.broadcasted_iota(jnp.int32, (rows, cols), 1) // col_block
    return row == col


def project(field, proj, states, slots):
    return of_tiles(lax.dot_general(field, proj, NT, preferred_element_type=F32), states, slots)


def of_tiles(both, states, slots):
    both = jnp.where(block_mask(*both.shape, states, slots), both, 0.0)
    return jnp.sum(both.reshape(-1, states, both.shape[1]), axis=0)


def folded(terms):
    half = terms.shape[1] // 2
    return jnp.concatenate([terms[:, :half], terms[:, half:]], axis=0).astype(BF16)


def unfolded(block):
    block = block.astype(F32)
    states = block.shape[0] // 2
    return jnp.concatenate([block[:states], block[states:]], axis=1)


def write_terms(message, base, block):
    high, width = block.shape[0], message.shape[1]
    for i in range(block.shape[1] // width):
        message[base + i * high : base + (i + 1) * high, :] = block[:, i * width : (i + 1) * width]


def read_terms(message, base, states, count):
    width, high = message.shape[1], 2 * states
    parts = [message[base + i * high : base + (i + 1) * high, :] for i in range(count // high * states // width)]
    return unfolded(jnp.concatenate(parts, axis=1))


def read_names(message, base, count):
    width = message.shape[1]
    digits = message[base : base + 16, :].astype(F32)
    parts = count // width
    names = [digits[i : i + 1] * 128.0 + digits[parts + i : parts + i + 1] for i in range(parts)]
    return jnp.concatenate(names, axis=1)


def halves_kernel(core, cells, mine, theirs):
    planes, height, width = mine.shape
    rows = width // 128
    first = core[0] == 0
    for z in range(planes):
        for pair in range(height // 16):
            for y in range(rows):
                one = cells[z, 2 * rows * pair + y].astype(F32)
                two = cells[z, 2 * rows * pair + rows + y].astype(F32)
                lower = jnp.concatenate([one[:8], two[:8]], axis=0)
                upper = jnp.concatenate([one[8:], two[8:]], axis=0)
                at = slice(pair * 16, pair * 16 + 16)
                mine[z, at, lane(y)] = jnp.where(first, lower, upper).astype(BF16)
                theirs[z, at, lane(y)] = jnp.where(first, upper, lower).astype(BF16)


def spread_rows(digits, rows_of):
    tiles, slots = digits.shape
    cols = tiles * slots
    to = lax.broadcasted_iota(jnp.int32, (slots, cols), 1) % slots
    pick = jnp.where(lax.broadcasted_iota(jnp.int32, (slots, cols), 0) == to, 1.0, 0.0)
    wide = lax.dot_general(digits.astype(BF16), pick.astype(BF16), NN, preferred_element_type=F32)
    return jnp.sum(jnp.where(rows_of, wide, 0.0), axis=0, keepdims=True)


def first_kernel(sizes, core, *refs):
    states, slots, rows = sizes
    ours, others = refs[0:4], refs[4:8]
    names, partial, low, high = refs[8:]
    half, height, width = ours[0].shape
    planes, cols, tiles = CORES * half, ours[1].shape[1], height // states
    rows_of = block_mask(tiles, cols, 1, slots)
    diagonal = block_mask(tiles, tiles, 1, 1)
    slot = (lax.broadcasted_iota(jnp.int32, (1, cols), 1) % slots).astype(F32)
    digits, terms = [], []
    for cells, proj_of, names_of, counts in (ours, others):
        found = []
        for z in range(half):
            terms.append(project(cells[z], proj_of[z], states, slots))
            name = names_of[z].astype(F32)
            top = jnp.floor(name * (1.0 / 128.0))
            count = jnp.broadcast_to(counts[z : z + 1, :].astype(F32), (tiles, tiles))
            count = jnp.sum(jnp.where(diagonal, count, 0.0), axis=1, keepdims=True)
            count = jnp.sum(jnp.where(rows_of, count, 0.0), axis=0, keepdims=True)
            is_used = slot < count
            found.append(jnp.where(is_used, spread_rows(top, rows_of), NO_NAME / 128.0))
            found.append(jnp.where(is_used, spread_rows(name - 128.0 * top, rows_of), 0.0))
        digits.append([jnp.concatenate(found[i::2], axis=1) for i in (0, 1)])
    first = core[0] == 0
    top, bottom = (
        jnp.concatenate([jnp.where(first, a, b), jnp.where(first, b, a)], axis=1)
        for a, b in zip(digits[0], digits[1])
    )
    named = top * 128.0 + bottom
    names[...] = named
    used = jnp.where(named < NO_NAME, 1.0, 0.0)
    mine, theirs = ours[0], others[0]
    for z in range(2):
        at = slice(z * height, (z + 1) * height)
        low[at, :] = jnp.where(first, mine[z], theirs[z])
        high[at, :] = jnp.where(first, theirs[half - 2 + z], mine[half - 2 + z])
    terms = [jnp.where(first, terms[z], terms[(z + half) % planes]) for z in range(planes)]
    terms = [terms[z] * used[:, z * cols : (z + 1) * cols] for z in range(planes)]
    terms = jnp.concatenate(terms, axis=1)
    partial[...] = terms
    block = folded(terms)
    parts = named.shape[1] // width
    lines = [v[:, i * width : (i + 1) * width] for v in (top, bottom) for i in range(parts)]
    lines = jnp.concatenate(lines + [jnp.zeros((16 - 2 * parts, width), F32)], axis=0).astype(BF16)
    for message in (low, high):
        write_terms(message, 2 * height, block)
        message[2 * height + 4 * states : 2 * height + 4 * states + 16, :] = lines


def same_names(names, own, store, wanted):
    for q in range(0, names.shape[1], 128):
        column = jnp.broadcast_to(names[:, q : q + 128], (128, 128)).T
        for p in range(0, own.shape[1], 128):
            if wanted(q, p):
                store(q, p, jnp.where(column == own[:, p : p + 128], 1.0, 0.0))


def doubled(terms):
    return jnp.concatenate([terms, terms], axis=0).astype(BF16)


def in_pieces(terms):
    largest = jnp.maximum(jnp.max(jnp.abs(terms), axis=1, keepdims=True), 1e-30)
    rest = terms * (240.0 / largest)
    pieces = []
    for _ in range(3):
        pieces.append(rest.astype(F8).astype(F32))
        rest = rest - pieces[-1]
    return jnp.concatenate(pieces + [jnp.zeros_like(terms)], axis=0).astype(F8), largest * (1.0 / 240.0)


def from_pieces(sums, scale):
    states = scale.shape[0]
    return (sums[:states] + sums[states : 2 * states] + sums[2 * states : 3 * states]) * scale


def look_up(strength, names):
    top = jnp.floor(names * (1.0 / 128.0))
    bottom = names - 128.0 * top
    lines, count = strength.shape[0], names.shape[1]
    line = lax.broadcasted_iota(jnp.int32, (lines, count), 0).astype(F32)
    pick = jnp.where(line == top, 1.0, 0.0)
    of_line = lax.dot_general(
        strength, pick, (((0,), (0,)), ((), ())), precision=lax.Precision.HIGHEST, preferred_element_type=F32
    )
    place = lax.broadcasted_iota(jnp.int32, (128, count), 0).astype(F32)
    return jnp.sum(jnp.where(place == bottom, of_line, 0.0), axis=0, keepdims=True)


def applied_to(chosen, proj, tiles, mask):
    spread = jnp.broadcast_to(chosen[None], (tiles,) + chosen.shape).reshape(mask.shape)
    spread = jnp.where(mask, spread, 0.0).astype(BF16)
    return lax.dot_general(spread, proj, NN, preferred_element_type=F32)


def inner_planes(planes):
    return range(2, planes - 2)


def local_kernel(sizes, first, *refs):
    states, slots, rows = sizes
    refs = list(refs)
    if first:
        core, own, names, strength = refs[0], refs[7], refs[8], refs[9]
        cur, potential, proj, base, share, inner, table, weight, square, turned = refs[10:]
        half = refs[1].shape[0]
        for start, (cells, values, proj_of) in ((core[0] * half, refs[1:4]), ((1 - core[0]) * half, refs[4:7])):
            for z in range(half):
                cur[start + z] = cells[z].astype(F32)
                potential[start + z] = values[z]
                proj[start + z] = proj_of[z]
        named = names[...]
        mine = jnp.where(named < NO_NAME, named, -1.0)

        def store(q, p, same):
            table[q : q + 128, p : p + 128] = same.astype(BF16)

        same_names(named, mine, store, lambda q, p: True)
        weight[...] = look_up(strength[...], named)
    else:
        outer, chosen, done, table, prev, potential, own, proj, cur, base, share, inner = refs
    planes, height, width = cur.shape
    tiles, cols = height // states, proj.shape[1]
    gain = (1.0 if first else 2.0) / half_width
    near, far = -gain * 2.0 / 3.0, gain / 24.0
    rest, pieces = own[...], []
    for _ in range(3):
        pieces.append(rest.astype(BF16).astype(F32))
        rest = rest - pieces[-1]
    terms = jnp.concatenate(pieces + [jnp.zeros_like(rest)], axis=0).astype(BF16)
    sums = lax.dot_general(terms, table[...], NN, preferred_element_type=F32)
    share[...] = sums[:states] + sums[states : 2 * states] + sums[2 * states : 3 * states]
    if first:
        same_tile = block_mask(cols, cols, slots, slots)
        for i, z in enumerate(inner_planes(planes)):
            products = lax.dot_general(proj[z], proj[z], NT, preferred_element_type=F32)
            square[i] = jnp.where(same_tile, products, 0.0).astype(BF16)
        for i, z in enumerate((0, 1, planes - 2, planes - 1)):
            turned[i] = proj[z].astype(F32).T.astype(BF16)
    else:
        mask = block_mask(height, cols, states, slots)
        for z in range(planes):
            if z in inner_planes(planes):
                cur[z] = done[z] + applied_to(chosen[:, z * cols : (z + 1) * cols], proj[z], tiles, mask)
            else:
                cur[z] = outer[z if z < 2 else z - planes + 4]

    def tile_step(j, carry):
        here = rows_at(j, states)
        left, right = rows_at((j + tiles - 1) % tiles, states), rows_at((j + 1) % tiles, states)

        def load(z, y):
            if y < 0:
                return cur[z, left, lane(y + rows)]
            if y >= rows:
                return cur[z, right, lane(y - rows)]
            return cur[z, here, lane(y)]

        for y in range(rows):
            mids = [load(z, y) for z in range(planes)]
            for z in range(planes):
                mid = mids[z]
                one = load(z, y - 1) + load(z, y + 1)
                two = load(z, y - 2) + load(z, y + 2)
                one += pltpu.roll(mid, 1, 1) + pltpu.roll(mid, 127, 1)
                two += pltpu.roll(mid, 2, 1) + pltpu.roll(mid, 126, 1)
                for by in (-1, 1):
                    if 0 <= z + by < planes:
                        one += mids[z + by]
                    if 0 <= z + 2 * by < planes:
                        two += mids[z + 2 * by]
                shift = potential[z, pl.ds(j * rows + y, 1), :] + (3.75 - center)
                new = near * one + far * two + shift * mid * gain
                if not first:
                    new = new - prev[z, here, lane(y)]
                base[z, here, lane(y)] = new
        return carry

    lax.fori_loop(0, tiles, tile_step, 0)
    for i, z in enumerate(inner_planes(planes)):
        inner[:, i * cols : (i + 1) * cols] = project(base[z].astype(BF16), proj[z], states, slots)


def turn_kernel(sizes, early, core, *refs):
    inputs, refs = refs[:9], refs[9:]
    made, refs = ([], refs) if early else (refs[:10], refs[10:])

    @pl.when((core[0] != 0) if early else (core[0] == 0))
    def _():
        local_kernel(sizes, True, core, *inputs, *refs)

    if not early:

        @pl.when(core[0] != 0)
        def _():
            for ready, out in zip(made, refs):
                out[...] = ready[...]


def step_kernel(sizes, first, last, *refs):
    states, slots, rows = sizes
    refs = list(refs)
    base, share, below, above, weight, names, proj, inner, square, turned = refs[:10]
    rest = refs[10:]
    planes, height, width = base.shape
    tiles = height // states
    cols = proj.shape[1]
    count = planes * cols
    reach = (planes + 1) * cols
    gain = (1.0 if first else 2.0) / half_width
    near, far = -gain * 2.0 / 3.0, gain / 24.0
    table = rest.pop(0)
    if last:
        (nxt, applied) = rest
    else:
        (nxt, low, high, partial, selected, applied) = rest

    named = names[...]
    if first:
        around = [read_names(r, 2 * height + 4 * states, count) for r in (below, above)]
        mine = jnp.where(named < NO_NAME, named, -1.0)

        def store(q, p, same):
            z = p // cols
            table[z, q - z * cols : q - z * cols + 128, p - z * cols : p - z * cols + 128] = same.astype(F8)

        def wanted(q, p):
            return 0 <= q // cols - p // cols <= planes

        same_names(jnp.concatenate(around, axis=1), mine, store, wanted)

    terms = [read_terms(r, 2 * height, states, count) for r in (below, above)]
    terms, scale = in_pieces(jnp.concatenate(terms, axis=1))
    mask = block_mask(height, cols, states, slots)
    used = jnp.where(named < NO_NAME, 1.0, 0.0)
    out = [None] * planes
    for z in range(planes):
        at = slice(z * cols, (z + 1) * cols)
        chosen = lax.dot_general(terms[:, z * cols : z * cols + reach], table[z], NN, preferred_element_type=F32)
        chosen = from_pieces(chosen, scale)
        chosen = (chosen + share[:, at]) * (weight[:, at] * gain)
        if not last:
            selected[:, at] = chosen
        if last or z not in inner_planes(planes):
            applied[z] = applied_to(chosen, proj[z], tiles, mask)
        else:
            i = z - inner_planes(planes)[0]
            of_chosen = lax.dot_general(doubled(chosen), square[i], NN, preferred_element_type=F32)
            out[z] = (inner[:, i * cols : (i + 1) * cols] + of_chosen[:states]) * used[:, at]

    def pair_step(pair, carry):
        here = rows_at(pair, 2 * states)
        for y in range(rows):
            b2, b1 = [below[rows_at(pair, 2 * states, z * height), lane(y)].astype(F32) for z in range(2)]
            a1, a2 = [above[rows_at(pair, 2 * states, z * height), lane(y)].astype(F32) for z in range(2)]
            outer = {0: near * b1 + far * b2, 1: far * b1}
            outer.update({planes - 2: far * a1, planes - 1: near * a1 + far * a2})
            for z in range(planes):
                if not last and z not in outer:
                    continue
                new = base[z, here, lane(y)] + applied[z, here, lane(y)]
                if z in outer:
                    new += outer[z]
                if last:
                    pairs = nxt.shape[1] // (2 * states)
                    parts = tiles // 2 // pairs
                    slab, plane = divmod(z, planes // CORES)
                    block = (plane * parts + pair // pairs) * CORES + slab
                    nxt[block, rows_at(pair % pairs, 2 * states), lane(y)] = new.astype(BF16)
                else:
                    i = z if z < 2 else z - planes + 4
                    nxt[i, here, lane(y)] = new
                    message = low if i < 2 else high
                    message[rows_at(pair, 2 * states, i % 2 * height), lane(y)] = new.astype(BF16)
        return carry

    lax.fori_loop(0, tiles // 2, pair_step, 0)
    if not last:
        for z in range(planes):
            if z in inner_planes(planes):
                continue
            i = z if z < 2 else z - planes + 4
            plane = (low if i < 2 else high)[i % 2 * height : (i % 2 + 1) * height, :]
            both = lax.dot_general(plane, turned[i], NN, preferred_element_type=F32)
            out[z] = of_tiles(both, states, slots) * used[:, z * cols : (z + 1) * cols]
        out = jnp.concatenate(out, axis=1)
        partial[...] = out
        block = folded(out)
        write_terms(low, 2 * height, block)
        write_terms(high, 2 * height, block)


def gram_kernel(states, cells, margin, ordered):
    sources, height, width = cells.shape
    total = jnp.zeros(margin.shape, F32)
    for pair in range(height // (2 * states)):
        both = cells[:, pair * 2 * states : (pair + 1) * 2 * states, :].astype(F32)
        for i in range(2):
            block = both[:, i * states : (i + 1) * states, :].reshape(sources * states, width).astype(BF16)
            ordered[2 * pair + i] = block
            total += lax.dot_general(block, block, NT, preferred_element_type=F32)
    margin[...] = total


def recip(x):
    r = pltpu.reciprocal(x, approx=True)
    r = r * (2.0 - x * r)
    return r

def inverse_factor(margin, inverse):
    n = margin.shape[0]
    lanes = lax.broadcasted_iota(jnp.int32, (8, n), 1)
    eye = lax.broadcasted_iota(jnp.int32, (n, n), 0) == lax.broadcasted_iota(jnp.int32, (n, n), 1)
    full = margin[...]
    diagonal = jnp.where(eye, full, 0.0)
    across = lax.rsqrt(jnp.sum(diagonal, axis=0, keepdims=True))
    down = lax.rsqrt(jnp.sum(diagonal, axis=1, keepdims=True))
    full = full * down * across
    work = [full[8 * i : 8 * i + 8, :] for i in range(n // 8)]
    for k in range(0, n, 8):
        b = k // 8
        wide = [jnp.broadcast_to(work[b][:, k + p : k + p + 1], (8, n)) for p in range(8)]
        s = {(q, p): jnp.broadcast_to(wide[p][q : q + 1, :], (8, n)) for p in range(8) for q in range(p, 8)}
        inside = (lanes >= k) & (lanes < k + 8)
        rows = [
            jnp.where(lanes == k + p, 1.0, jnp.where(inside, 0.0, jnp.broadcast_to(work[b][p : p + 1, :], (8, n))))
            for p in range(8)
        ]
        solved, x = [None] * 8, {}
        for p in range(0, 8, 2):
            a, bb, c = s[p, p], s[p + 1, p], s[p + 1, p + 1]
            det = recip(a * c - bb * bb)
            i00, i01, i11 = c * det, -bb * det, a * det
            for q in range(p + 2, 8):
                x[p, q] = i00 * s[q, p] + i01 * s[q, p + 1]
                x[p + 1, q] = i01 * s[q, p] + i11 * s[q, p + 1]
            for q in range(p + 2, 8):
                for w in range(p + 2, q + 1):
                    s[q, w] = s[q, w] - (s[q, p] * x[p, w] + s[q, p + 1] * x[p + 1, w])
                rows[q] = rows[q] - (x[p, q] * rows[p] + x[p + 1, q] * rows[p + 1])
            solved[p] = i00 * rows[p] + i01 * rows[p + 1]
            solved[p + 1] = i01 * rows[p] + i11 * rows[p + 1]
            ratio = bb * recip(a)
            out = [rows[p] * lax.rsqrt(a), (rows[p + 1] - ratio * rows[p]) * lax.rsqrt(c - bb * ratio)]
            for i in range(2):
                kept = jnp.where(lanes <= k + p + i, out[i], 0.0) * across
                inverse[k + p + i : k + p + i + 1, :] = kept[0:1]
        for p in (4, 2, 0):
            for q in range(p + 2, 8):
                solved[p] = solved[p] - x[p, q] * solved[q]
                solved[p + 1] = solved[p + 1] - x[p + 1, q] * solved[q]
        for i in range(b + 1, n // 8):
            column = [jnp.broadcast_to(work[i][:, k + p : k + p + 1], (8, n)) * solved[p] for p in range(8)]
            change = ((column[0] + column[1]) + (column[2] + column[3])) + ((column[4] + column[5]) + (column[6] + column[7]))
            work[i] = jnp.where(inside, 0.0, work[i]) - change

def rotate_kernel(margin, ordered, rotated, inverse):
    inverse_factor(margin, inverse)
    mine = inverse[...].astype(BF16)
    groups, _, states, _ = rotated.shape
    tiles, nstates, width = ordered.shape
    rows = width // 128
    for j in range(tiles):
        new = lax.dot_general(mine, ordered[j], NN, preferred_element_type=F32).astype(BF16)
        new = new.reshape(groups, states, width)
        for y in range(rows):
            rotated[:, j * rows + y, :, :] = new[:, :, lane(y)]


def per_device(states, potential, proj_values, block_list, tile_count, strength):
    local_states, slab_planes, rows_y, cells_x = states.shape
    _, tiles, slots, tile_cells = proj_values.shape
    rows = rows_y // tiles
    ring, groups = lax.axis_size("ring"), lax.axis_size("st")
    total_cells = slab_planes * rows_y * cells_x * ring * CORES
    share_states, planes = local_states // CORES, slab_planes * CORES
    height, cols, count = tiles * share_states, tiles * slots, planes * tiles * slots
    sizes = (share_states, slots, rows)
    shape = (planes, height, tile_cells)

    f32 = lambda s: jax.ShapeDtypeStruct(s, F32)
    bf16 = lambda s: jax.ShapeDtypeStruct(s, BF16)
    whole, scalar = pl.BlockSpec(), pl.BlockSpec(memory_space=pltpu.SMEM)

    def swapped(array):
        return lax.ppermute(array, "core", [(0, 1), (1, 0)])

    core = lax.axis_index("core").astype(jnp.int32).reshape(1)
    proj_own = proj_values.reshape(slab_planes, cols, tile_cells).astype(BF16)
    ours = [proj_own, block_list, tile_count]
    others = [swapped(array) for array in ours]
    potential_others = swapped(potential)
    piece = bf16((slab_planes, height, tile_cells))
    mine, theirs = call(
        halves_kernel, (piece, piece), in_specs=[scalar, whole], flops=10**7, nbytes=2 * 2**20
    )(core, states.transpose(1, 2, 0, 3))
    got = swapped(theirs)

    def sent(names):
        message = (2 * height + 4 * share_states + (16 if names else 0), tile_cells)
        return [f32((share_states, count)), bf16(message), bf16(message)]

    names, partial, low, high = call(
        lambda *r: first_kernel(sizes, *r),
        [f32((1, count))] + sent(True),
        in_specs=[scalar] + [whole] * 8,
        flops=10**9, nbytes=8 * 2**20,
    )(core, mine, *ours, got, *others)

    inside = len(inner_planes(planes))
    prev = cur = outer = None
    for m in range(4):
        first, last = m == 0, m == 3
        outs = [f32(shape), f32((share_states, count)), f32((share_states, inside * cols))]
        if first:
            args = [core, mine, potential, ours[0], got, potential_others, others[0]]
            args += [partial, names, strength.reshape(-1, 128)]
            outs = [f32(shape), f32((planes, rows_y, cells_x)), bf16((planes, cols, tile_cells))] + outs
            outs += [bf16((count, count)), f32((1, count)), bf16((inside, cols, cols)), bf16((4, tile_cells, cols))]
            made = call(
                lambda *r: turn_kernel(sizes, True, *r), outs,
                in_specs=[scalar] + [whole] * 9, flops=1e9, nbytes=8 * 2**20,
            )(*args)
            low, high, *made = lax.optimization_barrier((low, high, *made))
        below = passed_along(high, "ring", 1)
        above = passed_along(low, "ring", -1)
        if first:
            cur, shift, proj, base, share, inner, own_table, weight, square, turned = call(
                lambda *r: turn_kernel(sizes, False, *r), outs,
                in_specs=[scalar] + [whole] * 19, flops=1e9, nbytes=8 * 2**20,
            )(*args, *made)
        else:
            after, base, share, inner = call(
                lambda *r: local_kernel(sizes, False, *r), [f32(shape)] + outs, flops=1e9, nbytes=8 * 2**20
            )(outer, chosen, base, own_table, prev, shift, partial, proj)
            prev, cur = cur, after
        args = [base, share, below, above, weight, names, proj, inner, square, turned] + ([] if first else [table])
        outs = [jax.ShapeDtypeStruct((planes, (planes + 1) * cols, cols), F8)] if first else []
        if last:
            outs += [bf16((CORES * groups, planes * height // (CORES * groups), tile_cells))]
        else:
            made = sent(False)
            outs += [f32((4, height, tile_cells)), made[1], made[2], made[0], f32((share_states, count))]
        got = call(
            lambda *r, first=first, last=last: step_kernel(sizes, first, last, *r),
            outs, scratch=[pltpu.VMEM(shape, F32)], flops=1e9, nbytes=8 * 2**20,
        )(*args)
        if first:
            table, *got = got
        if last:
            (filtered,) = got
        else:
            outer, low, high, partial, chosen = got
            prev = cur

    cells = lax.all_to_all(filtered, ("st", "core"), 0, 0, tiled=True)
    nstates = groups * local_states
    own_tiles = cells.shape[1] // share_states
    part, ordered = call(
        lambda *r: gram_kernel(share_states, *r),
        (f32((nstates, nstates)), bf16((own_tiles, nstates, tile_cells))),
        flops=1e8, nbytes=2**20,
    )(cells)
    everywhere = ("ring", "core", "st")
    devices = ring * CORES * groups
    per = nstates // devices
    total = lax.all_to_all(part.reshape(devices, per, nstates), everywhere, 0, 0, tiled=True)
    total = jnp.sum(total, axis=0, keepdims=True) / total_cells
    margin = lax.all_to_all(jnp.broadcast_to(total, (devices, per, nstates)), everywhere, 0, 0, tiled=True)
    rotated = call(
        rotate_kernel,
        bf16((groups, slab_planes * rows_y // groups, local_states, cells_x)),
        scratch=[pltpu.VMEM((nstates, nstates), F32)],
        flops=2e8, nbytes=2**21,
    )(margin.reshape(nstates, nstates), ordered)
    rotated = lax.all_to_all(rotated, "st", 0, 0, tiled=True)
    return rotated.reshape(slab_planes, rows_y, local_states, cells_x).transpose(2, 0, 1, 3)


def solution(mesh):
    fine = Mesh(mesh.devices.reshape(-1, CORES, mesh.shape["st"]), ("ring", "core", "st"))
    dom = ("ring", "core")
    return jax.shard_map(
        per_device,
        mesh=fine,
        in_specs=(
            P("st", dom, None, None),
            P(dom, None, None),
            P(dom, None, None, None),
            P(dom, None, None),
            P(dom, None),
            P(),
        ),
        out_specs=P("st", dom, None, None),
        check_vma=False,
    )
```

```python
import jax
import jax.numpy as jnp
from jax import lax
from jax.experimental import pallas as pl
from jax.experimental.pallas import tpu as pltpu
from jax.sharding import Mesh, PartitionSpec as P

center = 8.25
half_width = 7.75

F32 = jnp.float32
BF16 = jnp.bfloat16
F8 = jnp.float8_e4m3fn
NT = (((1,), (1,)), ((), ()))
NN = (((1,), (0,)), ((), ()))
CORES = 2
NO_NAME = 255.0 * 128.0


def passed_along(array, axis, by):
    devices = lax.axis_size(axis)
    return lax.ppermute(array, axis, [(i, (i + by) % devices) for i in range(devices)])


def call(kernel, out_shape, scratch=(), vmem=12, flops=0, nbytes=0, **specs):
    return pl.pallas_call(
        kernel,
        out_shape=out_shape,
        **specs,
        scratch_shapes=list(scratch),
        compiler_params=pltpu.CompilerParams(vmem_limit_bytes=vmem * 2**20),
        cost_estimate=pl.CostEstimate(flops=int(flops), bytes_accessed=int(nbytes), transcendentals=0),
    )


def rows_at(t, states, base=0):
    return pl.ds(pl.multiple_of(base + t * states, states), states)


def lane(y):
    return slice(y * 128, (y + 1) * 128)


def block_mask(rows, cols, row_block, col_block):
    row = lax.broadcasted_iota(jnp.int32, (rows, cols), 0) // row_block
    col = lax.broadcasted_iota(jnp.int32, (rows, cols), 1) // col_block
    return row == col


def project(field, proj, states, slots):
    return of_tiles(lax.dot_general(field, proj, NT, preferred_element_type=F32), states, slots)


def of_tiles(both, states, slots):
    both = jnp.where(block_mask(*both.shape, states, slots), both, 0.0)
    return jnp.sum(both.reshape(-1, states, both.shape[1]), axis=0)


def folded(terms):
    half = terms.shape[1] // 2
    return jnp.concatenate([terms[:, :half], terms[:, half:]], axis=0).astype(BF16)


def unfolded(block):
    block = block.astype(F32)
    states = block.shape[0] // 2
    return jnp.concatenate([block[:states], block[states:]], axis=1)


def write_terms(message, base, block):
    high, width = block.shape[0], message.shape[1]
    for i in range(block.shape[1] // width):
        message[base + i * high : base + (i + 1) * high, :] = block[:, i * width : (i + 1) * width]


def read_terms(message, base, states, count):
    width, high = message.shape[1], 2 * states
    parts = [message[base + i * high : base + (i + 1) * high, :] for i in range(count // high * states // width)]
    return unfolded(jnp.concatenate(parts, axis=1))


def read_names(message, base, count):
    width = message.shape[1]
    digits = message[base : base + 16, :].astype(F32)
    parts = count // width
    names = [digits[i : i + 1] * 128.0 + digits[parts + i : parts + i + 1] for i in range(parts)]
    return jnp.concatenate(names, axis=1)


def halves_kernel(core, cells, mine, theirs):
    planes, height, width = mine.shape
    rows = width // 128
    first = core[0] == 0
    for z in range(planes):
        for pair in range(height // 16):
            for y in range(rows):
                one = cells[z, 2 * rows * pair + y].astype(F32)
                two = cells[z, 2 * rows * pair + rows + y].astype(F32)
                lower = jnp.concatenate([one[:8], two[:8]], axis=0)
                upper = jnp.concatenate([one[8:], two[8:]], axis=0)
                at = slice(pair * 16, pair * 16 + 16)
                mine[z, at, lane(y)] = jnp.where(first, lower, upper).astype(BF16)
                theirs[z, at, lane(y)] = jnp.where(first, upper, lower).astype(BF16)


def spread_rows(digits, rows_of):
    tiles, slots = digits.shape
    cols = tiles * slots
    to = lax.broadcasted_iota(jnp.int32, (slots, cols), 1) % slots
    pick = jnp.where(lax.broadcasted_iota(jnp.int32, (slots, cols), 0) == to, 1.0, 0.0)
    wide = lax.dot_general(digits.astype(BF16), pick.astype(BF16), NN, preferred_element_type=F32)
    return jnp.sum(jnp.where(rows_of, wide, 0.0), axis=0, keepdims=True)


def first_kernel(sizes, core, *refs):
    states, slots, rows = sizes
    ours, others = refs[0:4], refs[4:8]
    names, partial, low, high = refs[8:]
    half, height, width = ours[0].shape
    planes, cols, tiles = CORES * half, ours[1].shape[1], height // states
    rows_of = block_mask(tiles, cols, 1, slots)
    diagonal = block_mask(tiles, tiles, 1, 1)
    slot = (lax.broadcasted_iota(jnp.int32, (1, cols), 1) % slots).astype(F32)
    digits, terms = [], []
    for cells, proj_of, names_of, counts in (ours, others):
        found = []
        for z in range(half):
            terms.append(project(cells[z], proj_of[z], states, slots))
            name = names_of[z].astype(F32)
            top = jnp.floor(name * (1.0 / 128.0))
            count = jnp.broadcast_to(counts[z : z + 1, :].astype(F32), (tiles, tiles))
            count = jnp.sum(jnp.where(diagonal, count, 0.0), axis=1, keepdims=True)
            count = jnp.sum(jnp.where(rows_of, count, 0.0), axis=0, keepdims=True)
            is_used = slot < count
            found.append(jnp.where(is_used, spread_rows(top, rows_of), NO_NAME / 128.0))
            found.append(jnp.where(is_used, spread_rows(name - 128.0 * top, rows_of), 0.0))
        digits.append([jnp.concatenate(found[i::2], axis=1) for i in (0, 1)])
    first = core[0] == 0
    top, bottom = (
        jnp.concatenate([jnp.where(first, a, b), jnp.where(first, b, a)], axis=1)
        for a, b in zip(digits[0], digits[1])
    )
    named = top * 128.0 + bottom
    names[...] = named
    used = jnp.where(named < NO_NAME, 1.0, 0.0)
    mine, theirs = ours[0], others[0]
    for z in range(2):
        at = slice(z * height, (z + 1) * height)
        low[at, :] = jnp.where(first, mine[z], theirs[z])
        high[at, :] = jnp.where(first, theirs[half - 2 + z], mine[half - 2 + z])
    terms = [jnp.where(first, terms[z], terms[(z + half) % planes]) for z in range(planes)]
    terms = [terms[z] * used[:, z * cols : (z + 1) * cols] for z in range(planes)]
    terms = jnp.concatenate(terms, axis=1)
    partial[...] = terms
    block = folded(terms)
    parts = named.shape[1] // width
    lines = [v[:, i * width : (i + 1) * width] for v in (top, bottom) for i in range(parts)]
    lines = jnp.concatenate(lines + [jnp.zeros((16 - 2 * parts, width), F32)], axis=0).astype(BF16)
    for message in (low, high):
        write_terms(message, 2 * height, block)
        message[2 * height + 4 * states : 2 * height + 4 * states + 16, :] = lines


def same_names(names, own, store, wanted):
    for q in range(0, names.shape[1], 128):
        column = jnp.broadcast_to(names[:, q : q + 128], (128, 128)).T
        for p in range(0, own.shape[1], 128):
            if wanted(q, p):
                store(q, p, jnp.where(column == own[:, p : p + 128], 1.0, 0.0))


def doubled(terms):
    return jnp.concatenate([terms, terms], axis=0).astype(BF16)


def in_pieces(terms):
    largest = jnp.maximum(jnp.max(jnp.abs(terms), axis=1, keepdims=True), 1e-30)
    rest = terms * (240.0 / largest)
    pieces = []
    for _ in range(3):
        pieces.append(rest.astype(F8).astype(F32))
        rest = rest - pieces[-1]
    return jnp.concatenate(pieces + [jnp.zeros_like(terms)], axis=0).astype(F8), largest * (1.0 / 240.0)


def from_pieces(sums, scale):
    states = scale.shape[0]
    return (sums[:states] + sums[states : 2 * states] + sums[2 * states : 3 * states]) * scale


def look_up(strength, names):
    top = jnp.floor(names * (1.0 / 128.0))
    bottom = names - 128.0 * top
    lines, count = strength.shape[0], names.shape[1]
    line = lax.broadcasted_iota(jnp.int32, (lines, count), 0).astype(F32)
    pick = jnp.where(line == top, 1.0, 0.0)
    of_line = lax.dot_general(
        strength, pick, (((0,), (0,)), ((), ())), precision=lax.Precision.HIGHEST, preferred_element_type=F32
    )
    place = lax.broadcasted_iota(jnp.int32, (128, count), 0).astype(F32)
    return jnp.sum(jnp.where(place == bottom, of_line, 0.0), axis=0, keepdims=True)


def applied_to(chosen, proj, tiles, mask):
    spread = jnp.broadcast_to(chosen[None], (tiles,) + chosen.shape).reshape(mask.shape)
    spread = jnp.where(mask, spread, 0.0).astype(BF16)
    return lax.dot_general(spread, proj, NN, preferred_element_type=F32)


def inner_planes(planes):
    return range(2, planes - 2)


def local_kernel(sizes, first, *refs):
    states, slots, rows = sizes
    refs = list(refs)
    if first:
        core, own, names, strength = refs[0], refs[7], refs[8], refs[9]
        cur, potential, proj, base, share, inner, table, weight, square, turned = refs[10:]
        half = refs[1].shape[0]
        for start, (cells, values, proj_of) in ((core[0] * half, refs[1:4]), ((1 - core[0]) * half, refs[4:7])):
            for z in range(half):
                cur[start + z] = cells[z].astype(F32)
                potential[start + z] = values[z]
                proj[start + z] = proj_of[z]
        named = names[...]
        mine = jnp.where(named < NO_NAME, named, -1.0)

        def store(q, p, same):
            table[q : q + 128, p : p + 128] = same.astype(BF16)

        same_names(named, mine, store, lambda q, p: True)
        weight[...] = look_up(strength[...], named)
    else:
        outer, chosen, done, table, prev, potential, own, proj, cur, base, share, inner = refs
    planes, height, width = cur.shape
    tiles, cols = height // states, proj.shape[1]
    gain = (1.0 if first else 2.0) / half_width
    near, far = -gain * 2.0 / 3.0, gain / 24.0
    rest, pieces = own[...], []
    for _ in range(3):
        pieces.append(rest.astype(BF16).astype(F32))
        rest = rest - pieces[-1]
    terms = jnp.concatenate(pieces + [jnp.zeros_like(rest)], axis=0).astype(BF16)
    sums = lax.dot_general(terms, table[...], NN, preferred_element_type=F32)
    share[...] = sums[:states] + sums[states : 2 * states] + sums[2 * states : 3 * states]
    if first:
        same_tile = block_mask(cols, cols, slots, slots)
        for i, z in enumerate(inner_planes(planes)):
            products = lax.dot_general(proj[z], proj[z], NT, preferred_element_type=F32)
            square[i] = jnp.where(same_tile, products, 0.0).astype(BF16)
        for i, z in enumerate((0, 1, planes - 2, planes - 1)):
            turned[i] = proj[z].astype(F32).T.astype(BF16)
    else:
        mask = block_mask(height, cols, states, slots)
        for z in range(planes):
            if z in inner_planes(planes):
                cur[z] = done[z] + applied_to(chosen[:, z * cols : (z + 1) * cols], proj[z], tiles, mask)
            else:
                cur[z] = outer[z if z < 2 else z - planes + 4]

    def tile_step(j, carry):
        here = rows_at(j, states)
        left, right = rows_at((j + tiles - 1) % tiles, states), rows_at((j + 1) % tiles, states)

        def load(z, y):
            if y < 0:
                return cur[z, left, lane(y + rows)]
            if y >= rows:
                return cur[z, right, lane(y - rows)]
            return cur[z, here, lane(y)]

        for y in range(rows):
            mids = [load(z, y) for z in range(planes)]
            for z in range(planes):
                mid = mids[z]
                one = load(z, y - 1) + load(z, y + 1)
                two = load(z, y - 2) + load(z, y + 2)
                one += pltpu.roll(mid, 1, 1) + pltpu.roll(mid, 127, 1)
                two += pltpu.roll(mid, 2, 1) + pltpu.roll(mid, 126, 1)
                for by in (-1, 1):
                    if 0 <= z + by < planes:
                        one += mids[z + by]
                    if 0 <= z + 2 * by < planes:
                        two += mids[z + 2 * by]
                shift = potential[z, pl.ds(j * rows + y, 1), :] + (3.75 - center)
                new = near * one + far * two + shift * mid * gain
                if not first:
                    new = new - prev[z, here, lane(y)]
                base[z, here, lane(y)] = new
        return carry

    lax.fori_loop(0, tiles, tile_step, 0)
    for i, z in enumerate(inner_planes(planes)):
        inner[:, i * cols : (i + 1) * cols] = project(base[z].astype(BF16), proj[z], states, slots)


def turn_kernel(sizes, early, core, *refs):
    inputs, refs = refs[:9], refs[9:]
    made, refs = ([], refs) if early else (refs[:10], refs[10:])

    @pl.when((core[0] != 0) if early else (core[0] == 0))
    def _():
        local_kernel(sizes, True, core, *inputs, *refs)

    if not early:

        @pl.when(core[0] != 0)
        def _():
            for ready, out in zip(made, refs):
                out[...] = ready[...]


def step_kernel(sizes, first, last, *refs):
    states, slots, rows = sizes
    refs = list(refs)
    base, share, below, above, weight, names, proj, inner, square, turned = refs[:10]
    rest = refs[10:]
    planes, height, width = base.shape
    tiles = height // states
    cols = proj.shape[1]
    count = planes * cols
    reach = (planes + 1) * cols
    gain = (1.0 if first else 2.0) / half_width
    near, far = -gain * 2.0 / 3.0, gain / 24.0
    table = rest.pop(0)
    if last:
        (nxt, applied) = rest
    else:
        (nxt, low, high, partial, selected, applied) = rest

    named = names[...]
    if first:
        around = [read_names(r, 2 * height + 4 * states, count) for r in (below, above)]
        mine = jnp.where(named < NO_NAME, named, -1.0)

        def store(q, p, same):
            z = p // cols
            table[z, q - z * cols : q - z * cols + 128, p - z * cols : p - z * cols + 128] = same.astype(F8)

        def wanted(q, p):
            return 0 <= q // cols - p // cols <= planes

        same_names(jnp.concatenate(around, axis=1), mine, store, wanted)

    terms = [read_terms(r, 2 * height, states, count) for r in (below, above)]
    terms, scale = in_pieces(jnp.concatenate(terms, axis=1))
    mask = block_mask(height, cols, states, slots)
    used = jnp.where(named < NO_NAME, 1.0, 0.0)
    out = [None] * planes

    def couple(z):
        at = slice(z * cols, (z + 1) * cols)
        chosen = lax.dot_general(terms[:, z * cols : z * cols + reach], table[z], NN, preferred_element_type=F32)
        chosen = from_pieces(chosen, scale)
        chosen = (chosen + share[:, at]) * (weight[:, at] * gain)
        if not last:
            selected[:, at] = chosen
        if last or z not in inner_planes(planes):
            applied[z] = applied_to(chosen, proj[z], tiles, mask)
        else:
            i = z - inner_planes(planes)[0]
            of_chosen = lax.dot_general(doubled(chosen), square[i], NN, preferred_element_type=F32)
            out[z] = (inner[:, i * cols : (i + 1) * cols] + of_chosen[:states]) * used[:, at]

    for z in range(planes):
        if last or z not in inner_planes(planes):
            couple(z)

    def pair_step(pair, carry):
        here = rows_at(pair, 2 * states)
        for y in range(rows):
            b2, b1 = [below[rows_at(pair, 2 * states, z * height), lane(y)].astype(F32) for z in range(2)]
            a1, a2 = [above[rows_at(pair, 2 * states, z * height), lane(y)].astype(F32) for z in range(2)]
            outer = {0: near * b1 + far * b2, 1: far * b1}
            outer.update({planes - 2: far * a1, planes - 1: near * a1 + far * a2})
            for z in range(planes):
                if not last and z not in outer:
                    continue
                new = base[z, here, lane(y)] + applied[z, here, lane(y)]
                if z in outer:
                    new += outer[z]
                if last:
                    pairs = nxt.shape[1] // (2 * states)
                    parts = tiles // 2 // pairs
                    slab, plane = divmod(z, planes // CORES)
                    block = (plane * parts + pair // pairs) * CORES + slab
                    nxt[block, rows_at(pair % pairs, 2 * states), lane(y)] = new.astype(BF16)
                else:
                    i = z if z < 2 else z - planes + 4
                    nxt[i, here, lane(y)] = new
                    message = low if i < 2 else high
                    message[rows_at(pair, 2 * states, i % 2 * height), lane(y)] = new.astype(BF16)
        return carry

    lax.fori_loop(0, tiles // 2, pair_step, 0, unroll=not last)
    if not last:
        for z in inner_planes(planes):
            couple(z)
        for z in range(planes):
            if z in inner_planes(planes):
                continue
            i = z if z < 2 else z - planes + 4
            plane = (low if i < 2 else high)[i % 2 * height : (i % 2 + 1) * height, :]
            both = lax.dot_general(plane, turned[i], NN, preferred_element_type=F32)
            out[z] = of_tiles(both, states, slots) * used[:, z * cols : (z + 1) * cols]
        out = jnp.concatenate(out, axis=1)
        partial[...] = out
        block = folded(out)
        write_terms(low, 2 * height, block)
        write_terms(high, 2 * height, block)


def gram_kernel(states, cells, margin, ordered):
    sources, height, width = cells.shape
    total = jnp.zeros(margin.shape, F32)
    for pair in range(height // (2 * states)):
        both = cells[:, pair * 2 * states : (pair + 1) * 2 * states, :].astype(F32)
        for i in range(2):
            block = both[:, i * states : (i + 1) * states, :].reshape(sources * states, width).astype(BF16)
            ordered[2 * pair + i] = block
            total += lax.dot_general(block, block, NT, preferred_element_type=F32)
    margin[...] = total


def recip(x):
    r = pltpu.reciprocal(x, approx=True)
    r = r * (2.0 - x * r)
    return r

def inverse_factor(margin, inverse):
    n = margin.shape[0]
    lanes = lax.broadcasted_iota(jnp.int32, (8, n), 1)
    eye = lax.broadcasted_iota(jnp.int32, (n, n), 0) == lax.broadcasted_iota(jnp.int32, (n, n), 1)
    full = margin[...]
    diagonal = jnp.where(eye, full, 0.0)
    across = lax.rsqrt(jnp.sum(diagonal, axis=0, keepdims=True))
    down = lax.rsqrt(jnp.sum(diagonal, axis=1, keepdims=True))
    full = full * down * across
    work = [full[8 * i : 8 * i + 8, :] for i in range(n // 8)]
    for k in range(0, n, 8):
        b = k // 8
        wide = [jnp.broadcast_to(work[b][:, k + p : k + p + 1], (8, n)) for p in range(8)]
        s = {(q, p): jnp.broadcast_to(wide[p][q : q + 1, :], (8, n)) for p in range(8) for q in range(p, 8)}
        inside = (lanes >= k) & (lanes < k + 8)
        rows = [
            jnp.where(lanes == k + p, 1.0, jnp.where(inside, 0.0, jnp.broadcast_to(work[b][p : p + 1, :], (8, n))))
            for p in range(8)
        ]
        solved, x = [None] * 8, {}
        for p in range(0, 8, 2):
            a, bb, c = s[p, p], s[p + 1, p], s[p + 1, p + 1]
            det = recip(a * c - bb * bb)
            i00, i01, i11 = c * det, -bb * det, a * det
            for q in range(p + 2, 8):
                x[p, q] = i00 * s[q, p] + i01 * s[q, p + 1]
                x[p + 1, q] = i01 * s[q, p] + i11 * s[q, p + 1]
            for q in range(p + 2, 8):
                for w in range(p + 2, q + 1):
                    s[q, w] = s[q, w] - (s[q, p] * x[p, w] + s[q, p + 1] * x[p + 1, w])
                rows[q] = rows[q] - (x[p, q] * rows[p] + x[p + 1, q] * rows[p + 1])
            solved[p] = i00 * rows[p] + i01 * rows[p + 1]
            solved[p + 1] = i01 * rows[p] + i11 * rows[p + 1]
            ratio = bb * recip(a)
            out = [rows[p] * lax.rsqrt(a), (rows[p + 1] - ratio * rows[p]) * lax.rsqrt(c - bb * ratio)]
            for i in range(2):
                kept = jnp.where(lanes <= k + p + i, out[i], 0.0) * across
                inverse[k + p + i : k + p + i + 1, :] = kept[0:1]
        for p in (4, 2, 0):
            for q in range(p + 2, 8):
                solved[p] = solved[p] - x[p, q] * solved[q]
                solved[p + 1] = solved[p + 1] - x[p + 1, q] * solved[q]
        for i in range(b + 1, n // 8):
            column = [jnp.broadcast_to(work[i][:, k + p : k + p + 1], (8, n)) * solved[p] for p in range(8)]
            change = ((column[0] + column[1]) + (column[2] + column[3])) + ((column[4] + column[5]) + (column[6] + column[7]))
            work[i] = jnp.where(inside, 0.0, work[i]) - change

def rotate_kernel(margin, ordered, rotated, inverse):
    inverse_factor(margin, inverse)
    mine = inverse[...].astype(BF16)
    groups, _, states, _ = rotated.shape
    tiles, nstates, width = ordered.shape
    rows = width // 128
    for j in range(tiles):
        new = lax.dot_general(mine, ordered[j], NN, preferred_element_type=F32).astype(BF16)
        new = new.reshape(groups, states, width)
        for y in range(rows):
            rotated[:, j * rows + y, :, :] = new[:, :, lane(y)]


def per_device(states, potential, proj_values, block_list, tile_count, strength):
    local_states, slab_planes, rows_y, cells_x = states.shape
    _, tiles, slots, tile_cells = proj_values.shape
    rows = rows_y // tiles
    ring, groups = lax.axis_size("ring"), lax.axis_size("st")
    total_cells = slab_planes * rows_y * cells_x * ring * CORES
    share_states, planes = local_states // CORES, slab_planes * CORES
    height, cols, count = tiles * share_states, tiles * slots, planes * tiles * slots
    sizes = (share_states, slots, rows)
    shape = (planes, height, tile_cells)

    f32 = lambda s: jax.ShapeDtypeStruct(s, F32)
    bf16 = lambda s: jax.ShapeDtypeStruct(s, BF16)
    whole, scalar = pl.BlockSpec(), pl.BlockSpec(memory_space=pltpu.SMEM)

    def swapped(array):
        return lax.ppermute(array, "core", [(0, 1), (1, 0)])

    core = lax.axis_index("core").astype(jnp.int32).reshape(1)
    proj_own = proj_values.reshape(slab_planes, cols, tile_cells).astype(BF16)
    ours = [proj_own, block_list, tile_count]
    others = [swapped(array) for array in ours]
    potential_others = swapped(potential)
    piece = bf16((slab_planes, height, tile_cells))
    mine, theirs = call(
        halves_kernel, (piece, piece), in_specs=[scalar, whole], flops=10**7, nbytes=2 * 2**20
    )(core, states.transpose(1, 2, 0, 3))
    got = swapped(theirs)

    def sent(names):
        message = (2 * height + 4 * share_states + (16 if names else 0), tile_cells)
        return [f32((share_states, count)), bf16(message), bf16(message)]

    names, partial, low, high = call(
        lambda *r: first_kernel(sizes, *r),
        [f32((1, count))] + sent(True),
        in_specs=[scalar] + [whole] * 8,
        flops=10**9, nbytes=8 * 2**20,
    )(core, mine, *ours, got, *others)

    inside = len(inner_planes(planes))
    prev = cur = outer = None
    for m in range(4):
        first, last = m == 0, m == 3
        outs = [f32(shape), f32((share_states, count)), f32((share_states, inside * cols))]
        if first:
            args = [core, mine, potential, ours[0], got, potential_others, others[0]]
            args += [partial, names, strength.reshape(-1, 128)]
            outs = [f32(shape), f32((planes, rows_y, cells_x)), bf16((planes, cols, tile_cells))] + outs
            outs += [bf16((count, count)), f32((1, count)), bf16((inside, cols, cols)), bf16((4, tile_cells, cols))]
            made = call(
                lambda *r: turn_kernel(sizes, True, *r), outs,
                in_specs=[scalar] + [whole] * 9, flops=1e9, nbytes=8 * 2**20,
            )(*args)
            low, high, *made = lax.optimization_barrier((low, high, *made))
        below = passed_along(high, "ring", 1)
        above = passed_along(low, "ring", -1)
        if first:
            cur, shift, proj, base, share, inner, own_table, weight, square, turned = call(
                lambda *r: turn_kernel(sizes, False, *r), outs,
                in_specs=[scalar] + [whole] * 19, flops=1e9, nbytes=8 * 2**20,
            )(*args, *made)
        else:
            after, base, share, inner = call(
                lambda *r: local_kernel(sizes, False, *r), [f32(shape)] + outs, flops=1e9, nbytes=8 * 2**20
            )(outer, chosen, base, own_table, prev, shift, partial, proj)
            prev, cur = cur, after
        args = [base, share, below, above, weight, names, proj, inner, square, turned] + ([] if first else [table])
        outs = [jax.ShapeDtypeStruct((planes, (planes + 1) * cols, cols), F8)] if first else []
        if last:
            outs += [bf16((CORES * groups, planes * height // (CORES * groups), tile_cells))]
        else:
            made = sent(False)
            outs += [f32((4, height, tile_cells)), made[1], made[2], made[0], f32((share_states, count))]
        got = call(
            lambda *r, first=first, last=last: step_kernel(sizes, first, last, *r),
            outs, scratch=[pltpu.VMEM(shape, F32)], flops=1e9, nbytes=8 * 2**20,
        )(*args)
        if first:
            table, *got = got
        if last:
            (filtered,) = got
        else:
            outer, low, high, partial, chosen = got
            prev = cur

    cells = lax.all_to_all(filtered, ("st", "core"), 0, 0, tiled=True)
    nstates = groups * local_states
    own_tiles = cells.shape[1] // share_states
    part, ordered = call(
        lambda *r: gram_kernel(share_states, *r),
        (f32((nstates, nstates)), bf16((own_tiles, nstates, tile_cells))),
        flops=1e8, nbytes=2**20,
    )(cells)
    everywhere = ("ring", "core", "st")
    devices = ring * CORES * groups
    per = nstates // devices
    total = lax.all_to_all(part.reshape(devices, per, nstates), everywhere, 0, 0, tiled=True)
    total = jnp.sum(total, axis=0, keepdims=True) / total_cells
    margin = lax.all_to_all(jnp.broadcast_to(total, (devices, per, nstates)), everywhere, 0, 0, tiled=True)
    rotated = call(
        rotate_kernel,
        bf16((groups, slab_planes * rows_y // groups, local_states, cells_x)),
        scratch=[pltpu.VMEM((nstates, nstates), F32)],
        flops=2e8, nbytes=2**21,
    )(margin.reshape(nstates, nstates), ordered)
    rotated = lax.all_to_all(rotated, "st", 0, 0, tiled=True)
    return rotated.reshape(slab_planes, rows_y, local_states, cells_x).transpose(2, 0, 1, 3)


def solution(mesh):
    fine = Mesh(mesh.devices.reshape(-1, CORES, mesh.shape["st"]), ("ring", "core", "st"))
    dom = ("ring", "core")
    return jax.shard_map(
        per_device,
        mesh=fine,
        in_specs=(
            P("st", dom, None, None),
            P(dom, None, None),
            P(dom, None, None, None),
            P(dom, None, None),
            P(dom, None),
            P(),
        ),
        out_specs=P("st", dom, None, None),
        check_vma=False,
    )
```

```python
import jax
import jax.numpy as jnp
from jax import lax
from jax.experimental import pallas as pl
from jax.experimental.pallas import tpu as pltpu
from jax.sharding import Mesh, PartitionSpec as P

center = 8.25
half_width = 7.75

F32 = jnp.float32
BF16 = jnp.bfloat16
F8 = jnp.float8_e4m3fn
NT = (((1,), (1,)), ((), ()))
NN = (((1,), (0,)), ((), ()))
CORES = 2
NO_NAME = 255.0 * 128.0


def passed_along(array, axis, by):
    devices = lax.axis_size(axis)
    return lax.ppermute(array, axis, [(i, (i + by) % devices) for i in range(devices)])


def call(kernel, out_shape, scratch=(), vmem=12, flops=0, nbytes=0, **specs):
    return pl.pallas_call(
        kernel,
        out_shape=out_shape,
        **specs,
        scratch_shapes=list(scratch),
        compiler_params=pltpu.CompilerParams(vmem_limit_bytes=vmem * 2**20),
        cost_estimate=pl.CostEstimate(flops=int(flops), bytes_accessed=int(nbytes), transcendentals=0),
    )


def rows_at(t, states, base=0):
    return pl.ds(pl.multiple_of(base + t * states, states), states)


def lane(y):
    return slice(y * 128, (y + 1) * 128)


def block_mask(rows, cols, row_block, col_block):
    row = lax.broadcasted_iota(jnp.int32, (rows, cols), 0) // row_block
    col = lax.broadcasted_iota(jnp.int32, (rows, cols), 1) // col_block
    return row == col


def project(field, proj, states, slots):
    return of_tiles(lax.dot_general(field, proj, NT, preferred_element_type=F32), states, slots)


def of_tiles(both, states, slots):
    both = jnp.where(block_mask(*both.shape, states, slots), both, 0.0)
    return jnp.sum(both.reshape(-1, states, both.shape[1]), axis=0)


def folded(terms):
    half = terms.shape[1] // 2
    return jnp.concatenate([terms[:, :half], terms[:, half:]], axis=0).astype(BF16)


def unfolded(block):
    block = block.astype(F32)
    states = block.shape[0] // 2
    return jnp.concatenate([block[:states], block[states:]], axis=1)


def write_terms(message, base, block):
    high, width = block.shape[0], message.shape[1]
    for i in range(block.shape[1] // width):
        message[base + i * high : base + (i + 1) * high, :] = block[:, i * width : (i + 1) * width]


def read_terms(message, base, states, count):
    width, high = message.shape[1], 2 * states
    parts = [message[base + i * high : base + (i + 1) * high, :] for i in range(count // high * states // width)]
    return unfolded(jnp.concatenate(parts, axis=1))


def read_names(message, base, count):
    width = message.shape[1]
    digits = message[base : base + 16, :].astype(F32)
    parts = count // width
    names = [digits[i : i + 1] * 128.0 + digits[parts + i : parts + i + 1] for i in range(parts)]
    return jnp.concatenate(names, axis=1)


def halves_kernel(core, cells, mine, theirs):
    planes, height, width = mine.shape
    rows = width // 128
    first = core[0] == 0
    for z in range(planes):
        for pair in range(height // 16):
            for y in range(rows):
                one = cells[z, 2 * rows * pair + y].astype(F32)
                two = cells[z, 2 * rows * pair + rows + y].astype(F32)
                lower = jnp.concatenate([one[:8], two[:8]], axis=0)
                upper = jnp.concatenate([one[8:], two[8:]], axis=0)
                at = slice(pair * 16, pair * 16 + 16)
                mine[z, at, lane(y)] = jnp.where(first, lower, upper).astype(BF16)
                theirs[z, at, lane(y)] = jnp.where(first, upper, lower).astype(BF16)


def spread_rows(digits, rows_of):
    tiles, slots = digits.shape
    cols = tiles * slots
    to = lax.broadcasted_iota(jnp.int32, (slots, cols), 1) % slots
    pick = jnp.where(lax.broadcasted_iota(jnp.int32, (slots, cols), 0) == to, 1.0, 0.0)
    wide = lax.dot_general(digits.astype(BF16), pick.astype(BF16), NN, preferred_element_type=F32)
    return jnp.sum(jnp.where(rows_of, wide, 0.0), axis=0, keepdims=True)


def first_kernel(sizes, core, *refs):
    states, slots, rows = sizes
    ours, others = refs[0:4], refs[4:8]
    names, partial, low, high = refs[8:]
    half, height, width = ours[0].shape
    planes, cols, tiles = CORES * half, ours[1].shape[1], height // states
    rows_of = block_mask(tiles, cols, 1, slots)
    diagonal = block_mask(tiles, tiles, 1, 1)
    slot = (lax.broadcasted_iota(jnp.int32, (1, cols), 1) % slots).astype(F32)
    digits, terms = [], []
    for cells, proj_of, names_of, counts in (ours, others):
        found = []
        for z in range(half):
            terms.append(project(cells[z], proj_of[z], states, slots))
            name = names_of[z].astype(F32)
            top = jnp.floor(name * (1.0 / 128.0))
            count = jnp.broadcast_to(counts[z : z + 1, :].astype(F32), (tiles, tiles))
            count = jnp.sum(jnp.where(diagonal, count, 0.0), axis=1, keepdims=True)
            count = jnp.sum(jnp.where(rows_of, count, 0.0), axis=0, keepdims=True)
            is_used = slot < count
            found.append(jnp.where(is_used, spread_rows(top, rows_of), NO_NAME / 128.0))
            found.append(jnp.where(is_used, spread_rows(name - 128.0 * top, rows_of), 0.0))
        digits.append([jnp.concatenate(found[i::2], axis=1) for i in (0, 1)])
    first = core[0] == 0
    top, bottom = (
        jnp.concatenate([jnp.where(first, a, b), jnp.where(first, b, a)], axis=1)
        for a, b in zip(digits[0], digits[1])
    )
    named = top * 128.0 + bottom
    names[...] = named
    used = jnp.where(named < NO_NAME, 1.0, 0.0)
    mine, theirs = ours[0], others[0]
    for z in range(2):
        at = slice(z * height, (z + 1) * height)
        low[at, :] = jnp.where(first, mine[z], theirs[z])
        high[at, :] = jnp.where(first, theirs[half - 2 + z], mine[half - 2 + z])
    terms = [jnp.where(first, terms[z], terms[(z + half) % planes]) for z in range(planes)]
    terms = [terms[z] * used[:, z * cols : (z + 1) * cols] for z in range(planes)]
    terms = jnp.concatenate(terms, axis=1)
    partial[...] = terms
    block = folded(terms)
    parts = named.shape[1] // width
    lines = [v[:, i * width : (i + 1) * width] for v in (top, bottom) for i in range(parts)]
    lines = jnp.concatenate(lines + [jnp.zeros((16 - 2 * parts, width), F32)], axis=0).astype(BF16)
    for message in (low, high):
        write_terms(message, 2 * height, block)
        message[2 * height + 4 * states : 2 * height + 4 * states + 16, :] = lines


def same_names(names, own, store, wanted):
    for q in range(0, names.shape[1], 128):
        column = jnp.broadcast_to(names[:, q : q + 128], (128, 128)).T
        for p in range(0, own.shape[1], 128):
            if wanted(q, p):
                store(q, p, jnp.where(column == own[:, p : p + 128], 1.0, 0.0))


def doubled(terms):
    return jnp.concatenate([terms, terms], axis=0).astype(BF16)


def in_pieces(terms):
    largest = jnp.maximum(jnp.max(jnp.abs(terms), axis=1, keepdims=True), 1e-30)
    rest = terms * (240.0 / largest)
    pieces = []
    for _ in range(3):
        pieces.append(rest.astype(F8).astype(F32))
        rest = rest - pieces[-1]
    return jnp.concatenate(pieces + [jnp.zeros_like(terms)], axis=0).astype(F8), largest * (1.0 / 240.0)


def from_pieces(sums, scale):
    states = scale.shape[0]
    return (sums[:states] + sums[states : 2 * states] + sums[2 * states : 3 * states]) * scale


def look_up(strength, names):
    top = jnp.floor(names * (1.0 / 128.0))
    bottom = names - 128.0 * top
    lines, count = strength.shape[0], names.shape[1]
    line = lax.broadcasted_iota(jnp.int32, (lines, count), 0).astype(F32)
    pick = jnp.where(line == top, 1.0, 0.0)
    of_line = lax.dot_general(
        strength, pick, (((0,), (0,)), ((), ())), precision=lax.Precision.HIGHEST, preferred_element_type=F32
    )
    place = lax.broadcasted_iota(jnp.int32, (128, count), 0).astype(F32)
    return jnp.sum(jnp.where(place == bottom, of_line, 0.0), axis=0, keepdims=True)


def applied_to(chosen, proj, tiles, mask):
    spread = jnp.broadcast_to(chosen[None], (tiles,) + chosen.shape).reshape(mask.shape)
    spread = jnp.where(mask, spread, 0.0).astype(BF16)
    return lax.dot_general(spread, proj, NN, preferred_element_type=F32)


def inner_planes(planes):
    return range(2, planes - 2)


def local_kernel(sizes, first, *refs):
    states, slots, rows = sizes
    refs = list(refs)
    if first:
        core, own, names, strength = refs[0], refs[7], refs[8], refs[9]
        cur, potential, proj, base, share, inner, table, weight, square, turned = refs[10:]
        half = refs[1].shape[0]
        for start, (cells, values, proj_of) in ((core[0] * half, refs[1:4]), ((1 - core[0]) * half, refs[4:7])):
            for z in range(half):
                cur[start + z] = cells[z].astype(F32)
                potential[start + z] = values[z]
                proj[start + z] = proj_of[z]
        named = names[...]
        mine = jnp.where(named < NO_NAME, named, -1.0)

        def store(q, p, same):
            table[q : q + 128, p : p + 128] = same.astype(BF16)

        same_names(named, mine, store, lambda q, p: True)
        weight[...] = look_up(strength[...], named)
    else:
        outer, chosen, done, table, prev, potential, own, proj, cur, base, share, inner = refs
    planes, height, width = cur.shape
    tiles, cols = height // states, proj.shape[1]
    gain = (1.0 if first else 2.0) / half_width
    near, far = -gain * 2.0 / 3.0, gain / 24.0
    rest, pieces = own[...], []
    for _ in range(3):
        pieces.append(rest.astype(BF16).astype(F32))
        rest = rest - pieces[-1]
    terms = jnp.concatenate(pieces + [jnp.zeros_like(rest)], axis=0).astype(BF16)
    sums = lax.dot_general(terms, table[...], NN, preferred_element_type=F32)
    share[...] = sums[:states] + sums[states : 2 * states] + sums[2 * states : 3 * states]
    if first:
        same_tile = block_mask(cols, cols, slots, slots)
        for i, z in enumerate(inner_planes(planes)):
            products = lax.dot_general(proj[z], proj[z], NT, preferred_element_type=F32)
            square[i] = jnp.where(same_tile, products, 0.0).astype(BF16)
        for i, z in enumerate((0, 1, planes - 2, planes - 1)):
            turned[i] = proj[z].astype(F32).T.astype(BF16)
    else:
        mask = block_mask(height, cols, states, slots)
        for z in range(planes):
            if z in inner_planes(planes):
                cur[z] = done[z] + applied_to(chosen[:, z * cols : (z + 1) * cols], proj[z], tiles, mask)
            else:
                cur[z] = outer[z if z < 2 else z - planes + 4]

    def tile_step(j, carry):
        here = rows_at(j, states)
        left, right = rows_at((j + tiles - 1) % tiles, states), rows_at((j + 1) % tiles, states)

        def load(z, y):
            if y < 0:
                return cur[z, left, lane(y + rows)]
            if y >= rows:
                return cur[z, right, lane(y - rows)]
            return cur[z, here, lane(y)]

        for y in range(rows):
            mids = [load(z, y) for z in range(planes)]
            for z in range(planes):
                mid = mids[z]
                one = load(z, y - 1) + load(z, y + 1)
                two = load(z, y - 2) + load(z, y + 2)
                one += pltpu.roll(mid, 1, 1) + pltpu.roll(mid, 127, 1)
                two += pltpu.roll(mid, 2, 1) + pltpu.roll(mid, 126, 1)
                for by in (-1, 1):
                    if 0 <= z + by < planes:
                        one += mids[z + by]
                    if 0 <= z + 2 * by < planes:
                        two += mids[z + 2 * by]
                shift = potential[z, pl.ds(j * rows + y, 1), :] + (3.75 - center)
                new = near * one + far * two + shift * mid * gain
                if not first:
                    new = new - prev[z, here, lane(y)]
                base[z, here, lane(y)] = new
        return carry

    lax.fori_loop(0, tiles, tile_step, 0)
    for i, z in enumerate(inner_planes(planes)):
        inner[:, i * cols : (i + 1) * cols] = project(base[z].astype(BF16), proj[z], states, slots)


def turn_kernel(sizes, early, core, *refs):
    inputs, refs = refs[:9], refs[9:]
    made, refs = ([], refs) if early else (refs[:10], refs[10:])

    @pl.when((core[0] != 0) if early else (core[0] == 0))
    def _():
        local_kernel(sizes, True, core, *inputs, *refs)

    if not early:

        @pl.when(core[0] != 0)
        def _():
            for ready, out in zip(made, refs):
                out[...] = ready[...]


def step_kernel(sizes, first, last, *refs):
    states, slots, rows = sizes
    refs = list(refs)
    base, share, below, above, weight, names, proj, inner, square, turned = refs[:10]
    rest = refs[10:]
    planes, height, width = base.shape
    tiles = height // states
    cols = proj.shape[1]
    count = planes * cols
    reach = (planes + 1) * cols
    gain = (1.0 if first else 2.0) / half_width
    near, far = -gain * 2.0 / 3.0, gain / 24.0
    table = rest.pop(0)
    if last:
        (nxt, applied) = rest
    else:
        (nxt, low, high, partial, selected, applied) = rest

    named = names[...]
    if first:
        around = [read_names(r, 2 * height + 4 * states, count) for r in (below, above)]
        mine = jnp.where(named < NO_NAME, named, -1.0)

        def store(q, p, same):
            z = p // cols
            table[z, q - z * cols : q - z * cols + 128, p - z * cols : p - z * cols + 128] = same.astype(F8)

        def wanted(q, p):
            return 0 <= q // cols - p // cols <= planes

        same_names(jnp.concatenate(around, axis=1), mine, store, wanted)

    terms = [read_terms(r, 2 * height, states, count) for r in (below, above)]
    terms, scale = in_pieces(jnp.concatenate(terms, axis=1))
    mask = block_mask(height, cols, states, slots)
    used = jnp.where(named < NO_NAME, 1.0, 0.0)
    out = [None] * planes

    def couple(z):
        at = slice(z * cols, (z + 1) * cols)
        chosen = lax.dot_general(terms[:, z * cols : z * cols + reach], table[z], NN, preferred_element_type=F32)
        chosen = from_pieces(chosen, scale)
        chosen = (chosen + share[:, at]) * (weight[:, at] * gain)
        if not last:
            selected[:, at] = chosen
        if last or z not in inner_planes(planes):
            applied[z] = applied_to(chosen, proj[z], tiles, mask)
        else:
            i = z - inner_planes(planes)[0]
            of_chosen = lax.dot_general(doubled(chosen), square[i], NN, preferred_element_type=F32)
            out[z] = (inner[:, i * cols : (i + 1) * cols] + of_chosen[:states]) * used[:, at]

    for z in range(planes):
        if last or z not in inner_planes(planes):
            couple(z)

    def pair_step(pair, carry):
        here = rows_at(pair, 2 * states)
        for y in range(rows):
            b2, b1 = [below[rows_at(pair, 2 * states, z * height), lane(y)].astype(F32) for z in range(2)]
            a1, a2 = [above[rows_at(pair, 2 * states, z * height), lane(y)].astype(F32) for z in range(2)]
            outer = {0: near * b1 + far * b2, 1: far * b1}
            outer.update({planes - 2: far * a1, planes - 1: near * a1 + far * a2})
            for z in range(planes):
                if not last and z not in outer:
                    continue
                new = base[z, here, lane(y)] + applied[z, here, lane(y)]
                if z in outer:
                    new += outer[z]
                if last:
                    pairs = nxt.shape[1] // (2 * states)
                    parts = tiles // 2 // pairs
                    slab, plane = divmod(z, planes // CORES)
                    block = (plane * parts + pair // pairs) * CORES + slab
                    nxt[block, rows_at(pair % pairs, 2 * states), lane(y)] = new.astype(BF16)
                else:
                    i = z if z < 2 else z - planes + 4
                    nxt[i, here, lane(y)] = new
                    message = low if i < 2 else high
                    message[rows_at(pair, 2 * states, i % 2 * height), lane(y)] = new.astype(BF16)
        return carry

    lax.fori_loop(0, tiles // 2, pair_step, 0, unroll=True)
    if not last:
        for z in inner_planes(planes):
            couple(z)
        for z in range(planes):
            if z in inner_planes(planes):
                continue
            i = z if z < 2 else z - planes + 4
            plane = (low if i < 2 else high)[i % 2 * height : (i % 2 + 1) * height, :]
            both = lax.dot_general(plane, turned[i], NN, preferred_element_type=F32)
            out[z] = of_tiles(both, states, slots) * used[:, z * cols : (z + 1) * cols]
        out = jnp.concatenate(out, axis=1)
        partial[...] = out
        block = folded(out)
        write_terms(low, 2 * height, block)
        write_terms(high, 2 * height, block)


def gram_kernel(states, cells, margin, ordered):
    sources, height, width = cells.shape
    total = jnp.zeros(margin.shape, F32)
    for pair in range(height // (2 * states)):
        both = cells[:, pair * 2 * states : (pair + 1) * 2 * states, :].astype(F32)
        for i in range(2):
            block = both[:, i * states : (i + 1) * states, :].reshape(sources * states, width).astype(BF16)
            ordered[2 * pair + i] = block
            total += lax.dot_general(block, block, NT, preferred_element_type=F32)
    margin[...] = total


def recip(x):
    r = pltpu.reciprocal(x, approx=True)
    r = r * (2.0 - x * r)
    return r

def inverse_factor(margin, inverse):
    n = margin.shape[0]
    lanes = lax.broadcasted_iota(jnp.int32, (8, n), 1)
    eye = lax.broadcasted_iota(jnp.int32, (n, n), 0) == lax.broadcasted_iota(jnp.int32, (n, n), 1)
    full = margin[...]
    diagonal = jnp.where(eye, full, 0.0)
    across = lax.rsqrt(jnp.sum(diagonal, axis=0, keepdims=True))
    down = lax.rsqrt(jnp.sum(diagonal, axis=1, keepdims=True))
    full = full * down * across
    work = [full[8 * i : 8 * i + 8, :] for i in range(n // 8)]
    for k in range(0, n, 8):
        b = k // 8
        wide = [jnp.broadcast_to(work[b][:, k + p : k + p + 1], (8, n)) for p in range(8)]
        s = {(q, p): jnp.broadcast_to(wide[p][q : q + 1, :], (8, n)) for p in range(8) for q in range(p, 8)}
        inside = (lanes >= k) & (lanes < k + 8)
        rows = [
            jnp.where(lanes == k + p, 1.0, jnp.where(inside, 0.0, jnp.broadcast_to(work[b][p : p + 1, :], (8, n))))
            for p in range(8)
        ]
        solved, x = [None] * 8, {}
        for p in range(0, 8, 2):
            a, bb, c = s[p, p], s[p + 1, p], s[p + 1, p + 1]
            det = recip(a * c - bb * bb)
            i00, i01, i11 = c * det, -bb * det, a * det
            for q in range(p + 2, 8):
                x[p, q] = i00 * s[q, p] + i01 * s[q, p + 1]
                x[p + 1, q] = i01 * s[q, p] + i11 * s[q, p + 1]
            for q in range(p + 2, 8):
                for w in range(p + 2, q + 1):
                    s[q, w] = s[q, w] - (s[q, p] * x[p, w] + s[q, p + 1] * x[p + 1, w])
                rows[q] = rows[q] - (x[p, q] * rows[p] + x[p + 1, q] * rows[p + 1])
            solved[p] = i00 * rows[p] + i01 * rows[p + 1]
            solved[p + 1] = i01 * rows[p] + i11 * rows[p + 1]
            ratio = bb * recip(a)
            out = [rows[p] * lax.rsqrt(a), (rows[p + 1] - ratio * rows[p]) * lax.rsqrt(c - bb * ratio)]
            for i in range(2):
                kept = jnp.where(lanes <= k + p + i, out[i], 0.0) * across
                inverse[k + p + i : k + p + i + 1, :] = kept[0:1]
        for p in (4, 2, 0):
            for q in range(p + 2, 8):
                solved[p] = solved[p] - x[p, q] * solved[q]
                solved[p + 1] = solved[p + 1] - x[p + 1, q] * solved[q]
        for i in range(b + 1, n // 8):
            column = [jnp.broadcast_to(work[i][:, k + p : k + p + 1], (8, n)) * solved[p] for p in range(8)]
            change = ((column[0] + column[1]) + (column[2] + column[3])) + ((column[4] + column[5]) + (column[6] + column[7]))
            work[i] = jnp.where(inside, 0.0, work[i]) - change

def rotate_kernel(margin, ordered, rotated, inverse):
    inverse_factor(margin, inverse)
    mine = inverse[...].astype(BF16)
    groups, _, states, _ = rotated.shape
    tiles, nstates, width = ordered.shape
    rows = width // 128
    for j in range(tiles):
        new = lax.dot_general(mine, ordered[j], NN, preferred_element_type=F32).astype(BF16)
        new = new.reshape(groups, states, width)
        for y in range(rows):
            rotated[:, j * rows + y, :, :] = new[:, :, lane(y)]


def per_device(states, potential, proj_values, block_list, tile_count, strength):
    local_states, slab_planes, rows_y, cells_x = states.shape
    _, tiles, slots, tile_cells = proj_values.shape
    rows = rows_y // tiles
    ring, groups = lax.axis_size("ring"), lax.axis_size("st")
    total_cells = slab_planes * rows_y * cells_x * ring * CORES
    share_states, planes = local_states // CORES, slab_planes * CORES
    height, cols, count = tiles * share_states, tiles * slots, planes * tiles * slots
    sizes = (share_states, slots, rows)
    shape = (planes, height, tile_cells)

    f32 = lambda s: jax.ShapeDtypeStruct(s, F32)
    bf16 = lambda s: jax.ShapeDtypeStruct(s, BF16)
    whole, scalar = pl.BlockSpec(), pl.BlockSpec(memory_space=pltpu.SMEM)

    def swapped(array):
        return lax.ppermute(array, "core", [(0, 1), (1, 0)])

    core = lax.axis_index("core").astype(jnp.int32).reshape(1)
    proj_own = proj_values.reshape(slab_planes, cols, tile_cells).astype(BF16)
    ours = [proj_own, block_list, tile_count]
    others = [swapped(array) for array in ours]
    potential_others = swapped(potential)
    piece = bf16((slab_planes, height, tile_cells))
    mine, theirs = call(
        halves_kernel, (piece, piece), in_specs=[scalar, whole], flops=10**7, nbytes=2 * 2**20
    )(core, states.transpose(1, 2, 0, 3))
    got = swapped(theirs)

    def sent(names):
        message = (2 * height + 4 * share_states + (16 if names else 0), tile_cells)
        return [f32((share_states, count)), bf16(message), bf16(message)]

    names, partial, low, high = call(
        lambda *r: first_kernel(sizes, *r),
        [f32((1, count))] + sent(True),
        in_specs=[scalar] + [whole] * 8,
        flops=10**9, nbytes=8 * 2**20,
    )(core, mine, *ours, got, *others)

    inside = len(inner_planes(planes))
    prev = cur = outer = None
    for m in range(4):
        first, last = m == 0, m == 3
        outs = [f32(shape), f32((share_states, count)), f32((share_states, inside * cols))]
        if first:
            args = [core, mine, potential, ours[0], got, potential_others, others[0]]
            args += [partial, names, strength.reshape(-1, 128)]
            outs = [f32(shape), f32((planes, rows_y, cells_x)), bf16((planes, cols, tile_cells))] + outs
            outs += [bf16((count, count)), f32((1, count)), bf16((inside, cols, cols)), bf16((4, tile_cells, cols))]
            made = call(
                lambda *r: turn_kernel(sizes, True, *r), outs,
                in_specs=[scalar] + [whole] * 9, flops=1e9, nbytes=8 * 2**20,
            )(*args)
            low, high, *made = lax.optimization_barrier((low, high, *made))
        below = passed_along(high, "ring", 1)
        above = passed_along(low, "ring", -1)
        if first:
            cur, shift, proj, base, share, inner, own_table, weight, square, turned = call(
                lambda *r: turn_kernel(sizes, False, *r), outs,
                in_specs=[scalar] + [whole] * 19, flops=1e9, nbytes=8 * 2**20,
            )(*args, *made)
        else:
            after, base, share, inner = call(
                lambda *r: local_kernel(sizes, False, *r), [f32(shape)] + outs, flops=1e9, nbytes=8 * 2**20
            )(outer, chosen, base, own_table, prev, shift, partial, proj)
            prev, cur = cur, after
        args = [base, share, below, above, weight, names, proj, inner, square, turned] + ([] if first else [table])
        outs = [jax.ShapeDtypeStruct((planes, (planes + 1) * cols, cols), F8)] if first else []
        if last:
            outs += [bf16((CORES * groups, planes * height // (CORES * groups), tile_cells))]
        else:
            made = sent(False)
            outs += [f32((4, height, tile_cells)), made[1], made[2], made[0], f32((share_states, count))]
        got = call(
            lambda *r, first=first, last=last: step_kernel(sizes, first, last, *r),
            outs, scratch=[pltpu.VMEM(shape, F32)], flops=1e9, nbytes=8 * 2**20,
        )(*args)
        if first:
            table, *got = got
        if last:
            (filtered,) = got
        else:
            outer, low, high, partial, chosen = got
            prev = cur

    cells = lax.all_to_all(filtered, ("st", "core"), 0, 0, tiled=True)
    nstates = groups * local_states
    own_tiles = cells.shape[1] // share_states
    part, ordered = call(
        lambda *r: gram_kernel(share_states, *r),
        (f32((nstates, nstates)), bf16((own_tiles, nstates, tile_cells))),
        flops=1e8, nbytes=2**20,
    )(cells)
    everywhere = ("ring", "core", "st")
    devices = ring * CORES * groups
    per = nstates // devices
    total = lax.all_to_all(part.reshape(devices, per, nstates), everywhere, 0, 0, tiled=True)
    total = jnp.sum(total, axis=0, keepdims=True) / total_cells
    margin = lax.all_to_all(jnp.broadcast_to(total, (devices, per, nstates)), everywhere, 0, 0, tiled=True)
    rotated = call(
        rotate_kernel,
        bf16((groups, slab_planes * rows_y // groups, local_states, cells_x)),
        scratch=[pltpu.VMEM((nstates, nstates), F32)],
        flops=2e8, nbytes=2**21,
    )(margin.reshape(nstates, nstates), ordered)
    rotated = lax.all_to_all(rotated, "st", 0, 0, tiled=True)
    return rotated.reshape(slab_planes, rows_y, local_states, cells_x).transpose(2, 0, 1, 3)


def solution(mesh):
    fine = Mesh(mesh.devices.reshape(-1, CORES, mesh.shape["st"]), ("ring", "core", "st"))
    dom = ("ring", "core")
    return jax.shard_map(
        per_device,
        mesh=fine,
        in_specs=(
            P("st", dom, None, None),
            P(dom, None, None),
            P(dom, None, None, None),
            P(dom, None, None),
            P(dom, None),
            P(),
        ),
        out_specs=P("st", dom, None, None),
        check_vma=False,
    )
```
